32 devices in a mesh: wide: 8 (over z, x), narrow: 4 (over y, core).
Axes of the slice: x: 2, y: 2, z: 4, core: 2. Of those that a mesh axis runs over, the one named last changes fastest.
Arguments:
- hidden_in: bfloat16 [32768, 768], P(('wide', 'narrow')), may hold values from -6 to 6
- out_grad: bfloat16 [32768, 768], P(('wide', 'narrow')), may hold values from -6 to 6
- w_qkv: bfloat16 [768, 2304], replicated, may hold values from -0.3125 to 0.3125
- b_query: bfloat16 [768], replicated, may hold values from -3 to 3
- b_value: bfloat16 [768], replicated, may hold values from -3 to 3
- w_out: bfloat16 [768, 768], replicated, may hold values from -1.25 to 1.25
- b_out: bfloat16 [768], replicated, may hold values from -3 to 3
- ln1_gain: bfloat16 [768], replicated, may hold values from 0.25 to 1.75
- ln1_bias: bfloat16 [768], replicated, may hold values from -3 to 3
- w_in: bfloat16 [768, 3072], replicated, may hold values from -0.21875 to 0.21875
- b_in: bfloat16 [3072], replicated, may hold values from -3 to 3
- w_ff_out: bfloat16 [3072, 768], replicated, may hold values from -0.15625 to 0.15625
- b_ff_out: bfloat16 [768], replicated, may hold values from -3 to 3
- ln2_gain: bfloat16 [768], replicated, may hold values from 0.25 to 1.75
- ln2_bias: bfloat16 [768], replicated, may hold values from -3 to 3
- doc_count: int32 [32], replicated, may hold values from 1 to 8, as said below
- single_flag: int32 [32, 8], replicated, may hold values from 0 to 1, as said below
Outputs:
- block_out: bfloat16 [32768, 768], P(('wide', 'narrow'))
- loss: float32 [], replicated
- span_loss: float32 [256], P(('wide', 'narrow'))
- grad_in: float32 [32768, 768], P(('wide', 'narrow'))
- grad_w_qkv: float32 [768, 2304], replicated
- grad_b_query: float32 [768], replicated
- grad_b_value: float32 [768], replicated
- grad_w_out: float32 [768, 768], replicated
- grad_b_out: float32 [768], replicated
- grad_ln1_gain: float32 [768], replicated
- grad_ln1_bias: float32 [768], replicated
- grad_w_in: float32 [768, 3072], replicated
- grad_b_in: float32 [3072], replicated
- grad_w_ff_out: float32 [3072, 768], replicated
- grad_b_ff_out: float32 [768], replicated
- grad_ln2_gain: float32 [768], replicated
- grad_ln2_bias: float32 [768], replicated
The draws below stay inside these ranges and needn't reach their ends.
Inputs may be any that keep to these rules, and one draw needn't show every extreme that they name: doc_count[d] whole documents stand on device d (mesh index, wide slowest); its k-th document takes 2 - single_flag[d, k] consecutive span slots from slot 0 on, together at most 8; slots after them are empty. In every draw some device holds 8 single-span documents and another holds one document of two spans. `single_flag`: entries at k >= doc_count[d] are not read.
All inputs are finite; a program needn't handle non-finite values.
Results may differ from the reference program's by a relative error of at most 0.014.
The reference program's roundings to bfloat16 on the way count: a program that leaves them out, or rounds other values in their place, can miss the bound.
Values may be sent and summed in bfloat16 or wider, within the bound.
A program may use at most 192 MiB of HBM per device.

```python
from functools import partial
import jax
import jax.numpy as jnp
from jax import lax

D = 768
HEADS = 12
HEAD_DIM = 64
FF = 3072
SPAN_LEN = 128
SPAN_DEV = 8
DOCSETS = 32
TOKENS = 32768
N_WIDE = 8


def document_plan(key):
    flag_key, pick_key, full_key, lone_key = jax.random.split(key, 4)
    device_total = DOCSETS
    singles = (jax.random.randint(flag_key, (device_total, SPAN_DEV), 0, 3) == 0).astype(jnp.int32)
    spans_used = jnp.cumsum(2 - singles, axis=1)
    fitting = jnp.sum((spans_used <= SPAN_DEV).astype(jnp.int32), axis=1)
    doc_total = 1 + jax.random.randint(pick_key, (device_total,), 0, 1 << 20) % fitting
    full_device = jax.random.randint(full_key, (), 0, device_total)
    lone_device = (full_device + 1 + jax.random.randint(lone_key, (), 0, device_total - 1)) % device_total
    device_ids = jnp.arange(device_total)
    slot_ids = jnp.arange(SPAN_DEV)
    singles = jnp.where(device_ids[:, None] == full_device, 1, singles)
    singles = jnp.where((device_ids[:, None] == lone_device) & (slot_ids[None, :] == 0), 0, singles)
    doc_total = jnp.where(device_ids == full_device, SPAN_DEV, doc_total)
    doc_total = jnp.where(device_ids == lone_device, 1, doc_total)
    return (doc_total.astype(jnp.int32), singles.astype(jnp.int32))


def draw_doc_count(key, part):
    doc_total, singles = document_plan(key)
    return doc_total


def draw_single_flag(key, part):
    doc_total, singles = document_plan(key)
    return singles


def levels(own_key, shape, cuts, least, largest):
    level = 1.0
    for position, blocks in cuts:
        draws = jax.random.uniform(jax.random.fold_in(jax.random.fold_in(own_key, 6), position), (blocks,), jnp.float32, least / len(cuts), largest / len(cuts))
        level = level * jnp.repeat(jnp.exp(draws), shape[position] // blocks).reshape((-1,) + (1,) * (len(shape) - 1 - position))
    return level


def noise(rng, dims, scale, most, pieces=(), kind=jnp.bfloat16):
    drawn = jax.random.normal(rng, dims, jnp.float32) * scale
    if len(pieces) > 0:
        drawn = levels(rng, dims, pieces, -0.22, 0.18) * drawn
    return jnp.clip(drawn, min=-most, max=most).astype(kind)


def setup_inputs(seed: int = 0) -> dict:
    splits = jax.random.split(jax.random.key(seed), 18)
    hidden_in = noise(splits[0], (TOKENS, D), 1.0, 6.0, ((0, 32),))
    out_grad = noise(splits[1], (TOKENS, D), 1.0, 6.0, ((0, 32),))
    w_qkv = noise(splits[2], (D, 3 * D), (D // 2) ** -0.5, 0.3125)
    b_query = noise(splits[3], (D,), 0.5, 3.0)
    b_value = noise(splits[4], (D,), 0.5, 3.0)
    w_out = noise(splits[5], (D, D), (D // 32) ** -0.5, 1.25)
    b_out = noise(splits[6], (D,), 0.5, 3.0)
    ln1_gain = jnp.clip(1.0 + 0.15 * jax.random.normal(splits[7], (D,), jnp.float32), 0.25, 1.75).astype(jnp.bfloat16)
    ln1_bias = noise(splits[8], (D,), 0.5, 3.0)
    w_in = noise(splits[9], (D, FF), D ** -0.5, 0.21875)
    b_in = noise(splits[10], (FF,), 0.5, 3.0)
    w_ff_out = noise(splits[11], (FF, D), (FF // 2) ** -0.5, 0.15625)
    b_ff_out = noise(splits[12], (D,), 0.5, 3.0)
    ln2_gain = jnp.clip(1.0 + 0.15 * jax.random.normal(splits[13], (D,), jnp.float32), 0.25, 1.75).astype(jnp.bfloat16)
    ln2_bias = noise(splits[14], (D,), 0.5, 3.0)
    doc_count = draw_doc_count(jax.random.fold_in(splits[17], 71), 0)
    single_flag = draw_single_flag(jax.random.fold_in(splits[17], 71), 0)
    return dict(hidden_in=hidden_in, out_grad=out_grad, w_qkv=w_qkv, b_query=b_query, b_value=b_value, w_out=w_out, b_out=b_out, ln1_gain=ln1_gain, ln1_bias=ln1_bias, w_in=w_in, b_in=b_in, w_ff_out=w_ff_out, b_ff_out=b_ff_out, ln2_gain=ln2_gain, ln2_bias=ln2_bias, doc_count=doc_count, single_flag=single_flag)


highest = lax.Precision.HIGHEST
ln_eps = 1e-06
score_scale = 0.2
far_low = -1000000000.0

@jax.custom_vjp
def low(v):
    return lax.optimization_barrier(v.astype(jnp.bfloat16)).astype(jnp.float32)

@jax.custom_vjp
def low_back(v):
    return v

def low_keep(v):
    return (low(v), None)

def low_pass(kept, grad):
    return (grad,)

def back_keep(v):
    return (v, None)

def back_low(kept, grad):
    return (low(grad),)
low.defvjp(low_keep, low_pass)
low_back.defvjp(back_keep, back_low)

def span_layout(doc_count, single_flag):
    slot_total = single_flag.shape[1]
    places = jnp.arange(slot_total, dtype=jnp.int32)
    live_doc = places[None, :] < doc_count[:, None]
    length = jnp.where(live_doc, 2 - single_flag, 0).astype(jnp.int32)
    begins = (jnp.cumsum(length, axis=1).astype(jnp.int32) - length).astype(jnp.int32)
    inside = (places[None, :, None] >= begins[:, None, :]) & (places[None, :, None] < (begins + length)[:, None, :])
    live = jnp.any(inside, axis=2)
    double = inside & (length[:, None, :] == 2)
    has_pair = jnp.any(double, axis=2)
    other = lax.optimization_barrier(jnp.sum(jnp.where(double, 2 * begins[:, None, :] + 1 - places[None, :, None], 0), axis=2)).astype(jnp.int32)
    other = jnp.where(has_pair, other, places[None, :]).astype(jnp.int32)
    offsets = (jnp.arange(single_flag.shape[0], dtype=jnp.int32) * slot_total).astype(jnp.int32)
    return (live, has_pair, (offsets[:, None] + other).astype(jnp.int32))

def layer_norm(values, gain, shift):
    centered = values - lax.optimization_barrier(jnp.mean(values, axis=1, keepdims=True))
    scale = lax.rsqrt(lax.optimization_barrier(jnp.mean(centered * centered, axis=1, keepdims=True)) + ln_eps)
    return centered * scale * gain + shift

def layer_rows(inputs, params):
    w_qkv, b_query, b_value, w_out, b_out, gain_one, shift_one, w_in, b_in, w_ff_out, b_ff_out, gain_two, shift_two = params
    row_count = inputs.shape[0]
    span_count = row_count // SPAN_LEN
    shape_four = (span_count, SPAN_LEN, HEADS, HEAD_DIM)
    packed = jnp.dot(low(inputs), w_qkv, precision=highest)
    queries = low(low_back(packed[:, :D] + b_query)).reshape(shape_four)
    keys_low = low(low_back(packed[:, D:2 * D])).reshape(shape_four)
    values_low = low(low_back(packed[:, 2 * D:] + b_value)).reshape(shape_four)
    scores = low_back(jnp.einsum('slhe,smhe->shlm', queries, keys_low, precision=highest) * HEAD_DIM ** (-0.5))
    score_top = lax.optimization_barrier(jnp.max(scores, axis=3, keepdims=True))
    shifted = jnp.exp(scores - score_top)
    probs = shifted / lax.optimization_barrier(jnp.sum(shifted, axis=3, keepdims=True))
    context = jnp.einsum('shlm,smhe->slhe', low(probs), values_low, precision=highest).reshape(row_count, D)
    context = low(low_back(context))
    attended = low_back(jnp.dot(context, w_out, precision=highest) + b_out)
    mixed = layer_norm(inputs + attended, gain_one, shift_one)
    hidden = low_back(jnp.dot(low(mixed), w_in, precision=highest) + b_in)
    act = low(jax.nn.gelu(hidden, approximate=False))
    ffn = low_back(jnp.dot(act, w_ff_out, precision=highest) + b_ff_out)
    return layer_norm(mixed + ffn, gain_two, shift_two)

def forward(inputs, params, live, has_pair, mate):
    groups = inputs.reshape(N_WIDE, -1, D)
    block_float = lax.map(jax.checkpoint(partial(layer_rows, params=params)), groups).reshape(-1, D)
    cls = low(block_float.reshape(-1, SPAN_LEN, D)[:, 0, :])
    sims = low_back(score_scale * jnp.dot(cls, cls.T, precision=highest))
    idents = jnp.arange(cls.shape[0], dtype=jnp.int32)
    allowed = live[None, :] & (idents[None, :] != idents[:, None])
    masked = jnp.where(allowed, sims, far_low)
    row_top = lax.optimization_barrier(jnp.max(masked, axis=1))
    log_total = row_top + jnp.log(lax.optimization_barrier(jnp.sum(jnp.exp(masked - row_top[:, None]), axis=1)))
    positive = lax.optimization_barrier(jnp.sum(jnp.where(idents[None, :] == mate[:, None], sims, 0.0), axis=1))
    span_loss = jnp.where(has_pair, log_total - positive, 0.0)
    loss = jnp.sum(span_loss)
    return (block_float, loss, span_loss)

def as_float(array):
    return array.astype(jnp.float32)

def reference(hidden_in, out_grad, w_qkv, b_query, b_value, w_out, b_out, ln1_gain, ln1_bias, w_in, b_in, w_ff_out, b_ff_out, ln2_gain, ln2_bias, doc_count, single_flag):
    live, has_pair, mate = span_layout(doc_count, single_flag)
    live = live.reshape(-1)
    has_pair = has_pair.reshape(-1)
    mate = mate.reshape(-1).astype(jnp.int32)
    inputs = hidden_in.astype(jnp.float32)
    params = tuple(map(as_float, (w_qkv, b_query, b_value, w_out, b_out, ln1_gain, ln1_bias, w_in, b_in, w_ff_out, b_ff_out, ln2_gain, ln2_bias)))

    def objective(rows_in, weights):
        return forward(rows_in, weights, live, has_pair, mate)
    (block_float, loss, span_loss), pull_back = jax.vjp(objective, inputs, params)
    later_tokens = jnp.arange(block_float.shape[0], dtype=jnp.int32) % SPAN_LEN != 0
    cotangent = jnp.where(later_tokens[:, None], out_grad.astype(jnp.float32), 0.0)
    grad_in, grads = pull_back((cotangent, jnp.ones_like(loss), jnp.zeros_like(span_loss)))
    return (block_float.astype(jnp.bfloat16), loss, span_loss, grad_in, grads[0], grads[1], grads[2], grads[3], grads[4], grads[5], grads[6], grads[7], grads[8], grads[9], grads[10], grads[11], grads[12])
```

```python
import functools

import jax
import jax.numpy as jnp
from jax import lax
from jax.experimental import pallas as pl
from jax.experimental.pallas import tpu as pltpu
from jax.sharding import PartitionSpec as P

HEADS = 12
HEAD_DIM = 64
SPAN_LEN = 128


ln_eps = 1e-06
score_scale = 0.2
far_low = -1000000000.0


def matmul(left, right):
    return jnp.dot(left, right, preferred_element_type=jnp.float32)


def matmul_left_t(left, right):
    return lax.dot_general(
        left, right, (((0,), (0,)), ((), ())), preferred_element_type=jnp.float32
    )


def matmul_right_t(left, right):
    return lax.dot_general(
        left, right, (((1,), (1,)), ((), ())), preferred_element_type=jnp.float32
    )


def split_heads(block, span_count):
    return block.reshape(span_count, SPAN_LEN, HEADS, HEAD_DIM)


def head_scores(queries, keys_low):
    return jnp.einsum(
        "slhe,smhe->shlm", queries, keys_low, preferred_element_type=jnp.float32
    ) * HEAD_DIM ** (-0.5)


def layer_norm_parts(values, gain, shift):
    centered = values - jnp.mean(values, axis=1, keepdims=True)
    scale = lax.rsqrt(jnp.mean(centered * centered, axis=1, keepdims=True) + ln_eps)
    normed = centered * scale
    return (normed * gain + shift, normed, scale)


def norm_back(upstream, normed, scale, gain):
    scaled = upstream * gain
    return scale * (
        scaled
        - jnp.mean(scaled, axis=1, keepdims=True)
        - normed * jnp.mean(scaled * normed, axis=1, keepdims=True)
    )


def exact_gelu(values):
    return jax.nn.gelu(values, approximate=False)


def contrast_kernel(own_ref, cls_ref, count_ref, flag_ref, grad_ref, own_loss_ref, loss_ref):
    total, width = cls_ref.shape
    docsets, slots = flag_ref.shape
    span_count = grad_ref.shape[0]
    first = own_ref[0] * span_count
    block = min(total, 256)
    f32, bf16, i32 = jnp.float32, jnp.bfloat16, jnp.int32

    def layout(at):
        slot = at + lax.broadcasted_iota(i32, (block, 1), 0)
        device = slot // slots
        place = (slot - device * slots).astype(f32)
        member = lax.broadcasted_iota(i32, (block, docsets), 1) == device
        count = jnp.sum(jnp.where(member, count_ref[...].astype(f32), 0.0), axis=1, keepdims=True)
        flags = jnp.dot(
            member.astype(bf16), flag_ref[...].astype(bf16), preferred_element_type=f32
        )
        doc = lax.broadcasted_iota(i32, (block, slots), 1).astype(f32)
        length = jnp.where(doc < count, 2.0 - flags, 0.0)
        earlier = lax.broadcasted_iota(i32, (slots, slots), 0) < lax.broadcasted_iota(
            i32, (slots, slots), 1
        )
        begins = jnp.dot(length.astype(bf16), earlier.astype(bf16), preferred_element_type=f32)
        inside = (place >= begins) & (place < begins + length)
        double = inside & (length == 2.0)
        live = jnp.max(inside.astype(f32), axis=1, keepdims=True)
        pair = jnp.max(double.astype(f32), axis=1, keepdims=True)
        other = jnp.sum(jnp.where(double, 2.0 * begins + 1.0 - place, 0.0), axis=1, keepdims=True)
        mate = jnp.where(pair > 0.0, device * slots + other.astype(i32), slot)
        return slot, live, pair, mate

    eye = lax.broadcasted_iota(i32, (block, block), 0) == lax.broadcasted_iota(
        i32, (block, block), 1
    )
    live_row = jnp.concatenate(
        [
            jnp.sum(jnp.where(eye, layout(at)[1], 0.0), axis=0, keepdims=True)
            for at in range(0, total, block)
        ],
        axis=1,
    )
    column = lax.broadcasted_iota(i32, (block, total), 1)
    pick_col = (
        lax.broadcasted_iota(i32, (span_count, total), 1)
        == first + lax.broadcasted_iota(i32, (span_count, total), 0)
    ).astype(bf16)
    rows_own = jnp.zeros((span_count, total), f32)
    upward = jnp.zeros((span_count, width), f32)
    own_loss = jnp.zeros((1, span_count), f32)
    loss = jnp.zeros((1, 1), f32)
    for at in range(0, total, block):
        slot, live, pair, mate = layout(at)
        cls_block = cls_ref[at : at + block, :]
        sims = score_scale * lax.dot_general(
            cls_block, cls_ref[...], (((1,), (1,)), ((), ())), preferred_element_type=f32
        )
        allowed = (live_row > 0.0) & (column != slot)
        masked = jnp.where(allowed, sims, far_low)
        top = jnp.max(masked, axis=1, keepdims=True)
        lse = top + jnp.log(jnp.sum(jnp.exp(masked - top), axis=1, keepdims=True))
        matches = column == mate
        positive = jnp.sum(jnp.where(matches, sims, 0.0), axis=1, keepdims=True)
        span_loss = jnp.where(pair > 0.0, lse - positive, 0.0)
        loss = loss + jnp.sum(span_loss, axis=0, keepdims=True)
        mine = slot == first + lax.broadcasted_iota(i32, (block, span_count), 1)
        own_loss = own_loss + jnp.sum(jnp.where(mine, span_loss, 0.0), axis=0, keepdims=True)
        sim_grad = jnp.where(
            pair > 0.0, jnp.exp(masked - lse) - matches.astype(f32), 0.0
        ).astype(bf16)
        pick_row = (
            at + lax.broadcasted_iota(i32, (span_count, block), 1)
            == first + lax.broadcasted_iota(i32, (span_count, block), 0)
        ).astype(bf16)
        rows_own = rows_own + jnp.dot(pick_row, sim_grad, preferred_element_type=f32)
        cols_own = lax.dot_general(
            pick_col, sim_grad, (((1,), (1,)), ((), ())), preferred_element_type=f32
        )
        upward = upward + jnp.dot(cols_own.astype(bf16), cls_block, preferred_element_type=f32)
    upward = upward + jnp.dot(rows_own.astype(bf16), cls_ref[...], preferred_element_type=f32)
    grad_ref[...] = score_scale * upward
    own_loss_ref[...] = own_loss
    loss_ref[...] = loss


def contrast(cls_all, doc_count, single_flag, own, span_count):
    total, width = cls_all.shape
    vmem = pl.BlockSpec(memory_space=pltpu.VMEM)
    cls_grad, own_loss, loss = pl.pallas_call(
        contrast_kernel,
        out_shape=(
            jax.ShapeDtypeStruct((span_count, width), jnp.float32),
            jax.ShapeDtypeStruct((1, span_count), jnp.float32),
            jax.ShapeDtypeStruct((1, 1), jnp.float32),
        ),
        in_specs=[pl.BlockSpec(memory_space=pltpu.SMEM), vmem, vmem, vmem],
        out_specs=(vmem, vmem, vmem),
        compiler_params=pltpu.CompilerParams(vmem_limit_bytes=48 * 1024 * 1024),
        name="contrast",
    )(own.reshape(1), cls_all, doc_count.reshape(1, -1), single_flag)
    return cls_grad, own_loss.reshape(-1), loss.reshape(())


def per_device(
    hidden_in,
    out_grad,
    w_qkv,
    b_query,
    b_value,
    w_out,
    b_out,
    ln1_gain,
    ln1_bias,
    w_in,
    b_in,
    w_ff_out,
    b_ff_out,
    ln2_gain,
    ln2_bias,
    doc_count,
    single_flag,
):
    row_count, model_width = hidden_in.shape
    span_count = row_count // SPAN_LEN
    head_scale = HEAD_DIM ** (-0.5)
    inputs = hidden_in.astype(jnp.float32)
    gain_one = ln1_gain.astype(jnp.float32)
    gain_two = ln2_gain.astype(jnp.float32)
    packed = matmul(hidden_in, w_qkv)
    queries = split_heads(
        (packed[:, :model_width] + b_query.astype(jnp.float32)).astype(jnp.bfloat16), span_count
    )
    keys_low = split_heads(
        packed[:, model_width : 2 * model_width].astype(jnp.bfloat16), span_count
    )
    values_low = split_heads(
        (packed[:, 2 * model_width :] + b_value.astype(jnp.float32)).astype(jnp.bfloat16),
        span_count,
    )
    scores = head_scores(queries, keys_low)
    score_top = jnp.max(scores, axis=3, keepdims=True)
    shifted = jnp.exp(scores - score_top)
    score_total = jnp.sum(shifted, axis=3, keepdims=True)
    log_total = score_top + jnp.log(score_total)
    probs_low = (shifted / score_total).astype(jnp.bfloat16)
    context = jnp.einsum(
        "shlm,smhe->slhe", probs_low, values_low, preferred_element_type=jnp.float32
    )
    context = context.reshape(row_count, model_width).astype(jnp.bfloat16)
    attended = matmul(context, w_out) + b_out.astype(jnp.float32)
    mixed, normed_one, scale_one = layer_norm_parts(
        inputs + attended, gain_one, ln1_bias.astype(jnp.float32)
    )
    mixed_low = mixed.astype(jnp.bfloat16)
    hidden = matmul(mixed_low, w_in) + b_in.astype(jnp.float32)
    activation, gelu_back = jax.vjp(exact_gelu, hidden)
    act_low = activation.astype(jnp.bfloat16)
    ffn = matmul(act_low, w_ff_out) + b_ff_out.astype(jnp.float32)
    block_float, normed_two, scale_two = layer_norm_parts(
        mixed + ffn, gain_two, ln2_bias.astype(jnp.float32)
    )
    block_out = block_float.astype(jnp.bfloat16)
    cls_low = block_out.reshape(span_count, SPAN_LEN, model_width)[:, 0, :]
    cls_all = lax.all_gather(cls_low, ("wide", "narrow"), axis=0, tiled=True)
    own = lax.axis_index("wide") * lax.axis_size("narrow") + lax.axis_index("narrow")
    cls_grad, span_loss, loss_part = contrast(
        cls_all, doc_count, single_flag, own.astype(jnp.int32), span_count
    )
    upper_grad = out_grad.astype(jnp.float32).reshape(span_count, SPAN_LEN, model_width)
    top_grad = jnp.concatenate([cls_grad[:, None, :], upper_grad[:, 1:, :]], axis=1).reshape(
        row_count, model_width
    )
    grad_ln2_gain = jnp.sum(top_grad * normed_two, axis=0)
    grad_ln2_bias = jnp.sum(top_grad, axis=0)
    pre_two_grad = norm_back(top_grad, normed_two, scale_two, gain_two)
    ffn_grad = pre_two_grad.astype(jnp.bfloat16)
    grad_b_ff_out = jnp.sum(ffn_grad.astype(jnp.float32), axis=0)
    grad_w_ff_out = matmul_left_t(act_low, ffn_grad)
    hidden_grad = gelu_back(matmul_right_t(ffn_grad, w_ff_out))[0].astype(jnp.bfloat16)
    grad_b_in = jnp.sum(hidden_grad.astype(jnp.float32), axis=0)
    grad_w_in = matmul_left_t(mixed_low, hidden_grad)
    mixed_grad = pre_two_grad + matmul_right_t(hidden_grad, w_in)
    grad_ln1_gain = jnp.sum(mixed_grad * normed_one, axis=0)
    grad_ln1_bias = jnp.sum(mixed_grad, axis=0)
    pre_one_grad = norm_back(mixed_grad, normed_one, scale_one, gain_one)
    attn_grad = pre_one_grad.astype(jnp.bfloat16)
    grad_b_out = jnp.sum(attn_grad.astype(jnp.float32), axis=0)
    grad_w_out = matmul_left_t(context, attn_grad)
    context_grad = split_heads(matmul_right_t(attn_grad, w_out).astype(jnp.bfloat16), span_count)
    probs_again = jnp.exp(head_scores(queries, keys_low) - log_total)
    probs_again_low = probs_again.astype(jnp.bfloat16)
    value_grad = jnp.einsum(
        "shlm,slhe->smhe", probs_again_low, context_grad, preferred_element_type=jnp.float32
    ).astype(jnp.bfloat16)
    prob_grad = jnp.einsum(
        "slhe,smhe->shlm", context_grad, values_low, preferred_element_type=jnp.float32
    )
    score_grad = (
        probs_again * (prob_grad - jnp.sum(probs_again * prob_grad, axis=3, keepdims=True))
    ).astype(jnp.bfloat16)
    query_grad = (
        jnp.einsum("shlm,smhe->slhe", score_grad, keys_low, preferred_element_type=jnp.float32)
        * head_scale
    ).astype(jnp.bfloat16)
    key_grad = (
        jnp.einsum("shlm,slhe->smhe", score_grad, queries, preferred_element_type=jnp.float32)
        * head_scale
    ).astype(jnp.bfloat16)
    query_grad = query_grad.reshape(row_count, model_width)
    key_grad = key_grad.reshape(row_count, model_width)
    value_grad = value_grad.reshape(row_count, model_width)
    packed_grad = jnp.concatenate([query_grad, key_grad, value_grad], axis=1)
    grad_b_query = jnp.sum(query_grad.astype(jnp.float32), axis=0)
    grad_b_value = jnp.sum(value_grad.astype(jnp.float32), axis=0)
    grad_w_qkv = matmul_left_t(hidden_in, packed_grad)
    grad_in = pre_one_grad + matmul_right_t(packed_grad, w_qkv)
    both = ("wide", "narrow")
    grad_w_ff_out, grad_w_in, grad_w_out, grad_w_qkv = (
        lax.psum(grad.astype(jnp.bfloat16), both).astype(jnp.float32)
        for grad in (grad_w_ff_out, grad_w_in, grad_w_out, grad_w_qkv)
    )
    vectors = (
        grad_b_query,
        grad_b_value,
        grad_b_out,
        grad_ln1_gain,
        grad_ln1_bias,
        grad_b_ff_out,
        grad_ln2_gain,
        grad_ln2_bias,
        grad_b_in,
    )
    joined = lax.psum(jnp.concatenate(vectors), both)
    (
        grad_b_query,
        grad_b_value,
        grad_b_out,
        grad_ln1_gain,
        grad_ln1_bias,
        grad_b_ff_out,
        grad_ln2_gain,
        grad_ln2_bias,
        grad_b_in,
    ) = jnp.split(joined, [model_width * k for k in range(1, 9)])
    return (
        block_out,
        loss_part,
        span_loss,
        grad_in,
        grad_w_qkv,
        grad_b_query,
        grad_b_value,
        grad_w_out,
        grad_b_out,
        grad_ln1_gain,
        grad_ln1_bias,
        grad_w_in,
        grad_b_in,
        grad_w_ff_out,
        grad_b_ff_out,
        grad_ln2_gain,
        grad_ln2_bias,
    )


def solution(mesh):
    placed = (
        P(("wide", "narrow"), None),
        P(("wide", "narrow"), None),
        P(),
        P(),
        P(),
        P(),
        P(),
        P(),
        P(),
        P(),
        P(),
        P(),
        P(),
        P(),
        P(),
        P(),
        P(),
    )
    return jax.shard_map(
        per_device,
        mesh=mesh,
        in_specs=placed,
        out_specs=(
            P(("wide", "narrow"), None),
            P(),
            P(("wide", "narrow")),
            P(("wide", "narrow"), None),
            P(),
            P(),
            P(),
            P(),
            P(),
            P(),
            P(),
            P(),
            P(),
            P(),
            P(),
            P(),
            P(),
        ),
        check_vma=False,
    )
```

```python
import functools

import jax
import jax.numpy as jnp
from jax import lax
from jax.experimental import pallas as pl
from jax.experimental.pallas import tpu as pltpu
from jax.sharding import PartitionSpec as P

HEADS = 12
HEAD_DIM = 64
SPAN_LEN = 128


ln_eps = 1e-06
score_scale = 0.2
far_low = -1000000000.0


def matmul(left, right):
    return jnp.dot(left, right, preferred_element_type=jnp.float32)


def matmul_left_t(left, right):
    return lax.dot_general(
        left, right, (((0,), (0,)), ((), ())), preferred_element_type=jnp.float32
    )


def matmul_right_t(left, right):
    return lax.dot_general(
        left, right, (((1,), (1,)), ((), ())), preferred_element_type=jnp.float32
    )


def split_heads(block, span_count):
    return block.reshape(span_count, SPAN_LEN, HEADS, HEAD_DIM)


def head_scores(queries, keys_low):
    return jnp.einsum(
        "slhe,smhe->shlm", queries, keys_low, preferred_element_type=jnp.float32
    ) * HEAD_DIM ** (-0.5)


def layer_norm_parts(values, gain, shift):
    centered = values - jnp.mean(values, axis=1, keepdims=True)
    scale = lax.rsqrt(jnp.mean(centered * centered, axis=1, keepdims=True) + ln_eps)
    normed = centered * scale
    return (normed * gain + shift, normed, scale)


def norm_back(upstream, normed, scale, gain):
    scaled = upstream * gain
    return scale * (
        scaled
        - jnp.mean(scaled, axis=1, keepdims=True)
        - normed * jnp.mean(scaled * normed, axis=1, keepdims=True)
    )


def exact_gelu(values):
    return jax.nn.gelu(values, approximate=False)


def contrast_kernel(own_ref, cls_ref, count_ref, flag_ref, grad_ref, own_loss_ref, loss_ref):
    total, width = cls_ref.shape
    docsets, slots = flag_ref.shape
    span_count = grad_ref.shape[0]
    first = own_ref[0] * span_count
    block = min(total, 256)
    f32, bf16, i32 = jnp.float32, jnp.bfloat16, jnp.int32

    def layout(at):
        slot = at + lax.broadcasted_iota(i32, (block, 1), 0)
        device = slot // slots
        place = (slot - device * slots).astype(f32)
        member = lax.broadcasted_iota(i32, (block, docsets), 1) == device
        count = jnp.sum(jnp.where(member, count_ref[...].astype(f32), 0.0), axis=1, keepdims=True)
        flags = jnp.dot(
            member.astype(bf16), flag_ref[...].astype(bf16), preferred_element_type=f32
        )
        doc = lax.broadcasted_iota(i32, (block, slots), 1).astype(f32)
        length = jnp.where(doc < count, 2.0 - flags, 0.0)
        earlier = lax.broadcasted_iota(i32, (slots, slots), 0) < lax.broadcasted_iota(
            i32, (slots, slots), 1
        )
        begins = jnp.dot(length.astype(bf16), earlier.astype(bf16), preferred_element_type=f32)
        inside = (place >= begins) & (place < begins + length)
        double = inside & (length == 2.0)
        live = jnp.max(inside.astype(f32), axis=1, keepdims=True)
        pair = jnp.max(double.astype(f32), axis=1, keepdims=True)
        other = jnp.sum(jnp.where(double, 2.0 * begins + 1.0 - place, 0.0), axis=1, keepdims=True)
        mate = jnp.where(pair > 0.0, device * slots + other.astype(i32), slot)
        return slot, live, pair, mate

    eye = lax.broadcasted_iota(i32, (block, block), 0) == lax.broadcasted_iota(
        i32, (block, block), 1
    )
    live_row = jnp.concatenate(
        [
            jnp.sum(jnp.where(eye, layout(at)[1], 0.0), axis=0, keepdims=True)
            for at in range(0, total, block)
        ],
        axis=1,
    )
    column = lax.broadcasted_iota(i32, (block, total), 1)
    pick_col = (
        lax.broadcasted_iota(i32, (span_count, total), 1)
        == first + lax.broadcasted_iota(i32, (span_count, total), 0)
    ).astype(bf16)
    rows_own = jnp.zeros((span_count, total), f32)
    upward = jnp.zeros((span_count, width), f32)
    own_loss = jnp.zeros((1, span_count), f32)
    loss = jnp.zeros((1, 1), f32)
    for at in range(0, total, block):
        slot, live, pair, mate = layout(at)
        cls_block = cls_ref[at : at + block, :]
        sims = score_scale * lax.dot_general(
            cls_block, cls_ref[...], (((1,), (1,)), ((), ())), preferred_element_type=f32
        )
        allowed = (live_row > 0.0) & (column != slot)
        masked = jnp.where(allowed, sims, far_low)
        top = jnp.max(masked, axis=1, keepdims=True)
        lse = top + jnp.log(jnp.sum(jnp.exp(masked - top), axis=1, keepdims=True))
        matches = column == mate
        positive = jnp.sum(jnp.where(matches, sims, 0.0), axis=1, keepdims=True)
        span_loss = jnp.where(pair > 0.0, lse - positive, 0.0)
        loss = loss + jnp.sum(span_loss, axis=0, keepdims=True)
        mine = slot == first + lax.broadcasted_iota(i32, (block, span_count), 1)
        own_loss = own_loss + jnp.sum(jnp.where(mine, span_loss, 0.0), axis=0, keepdims=True)
        sim_grad = jnp.where(
            pair > 0.0, jnp.exp(masked - lse) - matches.astype(f32), 0.0
        ).astype(bf16)
        pick_row = (
            at + lax.broadcasted_iota(i32, (span_count, block), 1)
            == first + lax.broadcasted_iota(i32, (span_count, block), 0)
        ).astype(bf16)
        rows_own = rows_own + jnp.dot(pick_row, sim_grad, preferred_element_type=f32)
        cols_own = lax.dot_general(
            pick_col, sim_grad, (((1,), (1,)), ((), ())), preferred_element_type=f32
        )
        upward = upward + jnp.dot(cols_own.astype(bf16), cls_block, preferred_element_type=f32)
    upward = upward + jnp.dot(rows_own.astype(bf16), cls_ref[...], preferred_element_type=f32)
    grad_ref[...] = score_scale * upward
    own_loss_ref[...] = own_loss
    loss_ref[...] = loss


def contrast(cls_all, doc_count, single_flag, own, span_count):
    total, width = cls_all.shape
    vmem = pl.BlockSpec(memory_space=pltpu.VMEM)
    cls_grad, own_loss, loss = pl.pallas_call(
        contrast_kernel,
        out_shape=(
            jax.ShapeDtypeStruct((span_count, width), jnp.float32),
            jax.ShapeDtypeStruct((1, span_count), jnp.float32),
            jax.ShapeDtypeStruct((1, 1), jnp.float32),
        ),
        in_specs=[pl.BlockSpec(memory_space=pltpu.SMEM), vmem, vmem, vmem],
        out_specs=(vmem, vmem, vmem),
        compiler_params=pltpu.CompilerParams(vmem_limit_bytes=48 * 1024 * 1024),
        name="contrast",
    )(own.reshape(1), cls_all, doc_count.reshape(1, -1), single_flag)
    return cls_grad, own_loss.reshape(-1), loss.reshape(())


MESH = pl.DeviceIdType.MESH
TICKS = 6

def ar_kernel(n_x, n_z, ffo_ref, in_ref, out_ref, qkv_ref, vec_ref, o_ffo, o_rest, o_vec, part, sib, r1, r2, r3, vbuf, lsem, s_sem, r_sem, zs_sem, zr_sem, vs_sem, vr_sem):
    W = part.shape[2]
    H, Q = W // 2, W // 4
    E = Q // n_z
    wide, narrow = lax.axis_index("wide"), lax.axis_index("narrow")
    z, x = wide // n_x, wide % n_x
    y, c = narrow // 2, narrow % 2
    f32 = jnp.float32
    core = (wide, y * 2 + 1 - c)
    near_x = (z * n_x + 1 - x, narrow)
    near_y = (wide, (1 - y) * 2 + c)
    one = (jnp.where(c == 0, near_x[0], near_y[0]), jnp.where(c == 0, near_x[1], near_y[1]))
    two = (jnp.where(c == 0, near_y[0], near_x[0]), jnp.where(c == 0, near_y[1], near_x[1]))
    h1 = jnp.where(c == 0, x, y)
    h2 = jnp.where(c == 0, y, x)
    others = [lax.rem(z + k, n_z) for k in range(1, n_z)]
    zdev = [(o * n_x + x, narrow) for o in others]

    bar = pltpu.get_barrier_semaphore()
    for d in [core, near_x, near_y] + zdev:
        pl.semaphore_signal(bar, inc=1, device_id=d, device_id_type=MESH)

    loads = []
    for b in range(2 * TICKS):
        if b < 4:
            src = ffo_ref.at[pl.ds(b * W, W), :]
        elif b < 8:
            src = in_ref.at[:, pl.ds((b - 4) * W, W)]
        elif b < 9:
            src = out_ref
        else:
            src = qkv_ref.at[:, pl.ds((b - 9) * W, W)]
        cp = pltpu.make_async_copy(src, part.at[b], lsem.at[b])
        cp.start()
        loads.append(cp)
    pl.semaphore_wait(bar, 2 + n_z)

    def out_at(t, row, rows):
        if t < 2:
            return o_ffo.at[pl.ds(pl.multiple_of((2 * t + c) * W + row, 16), rows), :]
        return o_rest.at[pl.ds(pl.multiple_of(row, 16), rows), pl.ds(pl.multiple_of((2 * (t - 2) + c) * W, 128), W)]

    def rcopy(src, dst, k, t, dev):
        return pltpu.make_async_remote_copy(src, dst, s_sem.at[k, t], r_sem.at[k, t], device_id=dev, device_id_type=MESH)

    def add(t, row, rows, got):
        mine = 2 * t + c
        def body(i, _):
            at = pl.multiple_of(row + i * 48, 16)
            here = part[mine, pl.ds(at, 48), :].astype(f32) + got[pl.ds(pl.multiple_of(i * 48, 16), 48), :].astype(f32)
            part[mine, pl.ds(at, 48), :] = here.astype(jnp.bfloat16)
            return 0
        lax.fori_loop(0, rows // 48, body, 0)

    keep1 = h1 * H
    keep2 = keep1 + h2 * Q
    own = keep2 + z * E
    flight = {}
    def c0(t):
        return rcopy(part.at[2 * t + 1 - c], sib.at[t], 0, t, core)
    def c1(t):
        return rcopy(part.at[2 * t + c, pl.ds(pl.multiple_of((1 - h1) * H, 16), H), :], r1.at[t], 1, t, one)
    def c2(t):
        return rcopy(part.at[2 * t + c, pl.ds(pl.multiple_of(keep1 + (1 - h2) * Q, 16), Q), :], r2.at[t], 2, t, two)
    def c3(t):
        return [pltpu.make_async_remote_copy(
            part.at[2 * t + c, pl.ds(pl.multiple_of(keep2 + o * E, 16), E), :], r3.at[t, k],
            zs_sem.at[0, t, k], zr_sem.at[0, t, k], device_id=d, device_id_type=MESH)
            for k, (o, d) in enumerate(zip(others, zdev))]
    def c4(t):
        return [pltpu.make_async_remote_copy(
            out_at(t, own, E), out_at(t, own, E), zs_sem.at[1, t, k], zr_sem.at[1, t, k], device_id=d, device_id_type=MESH)
            for k, d in enumerate(zdev)]
    def c5(t):
        return rcopy(out_at(t, keep2, Q), out_at(t, keep2, Q), 3, t, two)
    def c6(t):
        return rcopy(out_at(t, keep1, H), out_at(t, keep1, H), 4, t, one)
    def c7(t):
        return rcopy(out_at(t, 0, W), out_at(t, 0, W), 5, t, core)

    def st0(t):
        loads[2 * t].wait(); loads[2 * t + 1].wait()
        c0(t).start()
    def st1(t):
        c0(t).wait()
        add(t, 0, W, sib.at[t])
        c1(t).start()
    def st2(t):
        c1(t).wait()
        add(t, keep1, H, r1.at[t])
        c2(t).start()
    def st3(t):
        c2(t).wait()
        add(t, keep2, Q, r2.at[t])
        for cp in c3(t): cp.start()
    def st4(t):
        for cp in c3(t): cp.wait()
        total = part[2 * t + c, pl.ds(pl.multiple_of(own, 16), E), :].astype(f32)
        for k in range(n_z - 1):
            total = total + r3[t, k].astype(f32)
        part[2 * t + c, pl.ds(pl.multiple_of(own, 16), E), :] = total.astype(jnp.bfloat16)
        cp = pltpu.make_async_copy(part.at[2 * t + c, pl.ds(pl.multiple_of(own, 16), E), :], out_at(t, own, E), lsem.at[2 * TICKS + t])
        cp.start(); cp.wait()
        for cp in c4(t): cp.start()
    def st5(t):
        for cp in c4(t): cp.wait()
        c5(t).start()
    def st6(t):
        c5(t).wait()
        c6(t).start()
    def st7(t):
        c6(t).wait()
        c7(t).start()
    def st8(t):
        c7(t).wait()

    def vcopy(k, dev):
        return pltpu.make_async_remote_copy(vbuf.at[2 * k], vbuf.at[2 * k + 1], vs_sem.at[k], vr_sem.at[k], device_id=dev, device_id_type=MESH)
    def vz():
        return [pltpu.make_async_remote_copy(vbuf.at[6], vbuf.at[7 + k], vs_sem.at[3 + k], vr_sem.at[3 + k], device_id=d, device_id_type=MESH) for k, d in enumerate(zdev)]
    def vstep(k):
        if k == 0:
            vbuf[0] = vec_ref[...]
            vcopy(0, core).start()
        elif k == 1:
            vcopy(0, core).wait()
            vbuf[2] = vbuf[0] + vbuf[1]
            vcopy(1, near_x).start()
        elif k == 2:
            vcopy(1, near_x).wait()
            vbuf[4] = vbuf[2] + vbuf[3]
            vcopy(2, near_y).start()
        elif k == 3:
            vcopy(2, near_y).wait()
            vbuf[6] = vbuf[4] + vbuf[5]
            for cp in vz(): cp.start()
        elif k == 4:
            for cp in vz(): cp.wait()
            total = vbuf[6]
            for k in range(n_z - 1):
                total = total + vbuf[7 + k]
            o_vec[...] = total

    stages = [st1, st2, st3, st4, st5, st6, st7, st8]
    for t in range(TICKS):
        st0(t)
    for step in range(TICKS + len(stages) - 1):
        if step >= 2: vstep(step - 2)
        for k, st in enumerate(stages):
            if 0 <= step - k < TICKS:
                st(step - k)

def all_reduce(ffo, inn, out, qkv, vec, n_x, n_z):
    W = ffo.shape[1]
    rest = jax.ShapeDtypeStruct((W, 8 * W), jnp.bfloat16)
    bf = jnp.bfloat16
    anyspec = pl.BlockSpec(memory_space=pl.ANY)
    vm = pl.BlockSpec(memory_space=pltpu.VMEM)
    T = TICKS
    return pl.pallas_call(
        functools.partial(ar_kernel, n_x, n_z),
        out_shape=(jax.ShapeDtypeStruct(ffo.shape, bf), jax.ShapeDtypeStruct(rest.shape, bf), jax.ShapeDtypeStruct(vec.shape, jnp.float32)),
        in_specs=[anyspec, anyspec, anyspec, anyspec, vm], out_specs=(anyspec, anyspec, vm),
        scratch_shapes=[
            pltpu.VMEM((2 * T, W, W), bf), pltpu.VMEM((T, W, W), bf), pltpu.VMEM((T, W // 2, W), bf), pltpu.VMEM((T, W // 4, W), bf),
            pltpu.VMEM((T, n_z - 1, W // 4 // n_z, W), bf), pltpu.VMEM((6 + n_z,) + vec.shape, jnp.float32),
            pltpu.SemaphoreType.DMA((3 * T,)), pltpu.SemaphoreType.DMA((6, T)), pltpu.SemaphoreType.DMA((6, T)),
            pltpu.SemaphoreType.DMA((2, T, n_z - 1)), pltpu.SemaphoreType.DMA((2, T, n_z - 1)),
            pltpu.SemaphoreType.DMA((2 + n_z,)), pltpu.SemaphoreType.DMA((2 + n_z,)),
        ],
        compiler_params=pltpu.CompilerParams(collective_id=0, has_side_effects=True, vmem_limit_bytes=56 * 2**20),
        name="grad_all_reduce",
    )(ffo, inn, out, qkv, vec)


def per_device(
    hidden_in,
    out_grad,
    w_qkv,
    b_query,
    b_value,
    w_out,
    b_out,
    ln1_gain,
    ln1_bias,
    w_in,
    b_in,
    w_ff_out,
    b_ff_out,
    ln2_gain,
    ln2_bias,
    doc_count,
    single_flag,
):
    row_count, model_width = hidden_in.shape
    span_count = row_count // SPAN_LEN
    head_scale = HEAD_DIM ** (-0.5)
    inputs = hidden_in.astype(jnp.float32)
    gain_one = ln1_gain.astype(jnp.float32)
    gain_two = ln2_gain.astype(jnp.float32)
    packed = matmul(hidden_in, w_qkv)
    queries = split_heads(
        (packed[:, :model_width] + b_query.astype(jnp.float32)).astype(jnp.bfloat16), span_count
    )
    keys_low = split_heads(
        packed[:, model_width : 2 * model_width].astype(jnp.bfloat16), span_count
    )
    values_low = split_heads(
        (packed[:, 2 * model_width :] + b_value.astype(jnp.float32)).astype(jnp.bfloat16),
        span_count,
    )
    scores = head_scores(queries, keys_low)
    score_top = jnp.max(scores, axis=3, keepdims=True)
    shifted = jnp.exp(scores - score_top)
    score_total = jnp.sum(shifted, axis=3, keepdims=True)
    log_total = score_top + jnp.log(score_total)
    probs_low = (shifted / score_total).astype(jnp.bfloat16)
    context = jnp.einsum(
        "shlm,smhe->slhe", probs_low, values_low, preferred_element_type=jnp.float32
    )
    context = context.reshape(row_count, model_width).astype(jnp.bfloat16)
    attended = matmul(context, w_out) + b_out.astype(jnp.float32)
    mixed, normed_one, scale_one = layer_norm_parts(
        inputs + attended, gain_one, ln1_bias.astype(jnp.float32)
    )
    mixed_low = mixed.astype(jnp.bfloat16)
    hidden = matmul(mixed_low, w_in) + b_in.astype(jnp.float32)
    activation, gelu_back = jax.vjp(exact_gelu, hidden)
    act_low = activation.astype(jnp.bfloat16)
    ffn = matmul(act_low, w_ff_out) + b_ff_out.astype(jnp.float32)
    block_float, normed_two, scale_two = layer_norm_parts(
        mixed + ffn, gain_two, ln2_bias.astype(jnp.float32)
    )
    block_out = block_float.astype(jnp.bfloat16)
    cls_low = block_out.reshape(span_count, SPAN_LEN, model_width)[:, 0, :]
    cls_all = lax.all_gather(cls_low, ("wide", "narrow"), axis=0, tiled=True)
    own = lax.axis_index("wide") * lax.axis_size("narrow") + lax.axis_index("narrow")
    cls_grad, span_loss, loss_part = contrast(
        cls_all, doc_count, single_flag, own.astype(jnp.int32), span_count
    )
    upper_grad = out_grad.astype(jnp.float32).reshape(span_count, SPAN_LEN, model_width)
    top_grad = jnp.concatenate([cls_grad[:, None, :], upper_grad[:, 1:, :]], axis=1).reshape(
        row_count, model_width
    )
    grad_ln2_gain = jnp.sum(top_grad * normed_two, axis=0)
    grad_ln2_bias = jnp.sum(top_grad, axis=0)
    pre_two_grad = norm_back(top_grad, normed_two, scale_two, gain_two)
    ffn_grad = pre_two_grad.astype(jnp.bfloat16)
    grad_b_ff_out = jnp.sum(ffn_grad.astype(jnp.float32), axis=0)
    grad_w_ff_out = matmul_left_t(act_low, ffn_grad)
    hidden_grad = gelu_back(matmul_right_t(ffn_grad, w_ff_out))[0].astype(jnp.bfloat16)
    grad_b_in = jnp.sum(hidden_grad.astype(jnp.float32), axis=0)
    grad_w_in = matmul_left_t(mixed_low, hidden_grad)
    mixed_grad = pre_two_grad + matmul_right_t(hidden_grad, w_in)
    grad_ln1_gain = jnp.sum(mixed_grad * normed_one, axis=0)
    grad_ln1_bias = jnp.sum(mixed_grad, axis=0)
    pre_one_grad = norm_back(mixed_grad, normed_one, scale_one, gain_one)
    attn_grad = pre_one_grad.astype(jnp.bfloat16)
    grad_b_out = jnp.sum(attn_grad.astype(jnp.float32), axis=0)
    grad_w_out = matmul_left_t(context, attn_grad)
    context_grad = split_heads(matmul_right_t(attn_grad, w_out).astype(jnp.bfloat16), span_count)
    probs_again = jnp.exp(head_scores(queries, keys_low) - log_total)
    probs_again_low = probs_again.astype(jnp.bfloat16)
    value_grad = jnp.einsum(
        "shlm,slhe->smhe", probs_again_low, context_grad, preferred_element_type=jnp.float32
    ).astype(jnp.bfloat16)
    prob_grad = jnp.einsum(
        "slhe,smhe->shlm", context_grad, values_low, preferred_element_type=jnp.float32
    )
    score_grad = (
        probs_again * (prob_grad - jnp.sum(probs_again * prob_grad, axis=3, keepdims=True))
    ).astype(jnp.bfloat16)
    query_grad = (
        jnp.einsum("shlm,smhe->slhe", score_grad, keys_low, preferred_element_type=jnp.float32)
        * head_scale
    ).astype(jnp.bfloat16)
    key_grad = (
        jnp.einsum("shlm,slhe->smhe", score_grad, queries, preferred_element_type=jnp.float32)
        * head_scale
    ).astype(jnp.bfloat16)
    query_grad = query_grad.reshape(row_count, model_width)
    key_grad = key_grad.reshape(row_count, model_width)
    value_grad = value_grad.reshape(row_count, model_width)
    packed_grad = jnp.concatenate([query_grad, key_grad, value_grad], axis=1)
    grad_b_query = jnp.sum(query_grad.astype(jnp.float32), axis=0)
    grad_b_value = jnp.sum(value_grad.astype(jnp.float32), axis=0)
    grad_w_qkv = matmul_left_t(hidden_in, packed_grad)
    grad_in = pre_one_grad + matmul_right_t(packed_grad, w_qkv)
    both = ("wide", "narrow")
    weights = [
        grad.astype(jnp.bfloat16) for grad in (grad_w_ff_out, grad_w_in, grad_w_out, grad_w_qkv)
    ]
    vectors = (
        grad_b_query,
        grad_b_value,
        grad_b_out,
        grad_ln1_gain,
        grad_ln1_bias,
        grad_b_ff_out,
        grad_ln2_gain,
        grad_ln2_bias,
        grad_b_in,
    )
    joined = jnp.concatenate(vectors)
    n_wide, n_narrow = lax.axis_size("wide"), lax.axis_size("narrow")
    n_x = n_narrow // 2
    n_z = n_wide // n_x
    if n_x == 2 and n_wide % n_x == 0 and model_width % (64 * n_z) == 0 and w_in.shape[1] == 4 * model_width:
        filled = jnp.pad(joined, (0, 4 * model_width)).reshape(16, model_width)
        grad_w_ff_out, rest, filled = all_reduce(*weights, filled, n_x, n_z)
        joined = filled.reshape(-1)[: joined.shape[0]]
        wide_in = w_in.shape[1]
        grad_w_in = rest[:, :wide_in].astype(jnp.float32)
        grad_w_out = rest[:, wide_in : wide_in + model_width].astype(jnp.float32)
        grad_w_qkv = rest[:, wide_in + model_width :].astype(jnp.float32)
        grad_w_ff_out = grad_w_ff_out.astype(jnp.float32)
    else:
        grad_w_ff_out, grad_w_in, grad_w_out, grad_w_qkv = (
            lax.psum(grad, both).astype(jnp.float32) for grad in weights
        )
        joined = lax.psum(joined, both)
    (
        grad_b_query,
        grad_b_value,
        grad_b_out,
        grad_ln1_gain,
        grad_ln1_bias,
        grad_b_ff_out,
        grad_ln2_gain,
        grad_ln2_bias,
        grad_b_in,
    ) = jnp.split(joined, [model_width * k for k in range(1, 9)])
    return (
        block_out,
        loss_part,
        span_loss,
        grad_in,
        grad_w_qkv,
        grad_b_query,
        grad_b_value,
        grad_w_out,
        grad_b_out,
        grad_ln1_gain,
        grad_ln1_bias,
        grad_w_in,
        grad_b_in,
        grad_w_ff_out,
        grad_b_ff_out,
        grad_ln2_gain,
        grad_ln2_bias,
    )


def solution(mesh):
    placed = (
        P(("wide", "narrow"), None),
        P(("wide", "narrow"), None),
        P(),
        P(),
        P(),
        P(),
        P(),
        P(),
        P(),
        P(),
        P(),
        P(),
        P(),
        P(),
        P(),
        P(),
        P(),
    )
    return jax.shard_map(
        per_device,
        mesh=mesh,
        in_specs=placed,
        out_specs=(
            P(("wide", "narrow"), None),
            P(),
            P(("wide", "narrow")),
            P(("wide", "narrow"), None),
            P(),
            P(),
            P(),
            P(),
            P(),
            P(),
            P(),
            P(),
            P(),
            P(),
            P(),
            P(),
            P(),
        ),
        check_vma=False,
    )
```

```python
import functools

import jax
import jax.numpy as jnp
from jax import lax
from jax.experimental import pallas as pl
from jax.experimental.pallas import tpu as pltpu
from jax.sharding import PartitionSpec as P

HEAD_DIM = 64
SPAN_LEN = 128
TILE = 256

ln_eps = 1e-06
score_scale = 0.2
far_low = -1000000000.0
head_scale = HEAD_DIM ** (-0.5)
MESH = pl.DeviceIdType.MESH
TICKS = 6
f32, bf16, i32 = jnp.float32, jnp.bfloat16, jnp.int32
MIB = 2**20


def dot(left, right):
    return jnp.dot(left, right, preferred_element_type=f32)


def dot_left_t(left, right):
    return lax.dot_general(left, right, (((0,), (0,)), ((), ())), preferred_element_type=f32)


def dot_right_t(left, right):
    return lax.dot_general(left, right, (((1,), (1,)), ((), ())), preferred_element_type=f32)


def row_mean(values):
    return jnp.mean(values, axis=1, keepdims=True)


def col_sum(values):
    return jnp.sum(values, axis=0, keepdims=True)


def norm_back(upstream, normed, scale, gain):
    scaled = upstream * gain
    return scale * (scaled - row_mean(scaled) - normed * row_mean(scaled * normed))


def head_halves():
    first = lax.broadcasted_iota(i32, (1, 2 * HEAD_DIM), 1) < HEAD_DIM
    return first, first.astype(bf16), jnp.logical_not(first).astype(bf16)


def pair_probs(stacked_queries, keys_low):
    scores = dot_right_t(stacked_queries, keys_low)
    shifted = jnp.exp((scores - jnp.max(scores, axis=1, keepdims=True)) * head_scale)
    return shifted * (1.0 / jnp.sum(shifted, axis=1, keepdims=True))


def attend_kernel(
    x_ref, w_qkv_ref, b_query_ref, b_value_ref, w_out_ref, b_out_ref, qkv_ref, context_ref, cent_ref
):
    rows, width = x_ref.shape
    inputs = x_ref[...]
    for third in range(3):
        cols = pl.ds(third * width, width)
        packed = dot(inputs, w_qkv_ref[:, cols])
        if third == 0:
            packed = packed + b_query_ref[...].astype(f32)
        if third == 2:
            packed = packed + b_value_ref[...].astype(f32)
        qkv_ref[:, cols] = packed.astype(bf16)
    first, low_one, low_two = head_halves()
    lanes = 2 * HEAD_DIM
    for span in range(rows // SPAN_LEN):
        at = pl.ds(span * SPAN_LEN, SPAN_LEN)
        for pair in range(width // lanes):
            queries = qkv_ref[at, pl.ds(pair * lanes, lanes)]
            keys_low = qkv_ref[at, pl.ds(width + pair * lanes, lanes)]
            values_low = qkv_ref[at, pl.ds(2 * width + pair * lanes, lanes)]
            stacked = jnp.concatenate([queries * low_one, queries * low_two], axis=0)
            mixed_values = dot(pair_probs(stacked, keys_low).astype(bf16), values_low)
            context_ref[at, pl.ds(pair * lanes, lanes)] = jnp.where(
                first, mixed_values[:SPAN_LEN], mixed_values[SPAN_LEN:]
            ).astype(bf16)
    attended = dot(context_ref[...], w_out_ref[...]) + b_out_ref[...].astype(f32)
    pre_one = inputs.astype(f32) + attended
    cent_ref[...] = pre_one - row_mean(pre_one)


def attend(x, w_qkv, b_query, b_value, w_out, b_out):
    rows, width = x.shape

    def whole(a):
        return pl.BlockSpec(a.shape, lambda i: (0, 0))

    def tiles(cols):
        return pl.BlockSpec((TILE, cols), lambda i: (i, 0))

    return pl.pallas_call(
        attend_kernel,
        grid=(rows // TILE,),
        out_shape=(
            jax.ShapeDtypeStruct((rows, 3 * width), bf16),
            jax.ShapeDtypeStruct((rows, width), bf16),
            jax.ShapeDtypeStruct((rows, width), f32),
        ),
        in_specs=[tiles(width)] + [whole(a) for a in (w_qkv, b_query, b_value, w_out, b_out)],
        out_specs=(tiles(3 * width), tiles(width), tiles(width)),
        compiler_params=pltpu.CompilerParams(vmem_limit_bytes=40 * MIB),
        name="attend",
    )(x, w_qkv, b_query, b_value, w_out, b_out)


def gelu_parts(values):
    cdf = 0.5 * (1.0 + lax.erf(values * 0.7071067811865476))
    pdf = 0.3989422804014327 * jnp.exp(-0.5 * values * values)
    return values * cdf, cdf + values * pdf


def contrast_rows(cls_low, count, flags, first, span_count):
    total, width = cls_low.shape
    docsets, slots = flags.shape
    block = min(total, 256)

    def layout(at):
        slot = at + lax.broadcasted_iota(i32, (block, 1), 0)
        device = slot // slots
        place = (slot - device * slots).astype(f32)
        member = lax.broadcasted_iota(i32, (block, docsets), 1) == device
        docs = jnp.sum(jnp.where(member, count, 0.0), axis=1, keepdims=True)
        single = dot(member.astype(bf16), flags.astype(bf16))
        doc = lax.broadcasted_iota(i32, (block, slots), 1).astype(f32)
        length = jnp.where(doc < docs, 2.0 - single, 0.0)
        earlier = lax.broadcasted_iota(i32, (slots, slots), 0) < lax.broadcasted_iota(
            i32, (slots, slots), 1
        )
        begins = dot(length.astype(bf16), earlier.astype(f32).astype(bf16))
        inside = (place >= begins) & (place < begins + length)
        double = inside & (length == 2.0)
        live = jnp.max(inside.astype(f32), axis=1, keepdims=True)
        pair = jnp.max(double.astype(f32), axis=1, keepdims=True)
        other = jnp.sum(jnp.where(double, 2.0 * begins + 1.0 - place, 0.0), axis=1, keepdims=True)
        mate = jnp.where(pair > 0.0, (device * slots).astype(f32) + other, slot.astype(f32))
        return slot.astype(f32), live, pair, mate

    eye = lax.broadcasted_iota(i32, (block, block), 0) == lax.broadcasted_iota(
        i32, (block, block), 1
    )
    live_row = jnp.concatenate(
        [col_sum(jnp.where(eye, layout(at)[1], 0.0)) for at in range(0, total, block)], axis=1
    )
    column = lax.broadcasted_iota(i32, (block, total), 1).astype(f32)
    pick_col = (
        lax.broadcasted_iota(i32, (span_count, total), 1)
        == first + lax.broadcasted_iota(i32, (span_count, total), 0)
    ).astype(f32).astype(bf16)
    rows_own = jnp.zeros((span_count, total), f32)
    upward = jnp.zeros((span_count, width), f32)
    own_loss = jnp.zeros((1, span_count), f32)
    loss = jnp.zeros((1, 1), f32)
    for at in range(0, total, block):
        slot, live, pair, mate = layout(at)
        cls_block = cls_low[at : at + block, :]
        sims = score_scale * dot_right_t(cls_block, cls_low)
        allowed = (live_row > 0.0) & (column != slot)
        masked = jnp.where(allowed, sims, far_low)
        top = jnp.max(masked, axis=1, keepdims=True)
        lse = top + jnp.log(jnp.sum(jnp.exp(masked - top), axis=1, keepdims=True))
        matches = column == mate
        positive = jnp.sum(jnp.where(matches, sims, 0.0), axis=1, keepdims=True)
        span_loss = jnp.where(pair > 0.0, lse - positive, 0.0)
        loss = loss + col_sum(span_loss)
        mine = at + lax.broadcasted_iota(i32, (block, span_count), 0) == (
            first + lax.broadcasted_iota(i32, (block, span_count), 1)
        )
        own_loss = own_loss + col_sum(jnp.where(mine, span_loss, 0.0))
        sim_grad = jnp.where(
            pair > 0.0, jnp.exp(masked - lse) - matches.astype(f32), 0.0
        ).astype(bf16)
        pick_row = (
            at + lax.broadcasted_iota(i32, (span_count, block), 1)
            == first + lax.broadcasted_iota(i32, (span_count, block), 0)
        ).astype(f32).astype(bf16)
        rows_own = rows_own + dot(pick_row, sim_grad)
        cols_own = dot_right_t(pick_col, sim_grad)
        upward = upward + dot(cols_own.astype(bf16), cls_block)
    upward = upward + dot(rows_own.astype(bf16), cls_low)
    return score_scale * upward, own_loss, loss


def middle_kernel(
    n_z,
    n_x,
    n_y,
    cent_hbm,
    w_in_hbm,
    w_ffo_hbm,
    out_grad_hbm,
    b_in_ref,
    b_ffo_ref,
    gain_one_ref,
    bias_one_ref,
    gain_two_ref,
    bias_two_ref,
    count_ref,
    flag_ref,
    block_hbm,
    mixed_hbm,
    act_hbm,
    ffn_grad_hbm,
    hidden_grad_hbm,
    pre_grad_hbm,
    vec_ref,
    own_loss_ref,
    loss_ref,
    cent_v,
    w_in,
    w_ffo,
    upper_v,
    block_v,
    mixed_v,
    act_v,
    slope_v,
    ffn_grad_v,
    two_v,
    first_v,
    cls_grad_v,
    b_in_v,
    cls_v,
    in_sem,
    out_sem,
    s_sem,
    r_sem,
):
    rows, width = cent_v.shape
    inner = w_in.shape[1]
    chunks = inner // width
    tiles = rows // TILE
    span_count = rows // SPAN_LEN
    wide, narrow = lax.axis_index("wide"), lax.axis_index("narrow")
    z, x = wide // n_x, lax.rem(wide, n_x)
    y, c = narrow // 2, lax.rem(narrow, 2)
    core = (wide, y * 2 + 1 - c)
    along_x = [(z * n_x + lax.rem(x + k, n_x), narrow) for k in range(1, n_x)]
    along_y = [(wide, lax.rem(y + k, n_y) * 2 + c) for k in range(1, n_y)]
    along_z = [(lax.rem(z + k, n_z) * n_x + x, narrow) for k in range(1, n_z)]
    partners = [core] + along_x + along_y + along_z

    barrier = pltpu.get_barrier_semaphore()
    for device in partners:
        pl.semaphore_signal(barrier, inc=1, device_id=device, device_id_type=MESH)

    loads = [
        pltpu.make_async_copy(src, dst, in_sem.at[k])
        for k, (src, dst) in enumerate(
            ((cent_hbm, cent_v), (w_in_hbm, w_in), (w_ffo_hbm, w_ffo), (out_grad_hbm, upper_v))
        )
    ]
    for copy in loads:
        copy.start()

    gain_one, bias_one = gain_one_ref[...].astype(f32), bias_one_ref[...].astype(f32)
    gain_two, bias_two = gain_two_ref[...].astype(f32), bias_two_ref[...].astype(f32)
    b_ffo = b_ffo_ref[...].astype(f32)
    b_in_v[...] = b_in_ref[...].astype(f32)

    def normed(cent):
        scale = lax.rsqrt(row_mean(cent * cent) + ln_eps)
        return cent * scale, scale

    def feed_forward(mixed, total, keep):
        mixed_low = mixed.astype(bf16)
        total[...] = mixed + b_ffo

        def step(j, carry):
            cols = pl.ds(pl.multiple_of(j * width, width), width)
            hidden = dot(mixed_low, w_in[:, cols]) + b_in_v[pl.ds(j, 1), :]
            act, slope = gelu_parts(hidden)
            act_low = act.astype(bf16)
            keep(cols, act_low, slope)
            total[...] += dot(act_low, w_ffo[cols, :])
            return carry

        lax.fori_loop(0, chunks, step, 0)
        pre_two = total[...]
        return pre_two - row_mean(pre_two)

    loads[0].wait()
    first_cent = jnp.concatenate(
        [cent_v[s * SPAN_LEN : s * SPAN_LEN + 1, :] for s in range(span_count)], axis=0
    )
    first_mixed = normed(first_cent)[0] * gain_one + bias_one
    loads[1].wait()
    loads[2].wait()
    first_two = feed_forward(first_mixed, first_v, lambda cols, act, slope: None)
    first_out = normed(first_two)[0] * gain_two + bias_two
    half = width // 2
    cls_v[z, x, y, c] = jnp.concatenate([first_out[:, :half], first_out[:, half:]], axis=0).astype(
        bf16
    )
    pl.semaphore_wait(barrier, len(partners))

    def gathers(stage):
        if stage == 0:
            ref, devices, base = cls_v.at[z, x, y, c], along_z, 0
        elif stage == 1:
            ref, devices, base = cls_v.at[:, x, y, c], along_x, n_z - 1
        elif stage == 2:
            ref, devices, base = cls_v.at[:, :, y, c], along_y, n_z + n_x - 2
        else:
            ref, devices, base = cls_v.at[:, :, :, c], [core], n_z + n_x + n_y - 3
        return [
            pltpu.make_async_remote_copy(
                ref, ref, s_sem.at[base + k], r_sem.at[base + k], device_id=d, device_id_type=MESH
            )
            for k, d in enumerate(devices)
        ]

    for copy in gathers(0):
        copy.start()
    loads[3].wait()

    def store(src, dst, at, k):
        return pltpu.make_async_copy(src.at[at, :], dst.at[at, :], out_sem.at[k])

    def tile_rows(tile):
        return pl.ds(pl.multiple_of(tile * TILE, TILE), TILE)

    def forward_stores(tile):
        at = tile_rows(tile)
        return [
            store(mixed_v, mixed_hbm, at, 6 * tile),
            store(block_v, block_hbm, at, 6 * tile + 1),
            store(act_v, act_hbm, at, 6 * tile + 2),
        ]

    def backward_stores(tile):
        at = tile_rows(tile)
        return [
            store(ffn_grad_v, ffn_grad_hbm, at, 6 * tile + 3),
            store(slope_v, hidden_grad_hbm, at, 6 * tile + 4),
            store(cent_v, pre_grad_hbm, at, 6 * tile + 5),
        ]

    def forward_tile(tile, carry):
        at = tile_rows(tile)
        mixed = normed(cent_v[at, :])[0] * gain_one + bias_one
        mixed_v[at, :] = mixed.astype(bf16)

        def keep(cols, act_low, slope):
            act_v[at, cols] = act_low
            slope_v[at, cols] = slope.astype(bf16)

        cent_two = feed_forward(mixed, two_v.at[at, :], keep)
        block_v[at, :] = (normed(cent_two)[0] * gain_two + bias_two).astype(bf16)
        two_v[at, :] = cent_two
        for copy in forward_stores(tile):
            copy.start()
        for stage in range(4):

            @pl.when(tile == min(stage, tiles - 1))
            def _():
                for copy in gathers(stage):
                    copy.wait()
                if stage < 3:
                    for copy in gathers(stage + 1):
                        copy.start()

        return carry

    lax.fori_loop(0, tiles, forward_tile, 0)

    low = cls_v[...].astype(f32).reshape(-1, 2 * span_count, half)
    cls_low = jnp.concatenate(
        [
            low[:, :span_count, :].reshape(-1, half),
            low[:, span_count:, :].reshape(-1, half),
        ],
        axis=1,
    ).astype(bf16)
    own = wide * (2 * n_y) + narrow
    cls_grad, own_loss, loss = contrast_rows(
        cls_low, count_ref[...].astype(f32), flag_ref[...].astype(f32), own * span_count, span_count
    )
    cls_grad_v[...] = cls_grad
    own_loss_ref[...] = own_loss
    loss_ref[...] = loss

    vec_ref[...] = jnp.zeros(vec_ref.shape, f32)

    def add_row(k, values):
        vec_ref[pl.ds(k, 1), :] += col_sum(values)

    def backward_tile(tile, carry):
        at = tile_rows(tile)
        upper = upper_v[at, :].astype(f32)
        place = lax.broadcasted_iota(i32, (TILE, 1), 0)
        for span in range(TILE // SPAN_LEN):
            upper = jnp.where(
                place == span * SPAN_LEN,
                cls_grad_v[pl.ds(tile * (TILE // SPAN_LEN) + span, 1), :],
                upper,
            )
        normed_two, scale_two = normed(two_v[at, :])
        add_row(6, upper * normed_two)
        add_row(7, upper)
        pre_two_grad = norm_back(upper, normed_two, scale_two, gain_two)
        ffn_grad = pre_two_grad.astype(bf16)
        ffn_grad_v[at, :] = ffn_grad
        add_row(5, ffn_grad.astype(f32))
        two_v[at, :] = pre_two_grad

        def step(j, inner_carry):
            cols = pl.ds(pl.multiple_of(j * width, width), width)
            back = dot_right_t(ffn_grad, w_ffo[cols, :]) * slope_v[at, cols].astype(f32)
            hidden_grad = back.astype(bf16)
            slope_v[at, cols] = hidden_grad
            add_row(8 + j, hidden_grad.astype(f32))
            two_v[at, :] += dot_right_t(hidden_grad, w_in[:, cols])
            return inner_carry

        lax.fori_loop(0, chunks, step, 0)
        mixed_grad = two_v[at, :]
        normed_one, scale_one = normed(cent_v[at, :])
        add_row(3, mixed_grad * normed_one)
        add_row(4, mixed_grad)
        pre_one_grad = norm_back(mixed_grad, normed_one, scale_one, gain_one)
        cent_v[at, :] = pre_one_grad
        add_row(2, pre_one_grad.astype(bf16).astype(f32))
        for copy in backward_stores(tile):
            copy.start()
        return carry

    lax.fori_loop(0, tiles, backward_tile, 0)

    for tile in range(tiles):
        for copy in forward_stores(tile) + backward_stores(tile):
            copy.wait()


def middle(cent, w_in, w_ffo, out_grad, b_in, b_ffo, gain_one, bias_one, gain_two, bias_two, doc_count, single_flag, sizes):
    rows, width = cent.shape
    inner = w_in.shape[1]
    span_count = rows // SPAN_LEN
    n_z, n_x, n_y = sizes
    moves = n_z + n_x + n_y - 2
    hbm = pl.BlockSpec(memory_space=pl.ANY)
    vmem = pl.BlockSpec(memory_space=pltpu.VMEM)
    shape = jax.ShapeDtypeStruct
    return pl.pallas_call(
        functools.partial(middle_kernel, n_z, n_x, n_y),
        out_shape=(
            shape((rows, width), bf16),
            shape((rows, width), bf16),
            shape((rows, inner), bf16),
            shape((rows, width), bf16),
            shape((rows, inner), bf16),
            shape((rows, width), f32),
            shape((16, width), f32),
            shape((1, span_count), f32),
            shape((1, 1), f32),
        ),
        in_specs=[hbm] * 4 + [vmem] * 8,
        out_specs=(hbm,) * 6 + (vmem,) * 3,
        scratch_shapes=[
            pltpu.VMEM((rows, width), f32),
            pltpu.VMEM((width, inner), bf16),
            pltpu.VMEM((inner, width), bf16),
            pltpu.VMEM((rows, width), bf16),
            pltpu.VMEM((rows, width), bf16),
            pltpu.VMEM((rows, width), bf16),
            pltpu.VMEM((rows, inner), bf16),
            pltpu.VMEM((rows, inner), bf16),
            pltpu.VMEM((rows, width), bf16),
            pltpu.VMEM((rows, width), f32),
            pltpu.VMEM((span_count, width), f32),
            pltpu.VMEM((span_count, width), f32),
            pltpu.VMEM((inner // width, width), f32),
            pltpu.VMEM((n_z, n_x, n_y, 2, 2 * span_count, width // 2), bf16),
            pltpu.SemaphoreType.DMA((4,)),
            pltpu.SemaphoreType.DMA((6 * (rows // TILE),)),
            pltpu.SemaphoreType.DMA((moves,)),
            pltpu.SemaphoreType.DMA((moves,)),
        ],
        compiler_params=pltpu.CompilerParams(
            collective_id=1, has_side_effects=True, vmem_limit_bytes=58 * MIB
        ),
        name="feed_forward_and_loss",
    )(
        cent, w_in, w_ffo, out_grad, b_in.reshape(-1, width), b_ffo, gain_one, bias_one, gain_two,
        bias_two, doc_count.reshape(1, -1), single_flag,
    )


def ar_kernel(n_x, n_z, ffo_ref, in_ref, out_ref, qkv_ref, vec_ref, o_ffo, o_rest, o_vec, part, sib, r1, r2, r3, vbuf, lsem, s_sem, r_sem, zs_sem, zr_sem, vs_sem, vr_sem):
    W = part.shape[2]
    H, Q = W // 2, W // 4
    E = Q // n_z
    wide, narrow = lax.axis_index("wide"), lax.axis_index("narrow")
    z, x = wide // n_x, wide % n_x
    y, c = narrow // 2, narrow % 2
    f32 = jnp.float32
    core = (wide, y * 2 + 1 - c)
    near_x = (z * n_x + 1 - x, narrow)
    near_y = (wide, (1 - y) * 2 + c)
    one = (jnp.where(c == 0, near_x[0], near_y[0]), jnp.where(c == 0, near_x[1], near_y[1]))
    two = (jnp.where(c == 0, near_y[0], near_x[0]), jnp.where(c == 0, near_y[1], near_x[1]))
    h1 = jnp.where(c == 0, x, y)
    h2 = jnp.where(c == 0, y, x)
    others = [lax.rem(z + k, n_z) for k in range(1, n_z)]
    zdev = [(o * n_x + x, narrow) for o in others]

    bar = pltpu.get_barrier_semaphore()
    for d in [core, near_x, near_y] + zdev:
        pl.semaphore_signal(bar, inc=1, device_id=d, device_id_type=MESH)

    loads = []
    for b in range(2 * TICKS):
        if b < 4:
            src = ffo_ref.at[pl.ds(b * W, W), :]
        elif b < 8:
            src = in_ref.at[:, pl.ds((b - 4) * W, W)]
        elif b < 9:
            src = out_ref
        else:
            src = qkv_ref.at[:, pl.ds((b - 9) * W, W)]
        cp = pltpu.make_async_copy(src, part.at[b], lsem.at[b])
        cp.start()
        loads.append(cp)
    pl.semaphore_wait(bar, 2 + n_z)

    def out_at(t, row, rows):
        if t < 2:
            return o_ffo.at[pl.ds(pl.multiple_of((2 * t + c) * W + row, 16), rows), :]
        return o_rest.at[pl.ds(pl.multiple_of(row, 16), rows), pl.ds(pl.multiple_of((2 * (t - 2) + c) * W, 128), W)]

    def rcopy(src, dst, k, t, dev):
        return pltpu.make_async_remote_copy(src, dst, s_sem.at[k, t], r_sem.at[k, t], device_id=dev, device_id_type=MESH)

    def add(t, row, rows, got):
        mine = 2 * t + c
        def body(i, _):
            at = pl.multiple_of(row + i * 48, 16)
            here = part[mine, pl.ds(at, 48), :].astype(f32) + got[pl.ds(pl.multiple_of(i * 48, 16), 48), :].astype(f32)
            part[mine, pl.ds(at, 48), :] = here.astype(jnp.bfloat16)
            return 0
        lax.fori_loop(0, rows // 48, body, 0)

    keep1 = h1 * H
    keep2 = keep1 + h2 * Q
    own = keep2 + z * E
    flight = {}
    def c0(t):
        return rcopy(part.at[2 * t + 1 - c], sib.at[t], 0, t, core)
    def c1(t):
        return rcopy(part.at[2 * t + c, pl.ds(pl.multiple_of((1 - h1) * H, 16), H), :], r1.at[t], 1, t, one)
    def c2(t):
        return rcopy(part.at[2 * t + c, pl.ds(pl.multiple_of(keep1 + (1 - h2) * Q, 16), Q), :], r2.at[t], 2, t, two)
    def c3(t):
        return [pltpu.make_async_remote_copy(
            part.at[2 * t + c, pl.ds(pl.multiple_of(keep2 + o * E, 16), E), :], r3.at[t, k],
            zs_sem.at[0, t, k], zr_sem.at[0, t, k], device_id=d, device_id_type=MESH)
            for k, (o, d) in enumerate(zip(others, zdev))]
    def c4(t):
        return [pltpu.make_async_remote_copy(
            out_at(t, own, E), out_at(t, own, E), zs_sem.at[1, t, k], zr_sem.at[1, t, k], device_id=d, device_id_type=MESH)
            for k, d in enumerate(zdev)]
    def c5(t):
        return rcopy(out_at(t, keep2, Q), out_at(t, keep2, Q), 3, t, two)
    def c6(t):
        return rcopy(out_at(t, keep1, H), out_at(t, keep1, H), 4, t, one)
    def c7(t):
        return rcopy(out_at(t, 0, W), out_at(t, 0, W), 5, t, core)

    def st0(t):
        loads[2 * t].wait(); loads[2 * t + 1].wait()
        c0(t).start()
    def st1(t):
        c0(t).wait()
        add(t, 0, W, sib.at[t])
        c1(t).start()
    def st2(t):
        c1(t).wait()
        add(t, keep1, H, r1.at[t])
        c2(t).start()
    def st3(t):
        c2(t).wait()
        add(t, keep2, Q, r2.at[t])
        for cp in c3(t): cp.start()
    def st4(t):
        for cp in c3(t): cp.wait()
        total = part[2 * t + c, pl.ds(pl.multiple_of(own, 16), E), :].astype(f32)
        for k in range(n_z - 1):
            total = total + r3[t, k].astype(f32)
        part[2 * t + c, pl.ds(pl.multiple_of(own, 16), E), :] = total.astype(jnp.bfloat16)
        cp = pltpu.make_async_copy(part.at[2 * t + c, pl.ds(pl.multiple_of(own, 16), E), :], out_at(t, own, E), lsem.at[2 * TICKS + t])
        cp.start(); cp.wait()
        for cp in c4(t): cp.start()
    def st5(t):
        for cp in c4(t): cp.wait()
        c5(t).start()
    def st6(t):
        c5(t).wait()
        c6(t).start()
    def st7(t):
        c6(t).wait()
        c7(t).start()
    def st8(t):
        c7(t).wait()

    def vcopy(k, dev):
        return pltpu.make_async_remote_copy(vbuf.at[2 * k], vbuf.at[2 * k + 1], vs_sem.at[k], vr_sem.at[k], device_id=dev, device_id_type=MESH)
    def vz():
        return [pltpu.make_async_remote_copy(vbuf.at[6], vbuf.at[7 + k], vs_sem.at[3 + k], vr_sem.at[3 + k], device_id=d, device_id_type=MESH) for k, d in enumerate(zdev)]
    def vstep(k):
        if k == 0:
            vbuf[0] = vec_ref[...]
            vcopy(0, core).start()
        elif k == 1:
            vcopy(0, core).wait()
            vbuf[2] = vbuf[0] + vbuf[1]
            vcopy(1, near_x).start()
        elif k == 2:
            vcopy(1, near_x).wait()
            vbuf[4] = vbuf[2] + vbuf[3]
            vcopy(2, near_y).start()
        elif k == 3:
            vcopy(2, near_y).wait()
            vbuf[6] = vbuf[4] + vbuf[5]
            for cp in vz(): cp.start()
        elif k == 4:
            for cp in vz(): cp.wait()
            total = vbuf[6]
            for k in range(n_z - 1):
                total = total + vbuf[7 + k]
            o_vec[...] = total

    stages = [st1, st2, st3, st4, st5, st6, st7, st8]
    for t in range(TICKS):
        st0(t)
    for step in range(TICKS + len(stages) - 1):
        if step >= 2: vstep(step - 2)
        for k, st in enumerate(stages):
            if 0 <= step - k < TICKS:
                st(step - k)

def all_reduce(ffo, inn, out, qkv, vec, n_x, n_z):
    W = ffo.shape[1]
    rest = jax.ShapeDtypeStruct((W, 8 * W), jnp.bfloat16)
    bf = jnp.bfloat16
    anyspec = pl.BlockSpec(memory_space=pl.ANY)
    vm = pl.BlockSpec(memory_space=pltpu.VMEM)
    T = TICKS
    return pl.pallas_call(
        functools.partial(ar_kernel, n_x, n_z),
        out_shape=(jax.ShapeDtypeStruct(ffo.shape, bf), jax.ShapeDtypeStruct(rest.shape, bf), jax.ShapeDtypeStruct(vec.shape, jnp.float32)),
        in_specs=[anyspec, anyspec, anyspec, anyspec, vm], out_specs=(anyspec, anyspec, vm),
        scratch_shapes=[
            pltpu.VMEM((2 * T, W, W), bf), pltpu.VMEM((T, W, W), bf), pltpu.VMEM((T, W // 2, W), bf), pltpu.VMEM((T, W // 4, W), bf),
            pltpu.VMEM((T, n_z - 1, W // 4 // n_z, W), bf), pltpu.VMEM((6 + n_z,) + vec.shape, jnp.float32),
            pltpu.SemaphoreType.DMA((3 * T,)), pltpu.SemaphoreType.DMA((6, T)), pltpu.SemaphoreType.DMA((6, T)),
            pltpu.SemaphoreType.DMA((2, T, n_z - 1)), pltpu.SemaphoreType.DMA((2, T, n_z - 1)),
            pltpu.SemaphoreType.DMA((2 + n_z,)), pltpu.SemaphoreType.DMA((2 + n_z,)),
        ],
        compiler_params=pltpu.CompilerParams(collective_id=0, has_side_effects=True, vmem_limit_bytes=56 * 2**20),
        name="grad_all_reduce",
    )(ffo, inn, out, qkv, vec)


def mesh_sizes():
    n_wide, n_narrow = lax.axis_size("wide"), lax.axis_size("narrow")
    n_y = n_narrow // 2
    n_x = n_y if n_wide % n_y == 0 else 1
    return n_wide // n_x, n_x, n_y


def per_device(
    hidden_in,
    out_grad,
    w_qkv,
    b_query,
    b_value,
    w_out,
    b_out,
    ln1_gain,
    ln1_bias,
    w_in,
    b_in,
    w_ff_out,
    b_ff_out,
    ln2_gain,
    ln2_bias,
    doc_count,
    single_flag,
):
    rows, width = hidden_in.shape
    span_count = rows // SPAN_LEN
    sizes = mesh_sizes()

    def line(vector):
        return vector.reshape(1, -1)

    qkv, context, cent = attend(
        hidden_in, w_qkv, line(b_query), line(b_value), w_out, line(b_out)
    )
    block_out, mixed_low, act, ffn_grad, hidden_grad, pre_one_grad, vectors, span_loss, loss = middle(
        cent, w_in, w_ff_out, out_grad, b_in, line(b_ff_out), line(ln1_gain), line(ln1_bias),
        line(ln2_gain), line(ln2_bias), doc_count, single_flag, sizes,
    )
    attn_grad = pre_one_grad.astype(bf16)
    heads = width // HEAD_DIM
    queries, keys_low, values_low = (
        p.reshape(span_count, SPAN_LEN, heads, HEAD_DIM) for p in jnp.split(qkv, 3, axis=1)
    )
    context_grad = dot_right_t(attn_grad, w_out).astype(bf16).reshape(
        span_count, SPAN_LEN, heads, HEAD_DIM
    )
    scores = jnp.einsum("slhe,smhe->shlm", queries, keys_low, preferred_element_type=f32) * head_scale
    probs = jax.nn.softmax(scores, axis=3)
    value_grad = jnp.einsum("shlm,slhe->smhe", probs.astype(bf16), context_grad, preferred_element_type=f32).astype(bf16)
    prob_grad = jnp.einsum("slhe,smhe->shlm", context_grad, values_low, preferred_element_type=f32)
    score_grad = (probs * (prob_grad - jnp.sum(probs * prob_grad, axis=3, keepdims=True))).astype(bf16)
    query_grad = (jnp.einsum("shlm,smhe->slhe", score_grad, keys_low, preferred_element_type=f32) * head_scale).astype(bf16)
    key_grad = (jnp.einsum("shlm,slhe->smhe", score_grad, queries, preferred_element_type=f32) * head_scale).astype(bf16)
    packed_grad = jnp.concatenate([g.reshape(rows, width) for g in (query_grad, key_grad, value_grad)], axis=1)
    sums = jnp.sum(packed_grad.astype(f32), axis=0)
    vectors = vectors.at[0].set(sums[:width]).at[1].set(sums[2 * width :])
    grad_in = pre_one_grad + dot_right_t(packed_grad, w_qkv)
    weights = [
        dot_left_t(act, ffn_grad).astype(bf16),
        dot_left_t(mixed_low, hidden_grad).astype(bf16),
        dot_left_t(context, attn_grad).astype(bf16),
        dot_left_t(hidden_in, packed_grad).astype(bf16),
    ]
    if sizes[1] == 2 and sizes[2] == 2 and width % (64 * sizes[0]) == 0:
        g_ffo, rest, vectors = all_reduce(*weights, vectors, sizes[1], sizes[0])
    else:
        both = ("wide", "narrow")
        g_ffo, rest = lax.psum((weights[0], jnp.concatenate(weights[1:], axis=1)), both)
        vectors = lax.psum(vectors, both)
    inner = w_in.shape[1]
    return (
        block_out,
        loss.reshape(()),
        span_loss.reshape(-1),
        grad_in,
        rest[:, inner + width :].astype(f32),
        vectors[0],
        vectors[1],
        rest[:, inner : inner + width].astype(f32),
        vectors[2],
        vectors[3],
        vectors[4],
        rest[:, :inner].astype(f32),
        vectors[8 : 8 + inner // width].reshape(-1),
        g_ffo.astype(f32),
        vectors[5],
        vectors[6],
        vectors[7],
    )


def solution(mesh):
    placed = (
        P(("wide", "narrow"), None),
        P(("wide", "narrow"), None),
        P(),
        P(),
        P(),
        P(),
        P(),
        P(),
        P(),
        P(),
        P(),
        P(),
        P(),
        P(),
        P(),
        P(),
        P(),
    )
    return jax.shard_map(
        per_device,
        mesh=mesh,
        in_specs=placed,
        out_specs=(
            P(("wide", "narrow"), None),
            P(),
            P(("wide", "narrow")),
            P(("wide", "narrow"), None),
            P(),
            P(),
            P(),
            P(),
            P(),
            P(),
            P(),
            P(),
            P(),
            P(),
            P(),
            P(),
            P(),
        ),
        check_vma=False,
    )
```

```python
import functools

import jax
import jax.numpy as jnp
from jax import lax
from jax.experimental import pallas as pl
from jax.experimental.pallas import tpu as pltpu
from jax.sharding import PartitionSpec as P

HEAD_DIM = 64
SPAN_LEN = 128
TILE = 256

ln_eps = 1e-06
score_scale = 0.2
far_low = -1000000000.0
head_scale = HEAD_DIM ** (-0.5)
MESH = pl.DeviceIdType.MESH
TICKS = 6
f32, bf16, i32 = jnp.float32, jnp.bfloat16, jnp.int32
MIB = 2**20


def dot(left, right):
    return jnp.dot(left, right, preferred_element_type=f32)


def dot_left_t(left, right):
    return lax.dot_general(left, right, (((0,), (0,)), ((), ())), preferred_element_type=f32)


def dot_right_t(left, right):
    return lax.dot_general(left, right, (((1,), (1,)), ((), ())), preferred_element_type=f32)


def row_mean(values):
    return jnp.mean(values, axis=1, keepdims=True)


def col_sum(values):
    return jnp.sum(values, axis=0, keepdims=True)


def norm_back(upstream, normed, scale, gain):
    scaled = upstream * gain
    return scale * (scaled - row_mean(scaled) - normed * row_mean(scaled * normed))


def head_halves():
    first = lax.broadcasted_iota(i32, (1, 2 * HEAD_DIM), 1) < HEAD_DIM
    return first, first.astype(bf16), jnp.logical_not(first).astype(bf16)


def pair_probs(stacked_queries, keys_low):
    scores = dot_right_t(stacked_queries, keys_low)
    shifted = jnp.exp((scores - jnp.max(scores, axis=1, keepdims=True)) * head_scale)
    return shifted * (1.0 / jnp.sum(shifted, axis=1, keepdims=True))


def attend_kernel(
    x_ref, w_qkv_ref, b_query_ref, b_value_ref, w_out_ref, b_out_ref, qkv_ref, context_ref, cent_ref
):
    rows, width = x_ref.shape
    inputs = x_ref[...]
    for third in range(3):
        cols = pl.ds(third * width, width)
        packed = dot(inputs, w_qkv_ref[:, cols])
        if third == 0:
            packed = packed + b_query_ref[...].astype(f32)
        if third == 2:
            packed = packed + b_value_ref[...].astype(f32)
        qkv_ref[:, cols] = packed.astype(bf16)
    first, low_one, low_two = head_halves()
    lanes = 2 * HEAD_DIM
    for span in range(rows // SPAN_LEN):
        at = pl.ds(span * SPAN_LEN, SPAN_LEN)
        for pair in range(width // lanes):
            queries = qkv_ref[at, pl.ds(pair * lanes, lanes)]
            keys_low = qkv_ref[at, pl.ds(width + pair * lanes, lanes)]
            values_low = qkv_ref[at, pl.ds(2 * width + pair * lanes, lanes)]
            stacked = jnp.concatenate([queries * low_one, queries * low_two], axis=0)
            mixed_values = dot(pair_probs(stacked, keys_low).astype(bf16), values_low)
            context_ref[at, pl.ds(pair * lanes, lanes)] = jnp.where(
                first, mixed_values[:SPAN_LEN], mixed_values[SPAN_LEN:]
            ).astype(bf16)
    attended = dot(context_ref[...], w_out_ref[...]) + b_out_ref[...].astype(f32)
    pre_one = inputs.astype(f32) + attended
    cent_ref[...] = pre_one - row_mean(pre_one)


def attend(x, w_qkv, b_query, b_value, w_out, b_out):
    rows, width = x.shape

    def whole(a):
        return pl.BlockSpec(a.shape, lambda i: (0, 0))

    def tiles(cols):
        return pl.BlockSpec((TILE, cols), lambda i: (i, 0))

    return pl.pallas_call(
        attend_kernel,
        grid=(rows // TILE,),
        out_shape=(
            jax.ShapeDtypeStruct((rows, 3 * width), bf16),
            jax.ShapeDtypeStruct((rows, width), bf16),
            jax.ShapeDtypeStruct((rows, width), f32),
        ),
        in_specs=[tiles(width)] + [whole(a) for a in (w_qkv, b_query, b_value, w_out, b_out)],
        out_specs=(tiles(3 * width), tiles(width), tiles(width)),
        compiler_params=pltpu.CompilerParams(vmem_limit_bytes=40 * MIB),
        name="attend",
    )(x, w_qkv, b_query, b_value, w_out, b_out)


def gelu_parts(values):
    cdf = 0.5 * (1.0 + lax.erf(values * 0.7071067811865476))
    pdf = 0.3989422804014327 * jnp.exp(-0.5 * values * values)
    return values * cdf, cdf + values * pdf


def contrast_rows(cls_low, count, flags, first, span_count):
    total, width = cls_low.shape
    docsets, slots = flags.shape
    block = min(total, 256)

    def layout(at):
        slot = at + lax.broadcasted_iota(i32, (block, 1), 0)
        device = slot // slots
        place = (slot - device * slots).astype(f32)
        member = lax.broadcasted_iota(i32, (block, docsets), 1) == device
        docs = jnp.sum(jnp.where(member, count, 0.0), axis=1, keepdims=True)
        single = dot(member.astype(bf16), flags.astype(bf16))
        doc = lax.broadcasted_iota(i32, (block, slots), 1).astype(f32)
        length = jnp.where(doc < docs, 2.0 - single, 0.0)
        earlier = lax.broadcasted_iota(i32, (slots, slots), 0) < lax.broadcasted_iota(
            i32, (slots, slots), 1
        )
        begins = dot(length.astype(bf16), earlier.astype(f32).astype(bf16))
        inside = (place >= begins) & (place < begins + length)
        double = inside & (length == 2.0)
        live = jnp.max(inside.astype(f32), axis=1, keepdims=True)
        pair = jnp.max(double.astype(f32), axis=1, keepdims=True)
        other = jnp.sum(jnp.where(double, 2.0 * begins + 1.0 - place, 0.0), axis=1, keepdims=True)
        mate = jnp.where(pair > 0.0, (device * slots).astype(f32) + other, slot.astype(f32))
        return slot.astype(f32), live, pair, mate

    eye = lax.broadcasted_iota(i32, (block, block), 0) == lax.broadcasted_iota(
        i32, (block, block), 1
    )
    live_row = jnp.concatenate(
        [col_sum(jnp.where(eye, layout(at)[1], 0.0)) for at in range(0, total, block)], axis=1
    )
    column = lax.broadcasted_iota(i32, (block, total), 1).astype(f32)
    pick_col = (
        lax.broadcasted_iota(i32, (span_count, total), 1)
        == first + lax.broadcasted_iota(i32, (span_count, total), 0)
    ).astype(f32).astype(bf16)
    rows_own = jnp.zeros((span_count, total), f32)
    upward = jnp.zeros((span_count, width), f32)
    own_loss = jnp.zeros((1, span_count), f32)
    loss = jnp.zeros((1, 1), f32)
    for at in range(0, total, block):
        slot, live, pair, mate = layout(at)
        cls_block = cls_low[at : at + block, :]
        sims = score_scale * dot_right_t(cls_block, cls_low)
        allowed = (live_row > 0.0) & (column != slot)
        masked = jnp.where(allowed, sims, far_low)
        top = jnp.max(masked, axis=1, keepdims=True)
        lse = top + jnp.log(jnp.sum(jnp.exp(masked - top), axis=1, keepdims=True))
        matches = column == mate
        positive = jnp.sum(jnp.where(matches, sims, 0.0), axis=1, keepdims=True)
        span_loss = jnp.where(pair > 0.0, lse - positive, 0.0)
        loss = loss + col_sum(span_loss)
        mine = at + lax.broadcasted_iota(i32, (block, span_count), 0) == (
            first + lax.broadcasted_iota(i32, (block, span_count), 1)
        )
        own_loss = own_loss + col_sum(jnp.where(mine, span_loss, 0.0))
        sim_grad = jnp.where(
            pair > 0.0, jnp.exp(masked - lse) - matches.astype(f32), 0.0
        ).astype(bf16)
        pick_row = (
            at + lax.broadcasted_iota(i32, (span_count, block), 1)
            == first + lax.broadcasted_iota(i32, (span_count, block), 0)
        ).astype(f32).astype(bf16)
        rows_own = rows_own + dot(pick_row, sim_grad)
        cols_own = dot_right_t(pick_col, sim_grad)
        upward = upward + dot(cols_own.astype(bf16), cls_block)
    upward = upward + dot(rows_own.astype(bf16), cls_low)
    return score_scale * upward, own_loss, loss


def middle_kernel(
    n_z,
    n_x,
    n_y,
    cent_hbm,
    w_in_hbm,
    w_ffo_hbm,
    out_grad_hbm,
    b_in_ref,
    b_ffo_ref,
    gain_one_ref,
    bias_one_ref,
    gain_two_ref,
    bias_two_ref,
    count_ref,
    flag_ref,
    block_hbm,
    mixed_hbm,
    act_hbm,
    ffn_grad_hbm,
    hidden_grad_hbm,
    pre_grad_hbm,
    vec_ref,
    own_loss_ref,
    loss_ref,
    cent_v,
    w_in,
    w_ffo,
    upper_v,
    block_v,
    mixed_v,
    act_v,
    slope_v,
    ffn_grad_v,
    two_v,
    first_v,
    cls_grad_v,
    b_in_v,
    cls_v,
    in_sem,
    out_sem,
    s_sem,
    r_sem,
):
    rows, width = cent_v.shape
    inner = w_in.shape[1]
    chunks = inner // width
    tiles = rows // TILE
    span_count = rows // SPAN_LEN
    wide, narrow = lax.axis_index("wide"), lax.axis_index("narrow")
    z, x = wide // n_x, lax.rem(wide, n_x)
    y, c = narrow // 2, lax.rem(narrow, 2)
    core = (wide, y * 2 + 1 - c)
    along_x = [(z * n_x + lax.rem(x + k, n_x), narrow) for k in range(1, n_x)]
    along_y = [(wide, lax.rem(y + k, n_y) * 2 + c) for k in range(1, n_y)]
    along_z = [(lax.rem(z + k, n_z) * n_x + x, narrow) for k in range(1, n_z)]
    partners = [core] + along_x + along_y + along_z

    barrier = pltpu.get_barrier_semaphore()
    for device in partners:
        pl.semaphore_signal(barrier, inc=1, device_id=device, device_id_type=MESH)

    loads = [
        pltpu.make_async_copy(src, dst, in_sem.at[k])
        for k, (src, dst) in enumerate(
            ((cent_hbm, cent_v), (w_in_hbm, w_in), (w_ffo_hbm, w_ffo), (out_grad_hbm, upper_v))
        )
    ]
    for copy in loads:
        copy.start()

    gain_one, bias_one = gain_one_ref[...].astype(f32), bias_one_ref[...].astype(f32)
    gain_two, bias_two = gain_two_ref[...].astype(f32), bias_two_ref[...].astype(f32)
    b_ffo = b_ffo_ref[...].astype(f32)
    b_in_v[...] = b_in_ref[...].astype(f32)

    def normed(cent):
        scale = lax.rsqrt(row_mean(cent * cent) + ln_eps)
        return cent * scale, scale

    def feed_forward(mixed, total, keep):
        mixed_low = mixed.astype(bf16)
        total[...] = mixed + b_ffo

        def step(j, carry):
            cols = pl.ds(pl.multiple_of(j * width, width), width)
            hidden = dot(mixed_low, w_in[:, cols]) + b_in_v[pl.ds(j, 1), :]
            act, slope = gelu_parts(hidden)
            act_low = act.astype(bf16)
            keep(cols, act_low, slope)
            total[...] += dot(act_low, w_ffo[cols, :])
            return carry

        lax.fori_loop(0, chunks, step, 0)
        pre_two = total[...]
        return pre_two - row_mean(pre_two)

    loads[0].wait()
    first_cent = jnp.concatenate(
        [cent_v[s * SPAN_LEN : s * SPAN_LEN + 1, :] for s in range(span_count)], axis=0
    )
    first_mixed = normed(first_cent)[0] * gain_one + bias_one
    loads[1].wait()
    loads[2].wait()
    first_two = feed_forward(first_mixed, first_v, lambda cols, act, slope: None)
    first_out = normed(first_two)[0] * gain_two + bias_two
    half = width // 2
    cls_v[z, x, y, c] = jnp.concatenate([first_out[:, :half], first_out[:, half:]], axis=0).astype(
        bf16
    )
    pl.semaphore_wait(barrier, len(partners))

    def gathers(stage):
        if stage == 0:
            ref, devices, base = cls_v.at[z, x, y, c], along_z, 0
        elif stage == 1:
            ref, devices, base = cls_v.at[:, x, y, c], along_x, n_z - 1
        elif stage == 2:
            ref, devices, base = cls_v.at[:, :, y, c], along_y, n_z + n_x - 2
        else:
            ref, devices, base = cls_v.at[:, :, :, c], [core], n_z + n_x + n_y - 3
        return [
            pltpu.make_async_remote_copy(
                ref, ref, s_sem.at[base + k], r_sem.at[base + k], device_id=d, device_id_type=MESH
            )
            for k, d in enumerate(devices)
        ]

    for copy in gathers(0):
        copy.start()
    loads[3].wait()

    def store(src, dst, at, k):
        return pltpu.make_async_copy(src.at[at, :], dst.at[at, :], out_sem.at[k])

    def tile_rows(tile):
        return pl.ds(pl.multiple_of(tile * TILE, TILE), TILE)

    def forward_stores(tile):
        at = tile_rows(tile)
        return [
            store(mixed_v, mixed_hbm, at, 6 * tile),
            store(block_v, block_hbm, at, 6 * tile + 1),
            store(act_v, act_hbm, at, 6 * tile + 2),
        ]

    def backward_stores(tile):
        at = tile_rows(tile)
        return [
            store(ffn_grad_v, ffn_grad_hbm, at, 6 * tile + 3),
            store(slope_v, hidden_grad_hbm, at, 6 * tile + 4),
            store(cent_v, pre_grad_hbm, at, 6 * tile + 5),
        ]

    def forward_tile(tile, carry):
        at = tile_rows(tile)
        mixed = normed(cent_v[at, :])[0] * gain_one + bias_one
        mixed_v[at, :] = mixed.astype(bf16)

        def keep(cols, act_low, slope):
            act_v[at, cols] = act_low
            slope_v[at, cols] = slope.astype(bf16)

        cent_two = feed_forward(mixed, two_v.at[at, :], keep)
        block_v[at, :] = (normed(cent_two)[0] * gain_two + bias_two).astype(bf16)
        two_v[at, :] = cent_two
        for copy in forward_stores(tile):
            copy.start()
        for stage in range(4):

            @pl.when(tile == min(stage, tiles - 1))
            def _():
                for copy in gathers(stage):
                    copy.wait()
                if stage < 3:
                    for copy in gathers(stage + 1):
                        copy.start()

        return carry

    lax.fori_loop(0, tiles, forward_tile, 0)

    low = cls_v[...].astype(f32).reshape(-1, 2 * span_count, half)
    cls_low = jnp.concatenate(
        [
            low[:, :span_count, :].reshape(-1, half),
            low[:, span_count:, :].reshape(-1, half),
        ],
        axis=1,
    ).astype(bf16)
    own = wide * (2 * n_y) + narrow
    cls_grad, own_loss, loss = contrast_rows(
        cls_low, count_ref[...].astype(f32), flag_ref[...].astype(f32), own * span_count, span_count
    )
    cls_grad_v[...] = cls_grad
    own_loss_ref[...] = own_loss
    loss_ref[...] = loss

    vec_ref[...] = jnp.zeros(vec_ref.shape, f32)

    def add_row(k, values):
        vec_ref[pl.ds(k, 1), :] += col_sum(values)

    def backward_tile(tile, carry):
        at = tile_rows(tile)
        upper = upper_v[at, :].astype(f32)
        place = lax.broadcasted_iota(i32, (TILE, 1), 0)
        for span in range(TILE // SPAN_LEN):
            upper = jnp.where(
                place == span * SPAN_LEN,
                cls_grad_v[pl.ds(tile * (TILE // SPAN_LEN) + span, 1), :],
                upper,
            )
        normed_two, scale_two = normed(two_v[at, :])
        add_row(6, upper * normed_two)
        add_row(7, upper)
        pre_two_grad = norm_back(upper, normed_two, scale_two, gain_two)
        ffn_grad = pre_two_grad.astype(bf16)
        ffn_grad_v[at, :] = ffn_grad
        add_row(5, ffn_grad.astype(f32))
        two_v[at, :] = pre_two_grad

        def step(j, inner_carry):
            cols = pl.ds(pl.multiple_of(j * width, width), width)
            back = dot_right_t(ffn_grad, w_ffo[cols, :]) * slope_v[at, cols].astype(f32)
            hidden_grad = back.astype(bf16)
            slope_v[at, cols] = hidden_grad
            add_row(8 + j, hidden_grad.astype(f32))
            two_v[at, :] += dot_right_t(hidden_grad, w_in[:, cols])
            return inner_carry

        lax.fori_loop(0, chunks, step, 0)
        mixed_grad = two_v[at, :]
        normed_one, scale_one = normed(cent_v[at, :])
        add_row(3, mixed_grad * normed_one)
        add_row(4, mixed_grad)
        pre_one_grad = norm_back(mixed_grad, normed_one, scale_one, gain_one)
        cent_v[at, :] = pre_one_grad
        add_row(2, pre_one_grad.astype(bf16).astype(f32))
        for copy in backward_stores(tile):
            copy.start()
        return carry

    lax.fori_loop(0, tiles, backward_tile, 0)

    for tile in range(tiles):
        for copy in forward_stores(tile) + backward_stores(tile):
            copy.wait()


def middle(cent, w_in, w_ffo, out_grad, b_in, b_ffo, gain_one, bias_one, gain_two, bias_two, doc_count, single_flag, sizes):
    rows, width = cent.shape
    inner = w_in.shape[1]
    span_count = rows // SPAN_LEN
    n_z, n_x, n_y = sizes
    moves = n_z + n_x + n_y - 2
    hbm = pl.BlockSpec(memory_space=pl.ANY)
    vmem = pl.BlockSpec(memory_space=pltpu.VMEM)
    shape = jax.ShapeDtypeStruct
    return pl.pallas_call(
        functools.partial(middle_kernel, n_z, n_x, n_y),
        out_shape=(
            shape((rows, width), bf16),
            shape((rows, width), bf16),
            shape((rows, inner), bf16),
            shape((rows, width), bf16),
            shape((rows, inner), bf16),
            shape((rows, width), f32),
            shape((16, width), f32),
            shape((1, span_count), f32),
            shape((1, 1), f32),
        ),
        in_specs=[hbm] * 4 + [vmem] * 8,
        out_specs=(hbm,) * 6 + (vmem,) * 3,
        scratch_shapes=[
            pltpu.VMEM((rows, width), f32),
            pltpu.VMEM((width, inner), bf16),
            pltpu.VMEM((inner, width), bf16),
            pltpu.VMEM((rows, width), bf16),
            pltpu.VMEM((rows, width), bf16),
            pltpu.VMEM((rows, width), bf16),
            pltpu.VMEM((rows, inner), bf16),
            pltpu.VMEM((rows, inner), bf16),
            pltpu.VMEM((rows, width), bf16),
            pltpu.VMEM((rows, width), f32),
            pltpu.VMEM((span_count, width), f32),
            pltpu.VMEM((span_count, width), f32),
            pltpu.VMEM((inner // width, width), f32),
            pltpu.VMEM((n_z, n_x, n_y, 2, 2 * span_count, width // 2), bf16),
            pltpu.SemaphoreType.DMA((4,)),
            pltpu.SemaphoreType.DMA((6 * (rows // TILE),)),
            pltpu.SemaphoreType.DMA((moves,)),
            pltpu.SemaphoreType.DMA((moves,)),
        ],
        compiler_params=pltpu.CompilerParams(
            collective_id=1, has_side_effects=True, vmem_limit_bytes=58 * MIB
        ),
        name="feed_forward_and_loss",
    )(
        cent, w_in, w_ffo, out_grad, b_in.reshape(-1, width), b_ffo, gain_one, bias_one, gain_two,
        bias_two, doc_count.reshape(1, -1), single_flag,
    )


def attend_back_kernel(
    n_z,
    n_x,
    comm,
    order,
    act_hbm,
    hidden_grad_hbm,
    ffn_grad_hbm,
    mixed_hbm,
    pre_grad_hbm,
    context_hbm,
    qkv_hbm,
    x_hbm,
    w_out_hbm,
    w_qkv_hbm,
    vec_ref,
    o_ffo,
    o_rest,
    grad_in_hbm,
    o_vec,
    stream,
    ffn_grad_v,
    mixed_v,
    pre_v,
    context_v,
    qkv_v,
    x_v,
    w_out,
    w_qkv,
    attn_v,
    context_grad_v,
    part,
    sib,
    r1,
    r2,
    r3,
    vbuf,
    in_sem,
    out_sem,
    s_sem,
    r_sem,
    zs_sem,
    zr_sem,
    vs_sem,
    vr_sem,
):
    rows, width = x_v.shape
    half, quarter = width // 2, width // 4
    eighth = quarter // n_z
    tiles = rows // TILE
    ahead = stream.shape[0]
    wide, narrow = lax.axis_index("wide"), lax.axis_index("narrow")
    z, x = wide // n_x, lax.rem(wide, n_x)
    y, c = narrow // 2, lax.rem(narrow, 2)
    core = (wide, y * 2 + 1 - c)
    near_x = (z * n_x + 1 - x, narrow)
    near_y = (wide, (1 - y) * 2 + c)
    one = tuple(jnp.where(c == 0, a, b) for a, b in zip(near_x, near_y))
    two = tuple(jnp.where(c == 0, b, a) for a, b in zip(near_x, near_y))
    h1 = jnp.where(c == 0, x, y)
    h2 = jnp.where(c == 0, y, x)
    others = [lax.rem(z + k, n_z) for k in range(1, n_z)]
    along_z = [(o * n_x + x, narrow) for o in others]

    if comm:
        barrier = pltpu.get_barrier_semaphore()
        for device in [core, near_x, near_y] + along_z:
            pl.semaphore_signal(barrier, inc=1, device_id=device, device_id_type=MESH)

    def stream_load(j):
        src = act_hbm if j < 4 else hidden_grad_hbm
        return pltpu.make_async_copy(
            src.at[:, pl.ds((j % 4) * width, width)], stream.at[j % ahead], in_sem.at[j]
        )

    resident = [
        pltpu.make_async_copy(src, dst, in_sem.at[8 + k])
        for k, (src, dst) in enumerate(
            (
                (ffn_grad_hbm, ffn_grad_v),
                (mixed_hbm, mixed_v),
                (pre_grad_hbm, pre_v),
                (w_out_hbm, w_out),
                (qkv_hbm, qkv_v),
                (w_qkv_hbm, w_qkv),
                (context_hbm, context_v),
                (x_hbm, x_v),
            )
        )
    ]
    stream_load(0).start()
    resident[0].start()
    for j in range(1, ahead):
        stream_load(j).start()
    for copy in resident[1:]:
        copy.start()
    vbuf[0] = vec_ref[...]
    waited = set()

    def need(*which):
        for k in which:
            if k not in waited:
                waited.add(k)
                resident[k].wait()

    first, low_one, low_two = head_halves()
    lanes = 2 * HEAD_DIM

    def weight_block(b):
        if b < 8:
            stream_load(b).wait()
        if b < 4:
            need(0)
            left, right = stream.at[b % ahead], ffn_grad_v
        elif b < 8:
            need(1)
            left, right = mixed_v, stream.at[b % ahead]
        elif b < 9:
            need(6)
            left, right = context_v, attn_v
        else:
            need(7)
            left, right = x_v, qkv_v.at[:, pl.ds((b - 9) * width, width)]

        def step(i, carry):
            at = pl.ds(pl.multiple_of(i * TILE, TILE), TILE)
            part[b, at, :] = dot_left_t(left[:, at], right[...]).astype(bf16)
            return carry

        lax.fori_loop(0, width // TILE, step, 0)
        if b + ahead < 8:
            stream_load(b + ahead).start()

    def grad_in_store(tile):
        at = pl.ds(tile * TILE, TILE)
        return pltpu.make_async_copy(pre_v.at[at, :], grad_in_hbm.at[at, :], out_sem.at[tile])

    def attend_tile(tile):
        need(2, 3, 4, 5)
        at = pl.ds(tile * TILE, TILE)
        attn_grad = pre_v[at, :].astype(bf16)
        attn_v[at, :] = attn_grad
        context_grad_v[...] = dot_right_t(attn_grad, w_out[...]).astype(bf16)

        def pair_step(pair):
            q_at, k_at, v_at = (pl.ds(third * width + pair * lanes, lanes) for third in range(3))
            for span in range(TILE // SPAN_LEN):
                sp = pl.ds(tile * TILE + span * SPAN_LEN, SPAN_LEN)
                queries, keys_low, values_low = qkv_v[sp, q_at], qkv_v[sp, k_at], qkv_v[sp, v_at]
                upper = context_grad_v[pl.ds(span * SPAN_LEN, SPAN_LEN), q_at]
                stacked = jnp.concatenate([queries * low_one, queries * low_two], axis=0)
                stacked_up = jnp.concatenate([upper * low_one, upper * low_two], axis=0)
                scores = dot_right_t(keys_low, stacked)
                shifted = jnp.exp((scores - jnp.max(scores, axis=0, keepdims=True)) * head_scale)
                probs = shifted * (1.0 / col_sum(shifted))
                value_grad = dot(probs.astype(bf16), stacked_up)
                prob_grad = dot_right_t(values_low, stacked_up)
                score_grad = (probs * (prob_grad - col_sum(probs * prob_grad))).astype(bf16)
                query_grad = dot_left_t(score_grad, keys_low) * head_scale
                key_grad = dot(score_grad, stacked) * head_scale
                qkv_v[sp, q_at] = jnp.where(
                    first, query_grad[:SPAN_LEN], query_grad[SPAN_LEN:]
                ).astype(bf16)
                qkv_v[sp, k_at] = key_grad.astype(bf16)
                qkv_v[sp, v_at] = value_grad.astype(bf16)

        for pair in range(width // lanes):
            pair_step(pair)
        vbuf[0, 0:1, :] += col_sum(qkv_v[at, 0:width].astype(f32))
        vbuf[0, 1:2, :] += col_sum(qkv_v[at, 2 * width : 3 * width].astype(f32))
        pre_v[at, :] += dot_right_t(qkv_v[at, :], w_qkv[...])
        grad_in_store(tile).start()

    def out_at(t, row, count):
        if t < 2:
            at = pl.multiple_of((2 * t + c) * width + row, 16)
            return o_ffo.at[pl.ds(at, count), :]
        cols = pl.multiple_of((2 * (t - 2) + c) * width, 128)
        return o_rest.at[pl.ds(pl.multiple_of(row, 16), count), pl.ds(cols, width)]

    def part_at(t, row, count):
        return part.at[2 * t + c, pl.ds(pl.multiple_of(row, 16), count), :]

    keep1 = h1 * half
    keep2 = keep1 + h2 * quarter
    own = keep2 + z * eighth

    def send(src, dst, stage, t, device):
        return pltpu.make_async_remote_copy(
            src, dst, s_sem.at[stage, t], r_sem.at[stage, t], device_id=device, device_id_type=MESH
        )

    def send_z(src, dst, stage, t, k):
        return pltpu.make_async_remote_copy(
            src,
            dst,
            zs_sem.at[stage, t, k],
            zr_sem.at[stage, t, k],
            device_id=along_z[k],
            device_id_type=MESH,
        )

    def sibling_slot(t, of):
        return sib.at[t] if t < 2 else part.at[2 * (t - 2) + 1 - of]

    def copies(stage, t):
        if stage == 0:
            return [send(part.at[2 * t + 1 - c], sibling_slot(t, 1 - c), 0, t, core)]
        if stage == 1:
            return [send(part_at(t, (1 - h1) * half, half), r1.at[t], 1, t, one)]
        if stage == 2:
            return [send(part_at(t, keep1 + (1 - h2) * quarter, quarter), r2.at[t], 2, t, two)]
        if stage == 3:
            return [
                send_z(part_at(t, keep2 + o * eighth, eighth), r3.at[t, k], 0, t, k)
                for k, o in enumerate(others)
            ]
        if stage == 4:
            place = out_at(t, own, eighth)
            return [send_z(place, place, 1, t, k) for k in range(n_z - 1)]
        if stage == 5:
            place = out_at(t, keep2, quarter)
            return [send(place, place, 3, t, two)]
        if stage == 6:
            place = out_at(t, keep1, half)
            return [send(place, place, 4, t, one)]
        place = out_at(t, 0, width)
        return [send(place, place, 5, t, core)]

    def add(t, row, count, got):
        def step(i, carry):
            at = pl.ds(pl.multiple_of(row + i * 48, 16), 48)
            here = part[2 * t + c, at, :].astype(f32) + got[
                pl.ds(pl.multiple_of(i * 48, 16), 48), :
            ].astype(f32)
            part[2 * t + c, at, :] = here.astype(bf16)
            return carry

        lax.fori_loop(0, count // 48, step, 0)

    def advance(stage, t):
        if stage > 0:
            for copy in copies(stage - 1, t):
                copy.wait()
        if stage == 1:
            add(t, 0, width, sibling_slot(t, c))
        elif stage == 2:
            add(t, keep1, half, r1.at[t])
        elif stage == 3:
            add(t, keep2, quarter, r2.at[t])
        elif stage == 4:
            total = part_at(t, own, eighth)[...].astype(f32)
            for k in range(n_z - 1):
                total = total + r3[t, k].astype(f32)
            part_at(t, own, eighth)[...] = total.astype(bf16)
            copy = pltpu.make_async_copy(
                part_at(t, own, eighth), out_at(t, own, eighth), out_sem.at[tiles + t]
            )
            copy.start()
            copy.wait()
        if stage < 8:
            for copy in copies(stage, t):
                copy.start()

    def vector_copies(k):
        if k < 3:
            device = (core, near_x, near_y)[k]
            ends = [(vbuf.at[2 * k], vbuf.at[2 * k + 1], k, device)]
        else:
            ends = [(vbuf.at[6], vbuf.at[7 + i], 3 + i, d) for i, d in enumerate(along_z)]
        return [
            pltpu.make_async_remote_copy(
                src, dst, vs_sem.at[s], vr_sem.at[s], device_id=d, device_id_type=MESH
            )
            for src, dst, s, d in ends
        ]

    def vector_step(k):
        if k > 0:
            for copy in vector_copies(k - 1):
                copy.wait()
        if k in (1, 2, 3):
            vbuf[2 * k] = vbuf[2 * k - 2] + vbuf[2 * k - 1]
        if k < 4:
            for copy in vector_copies(k):
                copy.start()
        else:
            total = vbuf[6]
            for i in range(n_z - 1):
                total = total + vbuf[7 + i]
            o_vec[...] = total

    entered = False
    for kind, *at in order:
        if kind == "w":
            weight_block(*at)
        elif kind == "a":
            attend_tile(*at)
        elif comm:
            if not entered:
                pl.semaphore_wait(barrier, 2 + n_z)
                entered = True
            if kind == "s":
                advance(*at)
            else:
                vector_step(*at)
    if not comm:
        o_vec[...] = vbuf[0]
        locals_ = [
            pltpu.make_async_copy(
                part.at[b],
                o_ffo.at[pl.ds(b * width, width), :]
                if b < 4
                else o_rest.at[:, pl.ds((b - 4) * width, width)],
                in_sem.at[b],
            )
            for b in range(2 * TICKS)
        ]
        for copy in locals_:
            copy.start()
        for copy in locals_:
            copy.wait()
    for tile in range(tiles):
        grad_in_store(tile).wait()


def schedule():
    steps = [
        ("w", 0), ("w", 1), ("s", 0, 0),
        ("w", 2), ("s", 1, 0), ("w", 3), ("s", 0, 1),
        ("w", 4), ("s", 1, 1), ("w", 5), ("s", 0, 2),
        ("w", 6), ("s", 2, 0), ("s", 1, 2), ("w", 7), ("s", 0, 3),
        ("a", 0), ("s", 3, 0), ("s", 2, 1), ("s", 1, 3),
        ("a", 1), ("s", 4, 0), ("s", 3, 1), ("s", 2, 2),
        ("a", 2), ("s", 5, 0), ("s", 4, 1), ("s", 3, 2),
        ("a", 3), ("w", 8), ("w", 9), ("s", 2, 3), ("s", 0, 4), ("v", 0),
        ("w", 10), ("s", 6, 0), ("s", 5, 1), ("s", 4, 2), ("s", 1, 4), ("v", 1), ("w", 11), ("s", 0, 5),
        ("s", 3, 3), ("s", 1, 5), ("v", 2),
        ("s", 7, 0), ("s", 6, 1), ("s", 5, 2), ("s", 4, 3), ("s", 2, 4), ("v", 3),
        ("s", 8, 0), ("s", 7, 1), ("s", 6, 2), ("s", 5, 3), ("s", 3, 4), ("s", 2, 5), ("v", 4),
        ("s", 8, 1), ("s", 7, 2), ("s", 4, 4), ("s", 6, 3), ("s", 3, 5),
        ("s", 5, 4), ("s", 4, 5), ("s", 8, 2), ("s", 7, 3),
        ("s", 6, 4), ("s", 5, 5), ("s", 8, 3),
        ("s", 6, 5), ("s", 7, 4), ("s", 7, 5), ("s", 8, 4), ("s", 8, 5),
    ]
    return steps


def attend_back(act, hidden_grad, ffn_grad, mixed_low, pre_grad, context, qkv, x, w_out, w_qkv, vectors, sizes, order=None):
    rows, width = x.shape
    inner = act.shape[1]
    n_z, n_x, n_y = sizes
    comm = n_x == 2 and n_y == 2 and width % (64 * n_z) == 0
    hbm = pl.BlockSpec(memory_space=pl.ANY)
    vmem = pl.BlockSpec(memory_space=pltpu.VMEM)
    shape = jax.ShapeDtypeStruct
    tiles = rows // TILE
    scratch = [
        pltpu.VMEM((4, rows, width), bf16),
        pltpu.VMEM((rows, width), bf16),
        pltpu.VMEM((rows, width), bf16),
        pltpu.VMEM((rows, width), f32),
        pltpu.VMEM((rows, width), bf16),
        pltpu.VMEM((rows, 3 * width), bf16),
        pltpu.VMEM((rows, width), bf16),
        pltpu.VMEM((width, width), bf16),
        pltpu.VMEM((width, 3 * width), bf16),
        pltpu.VMEM((rows, width), bf16),
        pltpu.VMEM((TILE, width), bf16),
        pltpu.VMEM((2 * TICKS, width, width), bf16),
        pltpu.VMEM((2, width, width), bf16),
        pltpu.VMEM((TICKS, width // 2, width), bf16),
        pltpu.VMEM((TICKS, width // 4, width), bf16),
        pltpu.VMEM((TICKS, n_z - 1, width // 4 // n_z, width), bf16),
        pltpu.VMEM((6 + n_z,) + vectors.shape, f32),
        pltpu.SemaphoreType.DMA((16,)),
        pltpu.SemaphoreType.DMA((tiles + TICKS,)),
        pltpu.SemaphoreType.DMA((6, TICKS)),
        pltpu.SemaphoreType.DMA((6, TICKS)),
        pltpu.SemaphoreType.DMA((2, TICKS, n_z - 1)),
        pltpu.SemaphoreType.DMA((2, TICKS, n_z - 1)),
        pltpu.SemaphoreType.DMA((2 + n_z,)),
        pltpu.SemaphoreType.DMA((2 + n_z,)),
    ]
    params = dict(vmem_limit_bytes=60 * MIB)
    if comm:
        params.update(collective_id=0, has_side_effects=True)
    g_ffo, rest, grad_in, vectors = pl.pallas_call(
        functools.partial(attend_back_kernel, n_z, n_x, comm, order or schedule()),
        out_shape=(
            shape((inner, width), bf16),
            shape((width, inner + 4 * width), bf16),
            shape((rows, width), f32),
            shape(vectors.shape, f32),
        ),
        in_specs=[hbm] * 10 + [vmem],
        out_specs=(hbm, hbm, hbm, vmem),
        scratch_shapes=scratch,
        compiler_params=pltpu.CompilerParams(**params),
        name="attend_back_and_sums",
    )(act, hidden_grad, ffn_grad, mixed_low, pre_grad, context, qkv, x, w_out, w_qkv, vectors)
    if not comm:
        g_ffo, rest, vectors = lax.psum((g_ffo, rest, vectors), ("wide", "narrow"))
    return g_ffo, rest, grad_in, vectors


def mesh_sizes():
    n_wide, n_narrow = lax.axis_size("wide"), lax.axis_size("narrow")
    n_y = n_narrow // 2
    n_x = n_y if n_wide % n_y == 0 else 1
    return n_wide // n_x, n_x, n_y


def per_device(
    hidden_in,
    out_grad,
    w_qkv,
    b_query,
    b_value,
    w_out,
    b_out,
    ln1_gain,
    ln1_bias,
    w_in,
    b_in,
    w_ff_out,
    b_ff_out,
    ln2_gain,
    ln2_bias,
    doc_count,
    single_flag,
):
    rows, width = hidden_in.shape
    span_count = rows // SPAN_LEN
    sizes = mesh_sizes()

    def line(vector):
        return vector.reshape(1, -1)

    qkv, context, cent = attend(
        hidden_in, w_qkv, line(b_query), line(b_value), w_out, line(b_out)
    )
    block_out, mixed_low, act, ffn_grad, hidden_grad, pre_one_grad, vectors, span_loss, loss = middle(
        cent, w_in, w_ff_out, out_grad, b_in, line(b_ff_out), line(ln1_gain), line(ln1_bias),
        line(ln2_gain), line(ln2_bias), doc_count, single_flag, sizes,
    )
    g_ffo, rest, grad_in, vectors = attend_back(
        act, hidden_grad, ffn_grad, mixed_low, pre_one_grad, context, qkv, hidden_in, w_out, w_qkv,
        vectors, sizes,
    )
    inner = w_in.shape[1]
    return (
        block_out,
        loss.reshape(()),
        span_loss.reshape(-1),
        grad_in,
        rest[:, inner + width :].astype(f32),
        vectors[0],
        vectors[1],
        rest[:, inner : inner + width].astype(f32),
        vectors[2],
        vectors[3],
        vectors[4],
        rest[:, :inner].astype(f32),
        vectors[8 : 8 + inner // width].reshape(-1),
        g_ffo.astype(f32),
        vectors[5],
        vectors[6],
        vectors[7],
    )


def solution(mesh):
    placed = (
        P(("wide", "narrow"), None),
        P(("wide", "narrow"), None),
        P(),
        P(),
        P(),
        P(),
        P(),
        P(),
        P(),
        P(),
        P(),
        P(),
        P(),
        P(),
        P(),
        P(),
        P(),
    )
    return jax.shard_map(
        per_device,
        mesh=mesh,
        in_specs=placed,
        out_specs=(
            P(("wide", "narrow"), None),
            P(),
            P(("wide", "narrow")),
            P(("wide", "narrow"), None),
            P(),
            P(),
            P(),
            P(),
            P(),
            P(),
            P(),
            P(),
            P(),
            P(),
            P(),
            P(),
            P(),
        ),
        check_vma=False,
    )
```

```python
import functools

import jax
import jax.numpy as jnp
from jax import lax
from jax.experimental import pallas as pl
from jax.experimental.pallas import tpu as pltpu
from jax.sharding import PartitionSpec as P

HEAD_DIM = 64
SPAN_LEN = 128
TILE = 256

ln_eps = 1e-06
score_scale = 0.2
far_low = -1000000000.0
head_scale = HEAD_DIM ** (-0.5)
MESH = pl.DeviceIdType.MESH
TICKS = 6
f32, bf16, i32 = jnp.float32, jnp.bfloat16, jnp.int32
MIB = 2**20


def dot(left, right):
    return jnp.dot(left, right, preferred_element_type=f32)


def dot_left_t(left, right):
    return lax.dot_general(left, right, (((0,), (0,)), ((), ())), preferred_element_type=f32)


def dot_right_t(left, right):
    return lax.dot_general(left, right, (((1,), (1,)), ((), ())), preferred_element_type=f32)


def row_mean(values):
    return jnp.mean(values, axis=1, keepdims=True)


def col_sum(values):
    return jnp.sum(values, axis=0, keepdims=True)


def norm_back(upstream, normed, scale, gain):
    scaled = upstream * gain
    return scale * (scaled - row_mean(scaled) - normed * row_mean(scaled * normed))


def head_halves():
    first = lax.broadcasted_iota(i32, (1, 2 * HEAD_DIM), 1) < HEAD_DIM
    return first, first.astype(bf16), jnp.logical_not(first).astype(bf16)


def pair_probs(stacked_queries, keys_low):
    scores = dot_right_t(stacked_queries, keys_low)
    shifted = jnp.exp((scores - jnp.max(scores, axis=1, keepdims=True)) * head_scale)
    return shifted * (1.0 / jnp.sum(shifted, axis=1, keepdims=True))


def attend_kernel(
    x_ref, w_qkv_ref, b_query_ref, b_value_ref, w_out_ref, b_out_ref, qkv_ref, context_ref, cent_ref
):
    rows, width = x_ref.shape
    inputs = x_ref[...]
    for third in range(3):
        cols = pl.ds(third * width, width)
        packed = dot(inputs, w_qkv_ref[:, cols])
        if third == 0:
            packed = packed + b_query_ref[...].astype(f32)
        if third == 2:
            packed = packed + b_value_ref[...].astype(f32)
        qkv_ref[:, cols] = packed.astype(bf16)
    first, low_one, low_two = head_halves()
    lanes = 2 * HEAD_DIM
    for span in range(rows // SPAN_LEN):
        at = pl.ds(span * SPAN_LEN, SPAN_LEN)
        for pair in range(width // lanes):
            queries = qkv_ref[at, pl.ds(pair * lanes, lanes)]
            keys_low = qkv_ref[at, pl.ds(width + pair * lanes, lanes)]
            values_low = qkv_ref[at, pl.ds(2 * width + pair * lanes, lanes)]
            stacked = jnp.concatenate([queries * low_one, queries * low_two], axis=0)
            mixed_values = dot(pair_probs(stacked, keys_low).astype(bf16), values_low)
            context_ref[at, pl.ds(pair * lanes, lanes)] = jnp.where(
                first, mixed_values[:SPAN_LEN], mixed_values[SPAN_LEN:]
            ).astype(bf16)
    attended = dot(context_ref[...], w_out_ref[...]) + b_out_ref[...].astype(f32)
    pre_one = inputs.astype(f32) + attended
    cent_ref[...] = pre_one - row_mean(pre_one)


def attend(x, w_qkv, b_query, b_value, w_out, b_out):
    rows, width = x.shape

    def whole(a):
        return pl.BlockSpec(a.shape, lambda i: (0,) * a.ndim)

    def tiles(cols):
        return pl.BlockSpec((TILE, cols), lambda i: (i, 0))

    return pl.pallas_call(
        attend_kernel,
        grid=(rows // TILE,),
        out_shape=(
            jax.ShapeDtypeStruct((rows, 3 * width), bf16),
            jax.ShapeDtypeStruct((rows, width), bf16),
            jax.ShapeDtypeStruct((rows, width), f32),
        ),
        in_specs=[tiles(width)] + [whole(a) for a in (w_qkv, b_query, b_value, w_out, b_out)],
        out_specs=(tiles(3 * width), tiles(width), tiles(width)),
        compiler_params=pltpu.CompilerParams(vmem_limit_bytes=60 * MIB),
        name="attend",
    )(x, w_qkv, b_query, b_value, w_out, b_out)


def gelu_parts(values):
    cdf = 0.5 * (1.0 + lax.erf(values * 0.7071067811865476))
    pdf = 0.3989422804014327 * jnp.exp(-0.5 * values * values)
    return values * cdf, cdf + values * pdf


def contrast_rows(cls_low, count, flags, first, span_count):
    total, width = cls_low.shape
    slots, docsets = flags.shape
    block = min(total, 256)

    def layout(at):
        slot = at + lax.broadcasted_iota(i32, (block, 1), 0)
        device = slot // slots
        place = (slot - device * slots).astype(f32)
        member = lax.broadcasted_iota(i32, (block, docsets), 1) == device
        docs = jnp.sum(jnp.where(member, count, 0.0), axis=1, keepdims=True)
        single = dot_right_t(member.astype(bf16), flags.astype(bf16))
        doc = lax.broadcasted_iota(i32, (block, slots), 1).astype(f32)
        length = jnp.where(doc < docs, 2.0 - single, 0.0)
        earlier = lax.broadcasted_iota(i32, (slots, slots), 0) < lax.broadcasted_iota(
            i32, (slots, slots), 1
        )
        begins = dot(length.astype(bf16), earlier.astype(f32).astype(bf16))
        inside = (place >= begins) & (place < begins + length)
        double = inside & (length == 2.0)
        live = jnp.max(inside.astype(f32), axis=1, keepdims=True)
        pair = jnp.max(double.astype(f32), axis=1, keepdims=True)
        other = jnp.sum(jnp.where(double, 2.0 * begins + 1.0 - place, 0.0), axis=1, keepdims=True)
        mate = jnp.where(pair > 0.0, (device * slots).astype(f32) + other, slot.astype(f32))
        return slot.astype(f32), live, pair, mate

    eye = lax.broadcasted_iota(i32, (block, block), 0) == lax.broadcasted_iota(
        i32, (block, block), 1
    )
    live_row = jnp.concatenate(
        [col_sum(jnp.where(eye, layout(at)[1], 0.0)) for at in range(0, total, block)], axis=1
    )
    column = lax.broadcasted_iota(i32, (block, total), 1).astype(f32)
    pick_col = (
        lax.broadcasted_iota(i32, (span_count, total), 1)
        == first + lax.broadcasted_iota(i32, (span_count, total), 0)
    ).astype(f32).astype(bf16)
    rows_own = jnp.zeros((span_count, total), f32)
    upward = jnp.zeros((span_count, width), f32)
    own_loss = jnp.zeros((1, span_count), f32)
    loss = jnp.zeros((1, 1), f32)
    for at in range(0, total, block):
        slot, live, pair, mate = layout(at)
        cls_block = cls_low[at : at + block, :]
        sims = score_scale * dot_right_t(cls_block, cls_low)
        allowed = (live_row > 0.0) & (column != slot)
        masked = jnp.where(allowed, sims, far_low)
        top = jnp.max(masked, axis=1, keepdims=True)
        lse = top + jnp.log(jnp.sum(jnp.exp(masked - top), axis=1, keepdims=True))
        matches = column == mate
        positive = jnp.sum(jnp.where(matches, sims, 0.0), axis=1, keepdims=True)
        span_loss = jnp.where(pair > 0.0, lse - positive, 0.0)
        loss = loss + col_sum(span_loss)
        mine = at + lax.broadcasted_iota(i32, (block, span_count), 0) == (
            first + lax.broadcasted_iota(i32, (block, span_count), 1)
        )
        own_loss = own_loss + col_sum(jnp.where(mine, span_loss, 0.0))
        sim_grad = jnp.where(
            pair > 0.0, jnp.exp(masked - lse) - matches.astype(f32), 0.0
        ).astype(bf16)
        pick_row = (
            at + lax.broadcasted_iota(i32, (span_count, block), 1)
            == first + lax.broadcasted_iota(i32, (span_count, block), 0)
        ).astype(f32).astype(bf16)
        rows_own = rows_own + dot(pick_row, sim_grad)
        cols_own = dot_right_t(pick_col, sim_grad)
        upward = upward + dot(cols_own.astype(bf16), cls_block)
    upward = upward + dot(rows_own.astype(bf16), cls_low)
    return score_scale * upward, own_loss, loss


def middle_kernel(
    n_z,
    n_x,
    n_y,
    cent_hbm,
    w_in_hbm,
    w_ffo_hbm,
    out_grad_hbm,
    b_in_ref,
    b_ffo_ref,
    gain_one_ref,
    bias_one_ref,
    gain_two_ref,
    bias_two_ref,
    count_ref,
    flag_ref,
    block_hbm,
    mixed_hbm,
    act_hbm,
    ffn_grad_hbm,
    hidden_grad_hbm,
    pre_grad_hbm,
    vec_ref,
    losses_ref,
    cent_v,
    w_in,
    w_ffo,
    upper_v,
    block_v,
    mixed_v,
    act_v,
    slope_v,
    ffn_grad_v,
    two_v,
    first_v,
    cls_grad_v,
    b_in_v,
    cls_v,
    in_sem,
    out_sem,
    s_sem,
    r_sem,
):
    rows, width = cent_v.shape
    inner = w_in.shape[1]
    chunks = inner // width
    tiles = rows // TILE
    span_count = rows // SPAN_LEN
    wide, narrow = lax.axis_index("wide"), lax.axis_index("narrow")
    z, x = wide // n_x, lax.rem(wide, n_x)
    y, c = narrow // 2, lax.rem(narrow, 2)
    core = (wide, y * 2 + 1 - c)
    along_x = [(z * n_x + lax.rem(x + k, n_x), narrow) for k in range(1, n_x)]
    along_y = [(wide, lax.rem(y + k, n_y) * 2 + c) for k in range(1, n_y)]
    along_z = [(lax.rem(z + k, n_z) * n_x + x, narrow) for k in range(1, n_z)]
    partners = [core] + along_x + along_y + along_z

    barrier = pltpu.get_barrier_semaphore()
    for device in partners:
        pl.semaphore_signal(barrier, inc=1, device_id=device, device_id_type=MESH)

    loads = [
        pltpu.make_async_copy(src, dst, in_sem.at[k])
        for k, (src, dst) in enumerate(
            ((cent_hbm, cent_v), (w_in_hbm, w_in), (w_ffo_hbm, w_ffo), (out_grad_hbm, upper_v))
        )
    ]
    for copy in loads:
        copy.start()

    def row(ref, at=0):
        return ref[pl.ds(at, width)].astype(f32).reshape(1, width)

    gain_one, bias_one, gain_two, bias_two, b_ffo = (
        row(r) for r in (gain_one_ref, bias_one_ref, gain_two_ref, bias_two_ref, b_ffo_ref)
    )
    for j in range(chunks):
        b_in_v[j : j + 1, :] = row(b_in_ref, j * width)

    def normed(cent):
        scale = lax.rsqrt(row_mean(cent * cent) + ln_eps)
        return cent * scale, scale

    def feed_forward(mixed, total, keep):
        mixed_low = mixed.astype(bf16)
        total[...] = mixed + b_ffo

        def step(j, carry):
            cols = pl.ds(pl.multiple_of(j * width, width), width)
            hidden = dot(mixed_low, w_in[:, cols]) + b_in_v[pl.ds(j, 1), :]
            act, slope = gelu_parts(hidden)
            act_low = act.astype(bf16)
            keep(cols, act_low, slope)
            total[...] += dot(act_low, w_ffo[cols, :])
            return carry

        lax.fori_loop(0, chunks, step, 0, unroll=True)
        pre_two = total[...]
        return pre_two - row_mean(pre_two)

    loads[0].wait()
    first_cent = jnp.concatenate(
        [cent_v[s * SPAN_LEN : s * SPAN_LEN + 1, :] for s in range(span_count)], axis=0
    )
    first_mixed = normed(first_cent)[0] * gain_one + bias_one
    loads[1].wait()
    loads[2].wait()
    first_two = feed_forward(first_mixed, first_v, lambda cols, act, slope: None)
    first_out = normed(first_two)[0] * gain_two + bias_two
    half = width // 2
    cls_v[z, x, y, c] = jnp.concatenate([first_out[:, :half], first_out[:, half:]], axis=0).astype(
        bf16
    )
    pl.semaphore_wait(barrier, len(partners))

    def gathers(stage):
        if stage == 0:
            ref, devices, base = cls_v.at[z, x, y, c], along_z, 0
        elif stage == 1:
            ref, devices, base = cls_v.at[:, x, y, c], along_x, n_z - 1
        elif stage == 2:
            ref, devices, base = cls_v.at[:, :, y, c], along_y, n_z + n_x - 2
        else:
            ref, devices, base = cls_v.at[:, :, :, c], [core], n_z + n_x + n_y - 3
        return [
            pltpu.make_async_remote_copy(
                ref, ref, s_sem.at[base + k], r_sem.at[base + k], device_id=d, device_id_type=MESH
            )
            for k, d in enumerate(devices)
        ]

    for copy in gathers(0):
        copy.start()
    loads[3].wait()

    def store(src, dst, at, k):
        return pltpu.make_async_copy(src.at[at, :], dst.at[at, :], out_sem.at[k])

    def tile_rows(tile):
        return pl.ds(pl.multiple_of(tile * TILE, TILE), TILE)

    def forward_stores(tile):
        at = tile_rows(tile)
        return [
            store(mixed_v, mixed_hbm, at, 6 * tile),
            store(block_v, block_hbm, at, 6 * tile + 1),
            store(act_v, act_hbm, at, 6 * tile + 2),
        ]

    def backward_stores(tile):
        at = tile_rows(tile)
        return [
            store(ffn_grad_v, ffn_grad_hbm, at, 6 * tile + 3),
            store(slope_v, hidden_grad_hbm, at, 6 * tile + 4),
            store(cent_v, pre_grad_hbm, at, 6 * tile + 5),
        ]

    def forward_tile(tile, carry):
        at = tile_rows(tile)
        mixed = normed(cent_v[at, :])[0] * gain_one + bias_one
        mixed_v[at, :] = mixed.astype(bf16)

        def keep(cols, act_low, slope):
            act_v[at, cols] = act_low
            slope_v[at, cols] = slope.astype(bf16)

        cent_two = feed_forward(mixed, two_v.at[at, :], keep)
        block_v[at, :] = (normed(cent_two)[0] * gain_two + bias_two).astype(bf16)
        two_v[at, :] = cent_two
        for copy in forward_stores(tile):
            copy.start()
        for stage in range(4):

            @pl.when(tile == min(stage, tiles - 1))
            def _():
                for copy in gathers(stage):
                    copy.wait()
                if stage < 3:
                    for copy in gathers(stage + 1):
                        copy.start()

        return carry

    lax.fori_loop(0, tiles, forward_tile, 0)

    low = cls_v[...].astype(f32).reshape(-1, 2 * span_count, half)
    cls_low = jnp.concatenate(
        [
            low[:, :span_count, :].reshape(-1, half),
            low[:, span_count:, :].reshape(-1, half),
        ],
        axis=1,
    ).astype(bf16)
    own = wide * (2 * n_y) + narrow
    cls_grad, own_loss, loss = contrast_rows(
        cls_low, count_ref[...].astype(f32).reshape(1, -1), flag_ref[...].astype(f32), own * span_count, span_count
    )
    cls_grad_v[...] = cls_grad
    lane = lax.broadcasted_iota(i32, losses_ref.shape, 1)
    losses_ref[...] = jnp.where(lane == span_count, loss, 0.0)
    losses_ref[:, :span_count] = own_loss

    vec_ref[...] = jnp.zeros(vec_ref.shape, f32)

    def add_row(k, values):
        vec_ref[pl.ds(k, 1), :] += col_sum(values)

    def backward_tile(tile, carry):
        at = tile_rows(tile)
        upper = upper_v[at, :].astype(f32)
        place = lax.broadcasted_iota(i32, (TILE, 1), 0)
        for span in range(TILE // SPAN_LEN):
            upper = jnp.where(
                place == span * SPAN_LEN,
                cls_grad_v[pl.ds(tile * (TILE // SPAN_LEN) + span, 1), :],
                upper,
            )
        normed_two, scale_two = normed(two_v[at, :])
        add_row(6, upper * normed_two)
        add_row(7, upper)
        pre_two_grad = norm_back(upper, normed_two, scale_two, gain_two)
        ffn_grad = pre_two_grad.astype(bf16)
        ffn_grad_v[at, :] = ffn_grad
        add_row(5, ffn_grad.astype(f32))
        two_v[at, :] = pre_two_grad

        def step(j, inner_carry):
            cols = pl.ds(pl.multiple_of(j * width, width), width)
            back = dot_right_t(ffn_grad, w_ffo[cols, :]) * slope_v[at, cols].astype(f32)
            hidden_grad = back.astype(bf16)
            slope_v[at, cols] = hidden_grad
            add_row(8 + j, hidden_grad.astype(f32))
            two_v[at, :] += dot_right_t(hidden_grad, w_in[:, cols])
            return inner_carry

        lax.fori_loop(0, chunks, step, 0, unroll=True)
        mixed_grad = two_v[at, :]
        normed_one, scale_one = normed(cent_v[at, :])
        add_row(3, mixed_grad * normed_one)
        add_row(4, mixed_grad)
        pre_one_grad = norm_back(mixed_grad, normed_one, scale_one, gain_one)
        cent_v[at, :] = pre_one_grad
        add_row(2, pre_one_grad.astype(bf16).astype(f32))
        for copy in backward_stores(tile):
            copy.start()
        return carry

    lax.fori_loop(0, tiles, backward_tile, 0)

    for tile in range(tiles):
        for copy in forward_stores(tile) + backward_stores(tile):
            copy.wait()


def middle(cent, w_in, w_ffo, out_grad, b_in, b_ffo, gain_one, bias_one, gain_two, bias_two, doc_count, single_flag, sizes):
    rows, width = cent.shape
    inner = w_in.shape[1]
    span_count = rows // SPAN_LEN
    n_z, n_x, n_y = sizes
    moves = n_z + n_x + n_y - 2
    hbm = pl.BlockSpec(memory_space=pl.ANY)
    vmem = pl.BlockSpec(memory_space=pltpu.VMEM)
    shape = jax.ShapeDtypeStruct
    return pl.pallas_call(
        functools.partial(middle_kernel, n_z, n_x, n_y),
        out_shape=(
            shape((rows, width), bf16),
            shape((rows, width), bf16),
            shape((rows, inner), bf16),
            shape((rows, width), bf16),
            shape((rows, inner), bf16),
            shape((rows, width), f32),
            shape((16, width), f32),
            shape((1, 128), f32),
        ),
        in_specs=[hbm] * 4 + [vmem] * 8,
        out_specs=(hbm,) * 6 + (vmem,) * 2,
        scratch_shapes=[
            pltpu.VMEM((rows, width), f32),
            pltpu.VMEM((width, inner), bf16),
            pltpu.VMEM((inner, width), bf16),
            pltpu.VMEM((rows, width), bf16),
            pltpu.VMEM((rows, width), bf16),
            pltpu.VMEM((rows, width), bf16),
            pltpu.VMEM((rows, inner), bf16),
            pltpu.VMEM((rows, inner), bf16),
            pltpu.VMEM((rows, width), bf16),
            pltpu.VMEM((rows, width), f32),
            pltpu.VMEM((span_count, width), f32),
            pltpu.VMEM((span_count, width), f32),
            pltpu.VMEM((inner // width, width), f32),
            pltpu.VMEM((n_z, n_x, n_y, 2, 2 * span_count, width // 2), bf16),
            pltpu.SemaphoreType.DMA((4,)),
            pltpu.SemaphoreType.DMA((6 * (rows // TILE),)),
            pltpu.SemaphoreType.DMA((moves,)),
            pltpu.SemaphoreType.DMA((moves,)),
        ],
        compiler_params=pltpu.CompilerParams(
            collective_id=1, has_side_effects=True, vmem_limit_bytes=58 * MIB
        ),
        name="feed_forward_and_loss",
    )(
        cent, w_in, w_ffo, out_grad, b_in, b_ffo, gain_one, bias_one, gain_two, bias_two, doc_count,
        single_flag.T,
    )


def attend_back_kernel(
    n_z,
    n_x,
    comm,
    order,
    act_hbm,
    hidden_grad_hbm,
    ffn_grad_hbm,
    mixed_hbm,
    pre_grad_hbm,
    context_hbm,
    qkv_hbm,
    x_hbm,
    w_out_hbm,
    w_qkv_hbm,
    vec_ref,
    o_ffo,
    o_rest,
    grad_in_hbm,
    o_vec,
    stream,
    ffn_grad_v,
    mixed_v,
    pre_v,
    context_v,
    qkv_v,
    x_v,
    w_out,
    w_qkv,
    attn_v,
    context_grad_v,
    part,
    sib,
    r1,
    r2,
    r3,
    vbuf,
    in_sem,
    out_sem,
    s_sem,
    r_sem,
    zs_sem,
    zr_sem,
    vs_sem,
    vr_sem,
):
    rows, width = x_v.shape
    half, quarter = width // 2, width // 4
    eighth = quarter // n_z
    tiles = rows // TILE
    ahead = stream.shape[0]
    wide, narrow = lax.axis_index("wide"), lax.axis_index("narrow")
    z, x = wide // n_x, lax.rem(wide, n_x)
    y, c = narrow // 2, lax.rem(narrow, 2)
    core = (wide, y * 2 + 1 - c)
    near_x = (z * n_x + 1 - x, narrow)
    near_y = (wide, (1 - y) * 2 + c)
    one = tuple(jnp.where(c == 0, a, b) for a, b in zip(near_x, near_y))
    two = tuple(jnp.where(c == 0, b, a) for a, b in zip(near_x, near_y))
    h1 = jnp.where(c == 0, x, y)
    h2 = jnp.where(c == 0, y, x)
    others = [lax.rem(z + k, n_z) for k in range(1, n_z)]
    along_z = [(o * n_x + x, narrow) for o in others]

    if comm:
        barrier = pltpu.get_barrier_semaphore()
        for device in [core, near_x, near_y] + along_z:
            pl.semaphore_signal(barrier, inc=1, device_id=device, device_id_type=MESH)

    def stream_load(j):
        src = act_hbm if j < 4 else hidden_grad_hbm
        return pltpu.make_async_copy(
            src.at[:, pl.ds((j % 4) * width, width)], stream.at[j % ahead], in_sem.at[j]
        )

    resident = [
        pltpu.make_async_copy(src, dst, in_sem.at[8 + k])
        for k, (src, dst) in enumerate(
            (
                (ffn_grad_hbm, ffn_grad_v),
                (mixed_hbm, mixed_v),
                (pre_grad_hbm, pre_v),
                (w_out_hbm, w_out),
                (qkv_hbm, qkv_v),
                (w_qkv_hbm, w_qkv),
                (context_hbm, context_v),
                (x_hbm, x_v),
            )
        )
    ]
    stream_load(0).start()
    resident[0].start()
    for j in range(1, ahead):
        stream_load(j).start()
    for copy in resident[1:]:
        copy.start()
    vbuf[0] = vec_ref[...]
    waited = set()

    def need(*which):
        for k in which:
            if k not in waited:
                waited.add(k)
                resident[k].wait()

    first, low_one, low_two = head_halves()
    lanes = 2 * HEAD_DIM

    def weight_block(b):
        if b < 8:
            stream_load(b).wait()
        if b < 4:
            need(0)
            left, right = stream.at[b % ahead], ffn_grad_v
        elif b < 8:
            need(1)
            left, right = mixed_v, stream.at[b % ahead]
        elif b < 9:
            need(6)
            left, right = context_v, attn_v
        else:
            need(7)
            left, right = x_v, qkv_v.at[:, pl.ds((b - 9) * width, width)]

        def step(i, carry):
            at = pl.ds(pl.multiple_of(i * TILE, TILE), TILE)
            part[b, at, :] = dot_left_t(left[:, at], right[...]).astype(bf16)
            return carry

        lax.fori_loop(0, width // TILE, step, 0, unroll=True)
        if b + ahead < 8:
            stream_load(b + ahead).start()

    def grad_in_store(tile):
        at = pl.ds(tile * TILE, TILE)
        return pltpu.make_async_copy(pre_v.at[at, :], grad_in_hbm.at[at, :], out_sem.at[tile])

    def attend_tile(tile, piece):
        need(2, 3, 4, 5)
        at = pl.ds(tile * TILE, TILE)
        if piece == 0:
            attn_grad = pre_v[at, :].astype(bf16)
            attn_v[at, :] = attn_grad
            context_grad_v[...] = dot_right_t(attn_grad, w_out[...]).astype(bf16)
        if piece == 2:
            vbuf[0, 0:1, :] += col_sum(qkv_v[at, 0:width].astype(f32))
            vbuf[0, 1:2, :] += col_sum(qkv_v[at, 2 * width : 3 * width].astype(f32))
            pre_v[at, :] += dot_right_t(qkv_v[at, :], w_qkv[...])
            grad_in_store(tile).start()
            return

        def pair_step(pair):
            q_at, k_at, v_at = (pl.ds(third * width + pair * lanes, lanes) for third in range(3))
            for span in range(TILE // SPAN_LEN):
                sp = pl.ds(tile * TILE + span * SPAN_LEN, SPAN_LEN)
                queries, keys_low, values_low = qkv_v[sp, q_at], qkv_v[sp, k_at], qkv_v[sp, v_at]
                upper = context_grad_v[pl.ds(span * SPAN_LEN, SPAN_LEN), q_at]
                stacked = jnp.concatenate([queries * low_one, queries * low_two], axis=0)
                stacked_up = jnp.concatenate([upper * low_one, upper * low_two], axis=0)
                scores = dot_right_t(keys_low, stacked)
                shifted = jnp.exp((scores - jnp.max(scores, axis=0, keepdims=True)) * head_scale)
                probs = shifted * (1.0 / col_sum(shifted))
                value_grad = dot(probs.astype(bf16), stacked_up)
                prob_grad = dot_right_t(values_low, stacked_up)
                score_grad = (probs * (prob_grad - col_sum(probs * prob_grad))).astype(bf16)
                query_grad = dot_left_t(score_grad, keys_low) * head_scale
                key_grad = dot(score_grad, stacked) * head_scale
                qkv_v[sp, q_at] = jnp.where(
                    first, query_grad[:SPAN_LEN], query_grad[SPAN_LEN:]
                ).astype(bf16)
                qkv_v[sp, k_at] = key_grad.astype(bf16)
                qkv_v[sp, v_at] = value_grad.astype(bf16)

        pairs = width // lanes
        for pair in range(pairs // 2) if piece == 0 else range(pairs // 2, pairs):
            pair_step(pair)

    def out_at(t, row, count):
        if t < 2:
            at = pl.multiple_of((2 * t + c) * width + row, 16)
            return o_ffo.at[pl.ds(at, count), :]
        cols = pl.multiple_of((2 * (t - 2) + c) * width, 128)
        return o_rest.at[pl.ds(pl.multiple_of(row, 16), count), pl.ds(cols, width)]

    def part_at(t, row, count):
        return part.at[2 * t + c, pl.ds(pl.multiple_of(row, 16), count), :]

    keep1 = h1 * half
    keep2 = keep1 + h2 * quarter
    own = keep2 + z * eighth

    def send(src, dst, stage, t, device):
        return pltpu.make_async_remote_copy(
            src, dst, s_sem.at[stage, t], r_sem.at[stage, t], device_id=device, device_id_type=MESH
        )

    def send_z(src, dst, stage, t, k):
        return pltpu.make_async_remote_copy(
            src,
            dst,
            zs_sem.at[stage, t, k],
            zr_sem.at[stage, t, k],
            device_id=along_z[k],
            device_id_type=MESH,
        )

    def sibling_slot(t, of):
        return sib.at[t] if t < 2 else part.at[2 * (t - 2) + 1 - of]

    def copies(stage, t):
        if stage == 0:
            return [send(part.at[2 * t + 1 - c], sibling_slot(t, 1 - c), 0, t, core)]
        if stage == 1:
            return [send(part_at(t, (1 - h1) * half, half), r1.at[t], 1, t, one)]
        if stage == 2:
            return [send(part_at(t, keep1 + (1 - h2) * quarter, quarter), r2.at[t], 2, t, two)]
        if stage == 3:
            return [
                send_z(part_at(t, keep2 + o * eighth, eighth), r3.at[t, k], 0, t, k)
                for k, o in enumerate(others)
            ]
        if stage == 4:
            return [
                send_z(part_at(t, own, eighth), out_at(t, own, eighth), 1, t, k)
                for k in range(n_z - 1)
            ]
        if stage == 5:
            place = out_at(t, keep2, quarter)
            return [send(place, place, 3, t, two)]
        if stage == 6:
            place = out_at(t, keep1, half)
            return [send(place, place, 4, t, one)]
        place = out_at(t, 0, width)
        return [send(place, place, 5, t, core)]

    def add(t, row, count, got):
        def step(i, carry):
            at = pl.ds(pl.multiple_of(row + i * 48, 16), 48)
            here = part[2 * t + c, at, :].astype(f32) + got[
                pl.ds(pl.multiple_of(i * 48, 16), 48), :
            ].astype(f32)
            part[2 * t + c, at, :] = here.astype(bf16)
            return carry

        lax.fori_loop(0, count // 48, step, 0)

    def own_store(t):
        return pltpu.make_async_copy(
            part_at(t, own, eighth), out_at(t, own, eighth), out_sem.at[tiles + t]
        )

    def advance(stage, t):
        if stage > 0:
            for copy in copies(stage - 1, t):
                copy.wait()
        if stage == 1:
            add(t, 0, width, sibling_slot(t, c))
        elif stage == 2:
            add(t, keep1, half, r1.at[t])
        elif stage == 3:
            add(t, keep2, quarter, r2.at[t])
        elif stage == 4:
            total = part_at(t, own, eighth)[...].astype(f32)
            for k in range(n_z - 1):
                total = total + r3[t, k].astype(f32)
            part_at(t, own, eighth)[...] = total.astype(bf16)
            own_store(t).start()
        elif stage == 5:
            own_store(t).wait()
        if stage < 8:
            for copy in copies(stage, t):
                copy.start()

    def vector_copies(k):
        if k < 3:
            device = (core, near_x, near_y)[k]
            ends = [(vbuf.at[2 * k], vbuf.at[2 * k + 1], k, device)]
        else:
            ends = [(vbuf.at[6], vbuf.at[7 + i], 3 + i, d) for i, d in enumerate(along_z)]
        return [
            pltpu.make_async_remote_copy(
                src, dst, vs_sem.at[s], vr_sem.at[s], device_id=d, device_id_type=MESH
            )
            for src, dst, s, d in ends
        ]

    def vector_step(k):
        if k > 0:
            for copy in vector_copies(k - 1):
                copy.wait()
        if k in (1, 2, 3):
            vbuf[2 * k] = vbuf[2 * k - 2] + vbuf[2 * k - 1]
        if k < 4:
            for copy in vector_copies(k):
                copy.start()
        else:
            total = vbuf[6]
            for i in range(n_z - 1):
                total = total + vbuf[7 + i]
            o_vec[...] = total

    entered = False
    for kind, *at in order:
        if kind == "w":
            weight_block(*at)
        elif kind == "a":
            attend_tile(*at)
        elif comm:
            if not entered:
                pl.semaphore_wait(barrier, 2 + n_z)
                entered = True
            if kind == "s":
                advance(*at)
            else:
                vector_step(*at)
    if not comm:
        o_vec[...] = vbuf[0]
        locals_ = [
            pltpu.make_async_copy(
                part.at[b],
                o_ffo.at[pl.ds(b * width, width), :]
                if b < 4
                else o_rest.at[:, pl.ds((b - 4) * width, width)],
                in_sem.at[b],
            )
            for b in range(2 * TICKS)
        ]
        for copy in locals_:
            copy.start()
        for copy in locals_:
            copy.wait()
    for tile in range(tiles):
        grad_in_store(tile).wait()


def schedule():
    return [
        ("w", 0), ("w", 1), ("s", 0, 0), ("w", 2), ("w", 3), ("s", 1, 0), ("s", 0, 1), ("w", 4),
        ("w", 5), ("s", 1, 1), ("s", 0, 2), ("w", 6), ("w", 7), ("s", 2, 0), ("s", 1, 2),
        ("s", 0, 3), ("a", 0, 0), ("s", 1, 3), ("a", 0, 1), ("a", 0, 2), ("a", 1, 0), ("s", 3, 0),
        ("s", 2, 1), ("a", 1, 1), ("a", 1, 2), ("a", 2, 0), ("a", 2, 1), ("s", 4, 0), ("s", 2, 2),
        ("a", 2, 2), ("s", 3, 1), ("s", 2, 3), ("a", 3, 0), ("a", 3, 1), ("s", 3, 2), ("a", 3, 2),
        ("s", 3, 3), ("v", 0), ("w", 8), ("w", 9), ("s", 0, 4), ("s", 5, 0), ("v", 1), ("w", 10),
        ("w", 11), ("s", 1, 4), ("s", 6, 0), ("v", 2), ("s", 0, 5), ("s", 4, 1), ("s", 1, 5),
        ("s", 4, 2), ("v", 3), ("s", 4, 3), ("s", 2, 4), ("s", 7, 0), ("s", 5, 1), ("v", 4),
        ("s", 2, 5), ("s", 8, 0), ("s", 5, 2), ("s", 5, 3), ("s", 3, 4), ("s", 6, 1), ("s", 3, 5),
        ("s", 4, 4), ("s", 6, 2), ("s", 6, 3), ("s", 4, 5), ("s", 7, 1), ("s", 5, 4), ("s", 8, 1),
        ("s", 5, 5), ("s", 7, 2), ("s", 7, 3), ("s", 6, 4), ("s", 8, 2), ("s", 8, 3), ("s", 6, 5),
        ("s", 7, 4), ("s", 7, 5), ("s", 8, 4), ("s", 8, 5),
    ]


def attend_back(act, hidden_grad, ffn_grad, mixed_low, pre_grad, context, qkv, x, w_out, w_qkv, vectors, sizes, order=None):
    rows, width = x.shape
    inner = act.shape[1]
    n_z, n_x, n_y = sizes
    comm = n_x == 2 and n_y == 2 and width % (64 * n_z) == 0
    hbm = pl.BlockSpec(memory_space=pl.ANY)
    vmem = pl.BlockSpec(memory_space=pltpu.VMEM)
    shape = jax.ShapeDtypeStruct
    tiles = rows // TILE
    scratch = [
        pltpu.VMEM((4, rows, width), bf16),
        pltpu.VMEM((rows, width), bf16),
        pltpu.VMEM((rows, width), bf16),
        pltpu.VMEM((rows, width), f32),
        pltpu.VMEM((rows, width), bf16),
        pltpu.VMEM((rows, 3 * width), bf16),
        pltpu.VMEM((rows, width), bf16),
        pltpu.VMEM((width, width), bf16),
        pltpu.VMEM((width, 3 * width), bf16),
        pltpu.VMEM((rows, width), bf16),
        pltpu.VMEM((TILE, width), bf16),
        pltpu.VMEM((2 * TICKS, width, width), bf16),
        pltpu.VMEM((2, width, width), bf16),
        pltpu.VMEM((TICKS, width // 2, width), bf16),
        pltpu.VMEM((TICKS, width // 4, width), bf16),
        pltpu.VMEM((TICKS, n_z - 1, width // 4 // n_z, width), bf16),
        pltpu.VMEM((6 + n_z,) + vectors.shape, f32),
        pltpu.SemaphoreType.DMA((16,)),
        pltpu.SemaphoreType.DMA((tiles + TICKS,)),
        pltpu.SemaphoreType.DMA((6, TICKS)),
        pltpu.SemaphoreType.DMA((6, TICKS)),
        pltpu.SemaphoreType.DMA((2, TICKS, n_z - 1)),
        pltpu.SemaphoreType.DMA((2, TICKS, n_z - 1)),
        pltpu.SemaphoreType.DMA((2 + n_z,)),
        pltpu.SemaphoreType.DMA((2 + n_z,)),
    ]
    params = dict(vmem_limit_bytes=60 * MIB)
    if comm:
        params.update(collective_id=0, has_side_effects=True)
    g_ffo, rest, grad_in, vectors = pl.pallas_call(
        functools.partial(attend_back_kernel, n_z, n_x, comm, order or schedule()),
        out_shape=(
            shape((inner, width), bf16),
            shape((width, inner + 4 * width), bf16),
            shape((rows, width), f32),
            shape(vectors.shape, f32),
        ),
        in_specs=[hbm] * 10 + [vmem],
        out_specs=(hbm, hbm, hbm, vmem),
        scratch_shapes=scratch,
        compiler_params=pltpu.CompilerParams(**params),
        name="attend_back_and_sums",
    )(act, hidden_grad, ffn_grad, mixed_low, pre_grad, context, qkv, x, w_out, w_qkv, vectors)
    if not comm:
        g_ffo, rest, vectors = lax.psum((g_ffo, rest, vectors), ("wide", "narrow"))
    return g_ffo, rest, grad_in, vectors


def widen_kernel(ffo_ref, rest_ref, vec_ref, losses_ref, w_ffo, w_in, w_out, w_qkv, span_loss, loss, b_in, *vectors):
    inner, width = w_in.shape[1], w_out.shape[1]
    w_ffo[...] = ffo_ref[...].astype(f32)
    w_in[...] = rest_ref[:, :inner].astype(f32)
    w_out[...] = rest_ref[:, inner : inner + width].astype(f32)
    w_qkv[...] = rest_ref[:, inner + width :].astype(f32)

    @pl.when(pl.program_id(0) == 0)
    def _():
        count = span_loss.shape[0]
        span_loss[...] = losses_ref[:, :count].reshape(count)
        loss[...] = losses_ref[:, count : count + 1].reshape(1)
        for k, vector in enumerate(vectors):
            vector[...] = vec_ref[k : k + 1, :].reshape(vector.shape)
        for j in range(inner // width):
            at = 8 + j
            b_in[pl.ds(j * width, width)] = vec_ref[at : at + 1, :].reshape(width)


def widen(ffo, rest, vectors, losses, span_count):
    inner, width = ffo.shape
    steps = 12
    shape = jax.ShapeDtypeStruct

    def tiles(rows, cols):
        return pl.BlockSpec((rows // steps, cols), lambda i: (i, 0))

    def whole(*sizes):
        return pl.BlockSpec(sizes, lambda i: (0,) * len(sizes))

    flat = [span_count, 1, inner] + [width] * 8
    return pl.pallas_call(
        widen_kernel,
        grid=(steps,),
        out_shape=(
            shape((inner, width), f32),
            shape((width, inner), f32),
            shape((width, width), f32),
            shape((width, 3 * width), f32),
            *(shape((n,), f32) for n in flat),
        ),
        in_specs=[
            tiles(inner, width),
            tiles(width, rest.shape[1]),
            whole(*vectors.shape),
            whole(*losses.shape),
        ],
        out_specs=(
            tiles(inner, width),
            tiles(width, inner),
            tiles(width, width),
            tiles(width, 3 * width),
            *(whole(n) for n in flat),
        ),
        compiler_params=pltpu.CompilerParams(vmem_limit_bytes=60 * MIB),
        name="widen",
    )(ffo, rest, vectors, losses)


def mesh_sizes():
    n_wide, n_narrow = lax.axis_size("wide"), lax.axis_size("narrow")
    n_y = n_narrow // 2
    n_x = n_y if n_wide % n_y == 0 else 1
    return n_wide // n_x, n_x, n_y


def per_device(
    hidden_in,
    out_grad,
    w_qkv,
    b_query,
    b_value,
    w_out,
    b_out,
    ln1_gain,
    ln1_bias,
    w_in,
    b_in,
    w_ff_out,
    b_ff_out,
    ln2_gain,
    ln2_bias,
    doc_count,
    single_flag,
):
    rows, width = hidden_in.shape
    span_count = rows // SPAN_LEN
    sizes = mesh_sizes()

    qkv, context, cent = attend(
        hidden_in, w_qkv, b_query, b_value, w_out, b_out
    )
    block_out, mixed_low, act, ffn_grad, hidden_grad, pre_one_grad, vectors, losses = middle(
        cent, w_in, w_ff_out, out_grad, b_in, b_ff_out, ln1_gain, ln1_bias,
        ln2_gain, ln2_bias, doc_count, single_flag, sizes,
    )
    g_ffo, rest, grad_in, vectors = attend_back(
        act, hidden_grad, ffn_grad, mixed_low, pre_one_grad, context, qkv, hidden_in, w_out, w_qkv,
        vectors, sizes,
    )
    g_ffo, g_in, g_out, g_qkv, span_loss, loss, g_b_in, *rest_grads = widen(
        g_ffo, rest, vectors, losses, span_count
    )
    g_b_query, g_b_value, g_b_out, g_gain_one, g_bias_one, g_b_ffo, g_gain_two, g_bias_two = rest_grads
    return (
        block_out,
        loss.reshape(()),
        span_loss,
        grad_in,
        g_qkv,
        g_b_query,
        g_b_value,
        g_out,
        g_b_out,
        g_gain_one,
        g_bias_one,
        g_in,
        g_b_in,
        g_ffo,
        g_b_ffo,
        g_gain_two,
        g_bias_two,
    )


def solution(mesh):
    placed = (
        P(("wide", "narrow"), None),
        P(("wide", "narrow"), None),
        P(),
        P(),
        P(),
        P(),
        P(),
        P(),
        P(),
        P(),
        P(),
        P(),
        P(),
        P(),
        P(),
        P(),
        P(),
    )
    return jax.shard_map(
        per_device,
        mesh=mesh,
        in_specs=placed,
        out_specs=(
            P(("wide", "narrow"), None),
            P(),
            P(("wide", "narrow")),
            P(("wide", "narrow"), None),
            P(),
            P(),
            P(),
            P(),
            P(),
            P(),
            P(),
            P(),
            P(),
            P(),
            P(),
            P(),
            P(),
        ),
        check_vma=False,
    )
```

```python
import functools

import jax
import jax.numpy as jnp
from jax import lax
from jax.experimental import pallas as pl
from jax.experimental.pallas import tpu as pltpu
from jax.sharding import PartitionSpec as P

HEAD_DIM = 64
SPAN_LEN = 128
TILE = 256

ln_eps = 1e-06
score_scale = 0.2
far_low = -1000000000.0
head_scale = HEAD_DIM ** (-0.5)
MESH = pl.DeviceIdType.MESH
TICKS = 6
f32, bf16, i32 = jnp.float32, jnp.bfloat16, jnp.int32
MIB = 2**20


def dot(left, right):
    return jnp.dot(left, right, preferred_element_type=f32)


def dot_left_t(left, right):
    return lax.dot_general(left, right, (((0,), (0,)), ((), ())), preferred_element_type=f32)


def dot_right_t(left, right):
    return lax.dot_general(left, right, (((1,), (1,)), ((), ())), preferred_element_type=f32)


def row_mean(values):
    return jnp.mean(values, axis=1, keepdims=True)


def col_sum(values):
    return jnp.sum(values, axis=0, keepdims=True)


def norm_back(upstream, normed, scale, gain):
    scaled = upstream * gain
    return scale * (scaled - row_mean(scaled) - normed * row_mean(scaled * normed))


def head_halves():
    first = lax.broadcasted_iota(i32, (1, 2 * HEAD_DIM), 1) < HEAD_DIM
    return first, first.astype(bf16), jnp.logical_not(first).astype(bf16)


def pair_probs(stacked_queries, keys_low):
    scores = dot_right_t(stacked_queries, keys_low)
    shifted = jnp.exp((scores - jnp.max(scores, axis=1, keepdims=True)) * head_scale)
    return shifted * (1.0 / jnp.sum(shifted, axis=1, keepdims=True))


def attend_tile(at, x_ref, w_qkv_ref, b_query, b_value, w_out_ref, b_out, qkv_ref, context_ref, cent_ref):
    width = x_ref.shape[1]
    inputs = x_ref[at, :]
    for third in range(3):
        cols = pl.ds(third * width, width)
        packed = dot(inputs, w_qkv_ref[:, cols])
        if third == 0:
            packed = packed + b_query
        if third == 2:
            packed = packed + b_value
        qkv_ref[at, cols] = packed.astype(bf16)
    first, low_one, low_two = head_halves()
    lanes = 2 * HEAD_DIM
    for span in range(at.size // SPAN_LEN):
        sp = pl.ds(pl.multiple_of(at.start + span * SPAN_LEN, SPAN_LEN), SPAN_LEN)
        for pair in range(width // lanes):
            queries = qkv_ref[sp, pl.ds(pair * lanes, lanes)]
            keys_low = qkv_ref[sp, pl.ds(width + pair * lanes, lanes)]
            values_low = qkv_ref[sp, pl.ds(2 * width + pair * lanes, lanes)]
            stacked = jnp.concatenate([queries * low_one, queries * low_two], axis=0)
            mixed_values = dot(pair_probs(stacked, keys_low).astype(bf16), values_low)
            context_ref[sp, pl.ds(pair * lanes, lanes)] = jnp.where(
                first, mixed_values[:SPAN_LEN], mixed_values[SPAN_LEN:]
            ).astype(bf16)
    pre_one = inputs.astype(f32) + (dot(context_ref[at, :], w_out_ref[...]) + b_out)
    cent_ref[at, :] = pre_one - row_mean(pre_one)


def gelu_parts(values):
    cdf = 0.5 * (1.0 + lax.erf(values * 0.7071067811865476))
    pdf = 0.3989422804014327 * jnp.exp(-0.5 * values * values)
    return values * cdf, cdf + values * pdf


def contrast_rows(cls_low, count, flags, first, span_count):
    total, width = cls_low.shape
    slots, docsets = flags.shape
    block = min(total, 256)

    def layout(at):
        slot = at + lax.broadcasted_iota(i32, (block, 1), 0)
        device = slot // slots
        place = (slot - device * slots).astype(f32)
        member = lax.broadcasted_iota(i32, (block, docsets), 1) == device
        docs = jnp.sum(jnp.where(member, count, 0.0), axis=1, keepdims=True)
        single = dot_right_t(member.astype(bf16), flags.astype(bf16))
        doc = lax.broadcasted_iota(i32, (block, slots), 1).astype(f32)
        length = jnp.where(doc < docs, 2.0 - single, 0.0)
        earlier = lax.broadcasted_iota(i32, (slots, slots), 0) < lax.broadcasted_iota(
            i32, (slots, slots), 1
        )
        begins = dot(length.astype(bf16), earlier.astype(f32).astype(bf16))
        inside = (place >= begins) & (place < begins + length)
        double = inside & (length == 2.0)
        live = jnp.max(inside.astype(f32), axis=1, keepdims=True)
        pair = jnp.max(double.astype(f32), axis=1, keepdims=True)
        other = jnp.sum(jnp.where(double, 2.0 * begins + 1.0 - place, 0.0), axis=1, keepdims=True)
        mate = jnp.where(pair > 0.0, (device * slots).astype(f32) + other, slot.astype(f32))
        return slot.astype(f32), live, pair, mate

    eye = lax.broadcasted_iota(i32, (block, block), 0) == lax.broadcasted_iota(
        i32, (block, block), 1
    )
    live_row = jnp.concatenate(
        [col_sum(jnp.where(eye, layout(at)[1], 0.0)) for at in range(0, total, block)], axis=1
    )
    column = lax.broadcasted_iota(i32, (block, total), 1).astype(f32)
    pick_col = (
        lax.broadcasted_iota(i32, (span_count, total), 1)
        == first + lax.broadcasted_iota(i32, (span_count, total), 0)
    ).astype(f32).astype(bf16)
    rows_own = jnp.zeros((span_count, total), f32)
    upward = jnp.zeros((span_count, width), f32)
    own_loss = jnp.zeros((1, span_count), f32)
    loss = jnp.zeros((1, 1), f32)
    for at in range(0, total, block):
        slot, live, pair, mate = layout(at)
        cls_block = cls_low[at : at + block, :]
        sims = score_scale * dot_right_t(cls_block, cls_low)
        allowed = (live_row > 0.0) & (column != slot)
        masked = jnp.where(allowed, sims, far_low)
        top = jnp.max(masked, axis=1, keepdims=True)
        lse = top + jnp.log(jnp.sum(jnp.exp(masked - top), axis=1, keepdims=True))
        matches = column == mate
        positive = jnp.sum(jnp.where(matches, sims, 0.0), axis=1, keepdims=True)
        span_loss = jnp.where(pair > 0.0, lse - positive, 0.0)
        loss = loss + col_sum(span_loss)
        mine = at + lax.broadcasted_iota(i32, (block, span_count), 0) == (
            first + lax.broadcasted_iota(i32, (block, span_count), 1)
        )
        own_loss = own_loss + col_sum(jnp.where(mine, span_loss, 0.0))
        sim_grad = jnp.where(
            pair > 0.0, jnp.exp(masked - lse) - matches.astype(f32), 0.0
        ).astype(bf16)
        pick_row = (
            at + lax.broadcasted_iota(i32, (span_count, block), 1)
            == first + lax.broadcasted_iota(i32, (span_count, block), 0)
        ).astype(f32).astype(bf16)
        rows_own = rows_own + dot(pick_row, sim_grad)
        cols_own = dot_right_t(pick_col, sim_grad)
        upward = upward + dot(cols_own.astype(bf16), cls_block)
    upward = upward + dot(rows_own.astype(bf16), cls_low)
    return score_scale * upward, own_loss, loss


def middle_kernel(
    n_z,
    n_x,
    n_y,
    x_hbm,
    w_qkv_hbm,
    w_out_hbm,
    w_in_hbm,
    w_ffo_hbm,
    out_grad_hbm,
    b_query_ref,
    b_value_ref,
    b_out_ref,
    b_in_ref,
    b_ffo_ref,
    gain_one_ref,
    bias_one_ref,
    gain_two_ref,
    bias_two_ref,
    count_ref,
    flag_ref,
    qkv_hbm,
    context_hbm,
    block_hbm,
    mixed_hbm,
    act_hbm,
    ffn_grad_hbm,
    hidden_grad_hbm,
    pre_grad_hbm,
    vec_ref,
    losses_ref,
    x_v,
    w_qkv,
    w_out,
    qkv_v,
    context_v,
    cent_v,
    w_in,
    w_ffo,
    upper_v,
    block_v,
    mixed_v,
    act_v,
    slope_v,
    ffn_grad_v,
    two_v,
    first_v,
    cls_grad_v,
    b_in_v,
    cls_v,
    in_sem,
    out_sem,
    s_sem,
    r_sem,
):
    rows, width = cent_v.shape
    inner = w_in.shape[1]
    chunks = inner // width
    tiles = rows // TILE
    span_count = rows // SPAN_LEN
    wide, narrow = lax.axis_index("wide"), lax.axis_index("narrow")
    z, x = wide // n_x, lax.rem(wide, n_x)
    y, c = narrow // 2, lax.rem(narrow, 2)
    core = (wide, y * 2 + 1 - c)
    along_x = [(z * n_x + lax.rem(x + k, n_x), narrow) for k in range(1, n_x)]
    along_y = [(wide, lax.rem(y + k, n_y) * 2 + c) for k in range(1, n_y)]
    along_z = [(lax.rem(z + k, n_z) * n_x + x, narrow) for k in range(1, n_z)]
    partners = [core] + along_x + along_y + along_z

    barrier = pltpu.get_barrier_semaphore()
    for device in partners:
        pl.semaphore_signal(barrier, inc=1, device_id=device, device_id_type=MESH)

    loads = [
        pltpu.make_async_copy(src, dst, in_sem.at[k])
        for k, (src, dst) in enumerate(
            (
                (x_hbm, x_v),
                (w_qkv_hbm, w_qkv),
                (w_out_hbm, w_out),
                (w_in_hbm, w_in),
                (w_ffo_hbm, w_ffo),
                (out_grad_hbm, upper_v),
            )
        )
    ]
    for copy in loads:
        copy.start()

    def row(ref, at=0):
        return ref[pl.ds(at, width)].astype(f32).reshape(1, width)

    gain_one, bias_one, gain_two, bias_two, b_ffo = (
        row(r) for r in (gain_one_ref, bias_one_ref, gain_two_ref, bias_two_ref, b_ffo_ref)
    )
    for j in range(chunks):
        b_in_v[j : j + 1, :] = row(b_in_ref, j * width)

    def normed(cent):
        scale = lax.rsqrt(row_mean(cent * cent) + ln_eps)
        return cent * scale, scale

    def feed_forward(mixed, total, keep):
        mixed_low = mixed.astype(bf16)
        total[...] = mixed + b_ffo

        def step(j, carry):
            cols = pl.ds(pl.multiple_of(j * width, width), width)
            hidden = dot(mixed_low, w_in[:, cols]) + b_in_v[pl.ds(j, 1), :]
            act, slope = gelu_parts(hidden)
            act_low = act.astype(bf16)
            keep(cols, act_low, slope)
            total[...] += dot(act_low, w_ffo[cols, :])
            return carry

        lax.fori_loop(0, chunks, step, 0, unroll=True)
        pre_two = total[...]
        return pre_two - row_mean(pre_two)

    b_query, b_value, b_out = (row(r) for r in (b_query_ref, b_value_ref, b_out_ref))

    def store(src, dst, at, k):
        return pltpu.make_async_copy(src.at[at, :], dst.at[at, :], out_sem.at[k])

    def tile_rows(tile):
        return pl.ds(pl.multiple_of(tile * TILE, TILE), TILE)

    def attend_stores(tile):
        at = tile_rows(tile)
        return [
            store(qkv_v, qkv_hbm, at, 8 * tile + 6),
            store(context_v, context_hbm, at, 8 * tile + 7),
        ]

    def attend_step(tile, carry):
        attend_tile(
            tile_rows(tile), x_v, w_qkv, b_query, b_value, w_out, b_out, qkv_v, context_v, cent_v
        )
        for copy in attend_stores(tile):
            copy.start()
        return carry

    for copy in loads[:3]:
        copy.wait()
    lax.fori_loop(0, tiles, attend_step, 0)

    first_cent = jnp.concatenate(
        [cent_v[s * SPAN_LEN : s * SPAN_LEN + 1, :] for s in range(span_count)], axis=0
    )
    first_mixed = normed(first_cent)[0] * gain_one + bias_one
    loads[3].wait()
    loads[4].wait()
    first_two = feed_forward(first_mixed, first_v, lambda cols, act, slope: None)
    first_out = normed(first_two)[0] * gain_two + bias_two
    half = width // 2
    cls_v[z, x, y, c] = jnp.concatenate([first_out[:, :half], first_out[:, half:]], axis=0).astype(
        bf16
    )
    pl.semaphore_wait(barrier, len(partners))

    def gathers(stage):
        if stage == 0:
            ref, devices, base = cls_v.at[z, x, y, c], along_z, 0
        elif stage == 1:
            ref, devices, base = cls_v.at[:, x, y, c], along_x, n_z - 1
        elif stage == 2:
            ref, devices, base = cls_v.at[:, :, y, c], along_y, n_z + n_x - 2
        else:
            ref, devices, base = cls_v.at[:, :, :, c], [core], n_z + n_x + n_y - 3
        return [
            pltpu.make_async_remote_copy(
                ref, ref, s_sem.at[base + k], r_sem.at[base + k], device_id=d, device_id_type=MESH
            )
            for k, d in enumerate(devices)
        ]

    for copy in gathers(0):
        copy.start()
    loads[5].wait()

    def forward_stores(tile):
        at = tile_rows(tile)
        return [
            store(mixed_v, mixed_hbm, at, 8 * tile),
            store(block_v, block_hbm, at, 8 * tile + 1),
            store(act_v, act_hbm, at, 8 * tile + 2),
        ]

    def backward_stores(tile):
        at = tile_rows(tile)
        return [
            store(ffn_grad_v, ffn_grad_hbm, at, 8 * tile + 3),
            store(slope_v, hidden_grad_hbm, at, 8 * tile + 4),
            store(cent_v, pre_grad_hbm, at, 8 * tile + 5),
        ]

    def forward_tile(tile, carry):
        at = tile_rows(tile)
        mixed = normed(cent_v[at, :])[0] * gain_one + bias_one
        mixed_v[at, :] = mixed.astype(bf16)

        def keep(cols, act_low, slope):
            act_v[at, cols] = act_low
            slope_v[at, cols] = slope.astype(bf16)

        cent_two = feed_forward(mixed, two_v.at[at, :], keep)
        block_v[at, :] = (normed(cent_two)[0] * gain_two + bias_two).astype(bf16)
        two_v[at, :] = cent_two
        for copy in forward_stores(tile):
            copy.start()
        for stage in range(4):

            @pl.when(tile == min(stage, tiles - 1))
            def _():
                for copy in gathers(stage):
                    copy.wait()
                if stage < 3:
                    for copy in gathers(stage + 1):
                        copy.start()

        return carry

    lax.fori_loop(0, tiles, forward_tile, 0)

    low = cls_v[...].astype(f32).reshape(-1, 2 * span_count, half)
    cls_low = jnp.concatenate(
        [
            low[:, :span_count, :].reshape(-1, half),
            low[:, span_count:, :].reshape(-1, half),
        ],
        axis=1,
    ).astype(bf16)
    own = wide * (2 * n_y) + narrow
    cls_grad, own_loss, loss = contrast_rows(
        cls_low, count_ref[...].astype(f32).reshape(1, -1), flag_ref[...].astype(f32), own * span_count, span_count
    )
    cls_grad_v[...] = cls_grad
    lane = lax.broadcasted_iota(i32, losses_ref.shape, 1)
    losses_ref[...] = jnp.where(lane == span_count, loss, 0.0)
    losses_ref[:, :span_count] = own_loss

    vec_ref[...] = jnp.zeros(vec_ref.shape, f32)

    def add_row(k, values):
        vec_ref[pl.ds(k, 1), :] += col_sum(values)

    def backward_tile(tile, carry):
        at = tile_rows(tile)
        upper = upper_v[at, :].astype(f32)
        place = lax.broadcasted_iota(i32, (TILE, 1), 0)
        for span in range(TILE // SPAN_LEN):
            upper = jnp.where(
                place == span * SPAN_LEN,
                cls_grad_v[pl.ds(tile * (TILE // SPAN_LEN) + span, 1), :],
                upper,
            )
        normed_two, scale_two = normed(two_v[at, :])
        add_row(6, upper * normed_two)
        add_row(7, upper)
        pre_two_grad = norm_back(upper, normed_two, scale_two, gain_two)
        ffn_grad = pre_two_grad.astype(bf16)
        ffn_grad_v[at, :] = ffn_grad
        add_row(5, ffn_grad.astype(f32))
        two_v[at, :] = pre_two_grad

        def step(j, inner_carry):
            cols = pl.ds(pl.multiple_of(j * width, width), width)
            back = dot_right_t(ffn_grad, w_ffo[cols, :]) * slope_v[at, cols].astype(f32)
            hidden_grad = back.astype(bf16)
            slope_v[at, cols] = hidden_grad
            add_row(8 + j, hidden_grad.astype(f32))
            two_v[at, :] += dot_right_t(hidden_grad, w_in[:, cols])
            return inner_carry

        lax.fori_loop(0, chunks, step, 0, unroll=True)
        mixed_grad = two_v[at, :]
        normed_one, scale_one = normed(cent_v[at, :])
        add_row(3, mixed_grad * normed_one)
        add_row(4, mixed_grad)
        pre_one_grad = norm_back(mixed_grad, normed_one, scale_one, gain_one)
        cent_v[at, :] = pre_one_grad
        add_row(2, pre_one_grad.astype(bf16).astype(f32))
        for copy in backward_stores(tile):
            copy.start()
        return carry

    lax.fori_loop(0, tiles, backward_tile, 0)

    for tile in range(tiles):
        for copy in attend_stores(tile) + forward_stores(tile) + backward_stores(tile):
            copy.wait()


def middle(
    x,
    w_qkv,
    w_out,
    w_in,
    w_ffo,
    out_grad,
    b_query,
    b_value,
    b_out,
    b_in,
    b_ffo,
    gain_one,
    bias_one,
    gain_two,
    bias_two,
    doc_count,
    single_flag,
    sizes,
):
    rows, width = x.shape
    inner = w_in.shape[1]
    span_count = rows // SPAN_LEN
    n_z, n_x, n_y = sizes
    moves = n_z + n_x + n_y - 2
    hbm = pl.BlockSpec(memory_space=pl.ANY)
    vmem = pl.BlockSpec(memory_space=pltpu.VMEM)
    shape = jax.ShapeDtypeStruct
    return pl.pallas_call(
        functools.partial(middle_kernel, n_z, n_x, n_y),
        out_shape=(
            shape((rows, 3 * width), bf16),
            shape((rows, width), bf16),
            shape((rows, width), bf16),
            shape((rows, width), bf16),
            shape((rows, inner), bf16),
            shape((rows, width), bf16),
            shape((rows, inner), bf16),
            shape((rows, width), f32),
            shape((16, width), f32),
            shape((1, 128), f32),
        ),
        in_specs=[hbm] * 6 + [vmem] * 11,
        out_specs=(hbm,) * 8 + (vmem,) * 2,
        scratch_shapes=[
            pltpu.VMEM((rows, width), bf16),
            pltpu.VMEM((width, 3 * width), bf16),
            pltpu.VMEM((width, width), bf16),
            pltpu.VMEM((rows, 3 * width), bf16),
            pltpu.VMEM((rows, width), bf16),
            pltpu.VMEM((rows, width), f32),
            pltpu.VMEM((width, inner), bf16),
            pltpu.VMEM((inner, width), bf16),
            pltpu.VMEM((rows, width), bf16),
            pltpu.VMEM((rows, width), bf16),
            pltpu.VMEM((rows, width), bf16),
            pltpu.VMEM((rows, inner), bf16),
            pltpu.VMEM((rows, inner), bf16),
            pltpu.VMEM((rows, width), bf16),
            pltpu.VMEM((rows, width), f32),
            pltpu.VMEM((span_count, width), f32),
            pltpu.VMEM((span_count, width), f32),
            pltpu.VMEM((inner // width, width), f32),
            pltpu.VMEM((n_z, n_x, n_y, 2, 2 * span_count, width // 2), bf16),
            pltpu.SemaphoreType.DMA((6,)),
            pltpu.SemaphoreType.DMA((8 * (rows // TILE),)),
            pltpu.SemaphoreType.DMA((moves,)),
            pltpu.SemaphoreType.DMA((moves,)),
        ],
        compiler_params=pltpu.CompilerParams(
            collective_id=1, has_side_effects=True, vmem_limit_bytes=60 * MIB
        ),
        name="forward_and_loss",
    )(
        x, w_qkv, w_out, w_in, w_ffo, out_grad, b_query, b_value, b_out, b_in, b_ffo, gain_one, bias_one,
        gain_two, bias_two, doc_count, single_flag.T,
    )


def attend_back_kernel(
    n_z,
    n_x,
    comm,
    order,
    act_hbm,
    hidden_grad_hbm,
    ffn_grad_hbm,
    mixed_hbm,
    pre_grad_hbm,
    context_hbm,
    qkv_hbm,
    x_hbm,
    w_out_hbm,
    w_qkv_hbm,
    vec_ref,
    o_ffo,
    o_rest,
    grad_in_hbm,
    o_vec,
    stream,
    ffn_grad_v,
    mixed_v,
    pre_v,
    context_v,
    qkv_v,
    x_v,
    w_out,
    w_qkv,
    attn_v,
    context_grad_v,
    part,
    sib,
    r1,
    r2,
    r3,
    vbuf,
    in_sem,
    out_sem,
    s_sem,
    r_sem,
    zs_sem,
    zr_sem,
    vs_sem,
    vr_sem,
):
    rows, width = x_v.shape
    half, quarter = width // 2, width // 4
    eighth = quarter // n_z
    tiles = rows // TILE
    ahead = stream.shape[0]
    wide, narrow = lax.axis_index("wide"), lax.axis_index("narrow")
    z, x = wide // n_x, lax.rem(wide, n_x)
    y, c = narrow // 2, lax.rem(narrow, 2)
    core = (wide, y * 2 + 1 - c)
    near_x = (z * n_x + 1 - x, narrow)
    near_y = (wide, (1 - y) * 2 + c)
    one = tuple(jnp.where(c == 0, a, b) for a, b in zip(near_x, near_y))
    two = tuple(jnp.where(c == 0, b, a) for a, b in zip(near_x, near_y))
    h1 = jnp.where(c == 0, x, y)
    h2 = jnp.where(c == 0, y, x)
    others = [lax.rem(z + k, n_z) for k in range(1, n_z)]
    along_z = [(o * n_x + x, narrow) for o in others]

    if comm:
        barrier = pltpu.get_barrier_semaphore()
        for device in [core, near_x, near_y] + along_z:
            pl.semaphore_signal(barrier, inc=1, device_id=device, device_id_type=MESH)

    def stream_load(j):
        src = act_hbm if j < 4 else hidden_grad_hbm
        return pltpu.make_async_copy(
            src.at[:, pl.ds((j % 4) * width, width)], stream.at[j % ahead], in_sem.at[j]
        )

    resident = [
        pltpu.make_async_copy(src, dst, in_sem.at[8 + k])
        for k, (src, dst) in enumerate(
            (
                (ffn_grad_hbm, ffn_grad_v),
                (mixed_hbm, mixed_v),
                (pre_grad_hbm, pre_v),
                (w_out_hbm, w_out),
                (qkv_hbm, qkv_v),
                (w_qkv_hbm, w_qkv),
                (context_hbm, context_v),
                (x_hbm, x_v),
            )
        )
    ]
    stream_load(0).start()
    resident[0].start()
    for j in range(1, ahead):
        stream_load(j).start()
    for copy in resident[1:]:
        copy.start()
    vbuf[0] = vec_ref[...]
    waited = set()

    def need(*which):
        for k in which:
            if k not in waited:
                waited.add(k)
                resident[k].wait()

    first, low_one, low_two = head_halves()
    lanes = 2 * HEAD_DIM

    def weight_block(b):
        if b < 8:
            stream_load(b).wait()
        if b < 4:
            need(0)
            left, right = stream.at[b % ahead], ffn_grad_v
        elif b < 8:
            need(1)
            left, right = mixed_v, stream.at[b % ahead]
        elif b < 9:
            need(6)
            left, right = context_v, attn_v
        else:
            need(7)
            left, right = x_v, qkv_v.at[:, pl.ds((b - 9) * width, width)]

        def step(i, carry):
            at = pl.ds(pl.multiple_of(i * TILE, TILE), TILE)
            part[b, at, :] = dot_left_t(left[:, at], right[...]).astype(bf16)
            return carry

        lax.fori_loop(0, width // TILE, step, 0, unroll=True)
        if b + ahead < 8:
            stream_load(b + ahead).start()

    def grad_in_store(tile):
        at = pl.ds(tile * TILE, TILE)
        return pltpu.make_async_copy(pre_v.at[at, :], grad_in_hbm.at[at, :], out_sem.at[tile])

    def attend_tile(tile, piece):
        need(2, 3, 4, 5)
        at = pl.ds(tile * TILE, TILE)
        if piece == 0:
            attn_grad = pre_v[at, :].astype(bf16)
            attn_v[at, :] = attn_grad
            context_grad_v[...] = dot_right_t(attn_grad, w_out[...]).astype(bf16)
        if piece == 2:
            vbuf[0, 0:1, :] += col_sum(qkv_v[at, 0:width].astype(f32))
            vbuf[0, 1:2, :] += col_sum(qkv_v[at, 2 * width : 3 * width].astype(f32))
            pre_v[at, :] += dot_right_t(qkv_v[at, :], w_qkv[...])
            grad_in_store(tile).start()
            return

        def pair_step(pair):
            q_at, k_at, v_at = (pl.ds(third * width + pair * lanes, lanes) for third in range(3))
            for span in range(TILE // SPAN_LEN):
                sp = pl.ds(tile * TILE + span * SPAN_LEN, SPAN_LEN)
                queries, keys_low, values_low = qkv_v[sp, q_at], qkv_v[sp, k_at], qkv_v[sp, v_at]
                upper = context_grad_v[pl.ds(span * SPAN_LEN, SPAN_LEN), q_at]
                stacked = jnp.concatenate([queries * low_one, queries * low_two], axis=0)
                stacked_up = jnp.concatenate([upper * low_one, upper * low_two], axis=0)
                scores = dot_right_t(keys_low, stacked)
                shifted = jnp.exp((scores - jnp.max(scores, axis=0, keepdims=True)) * head_scale)
                probs = shifted * (1.0 / col_sum(shifted))
                value_grad = dot(probs.astype(bf16), stacked_up)
                prob_grad = dot_right_t(values_low, stacked_up)
                score_grad = (probs * (prob_grad - col_sum(probs * prob_grad))).astype(bf16)
                query_grad = dot_left_t(score_grad, keys_low) * head_scale
                key_grad = dot(score_grad, stacked) * head_scale
                qkv_v[sp, q_at] = jnp.where(
                    first, query_grad[:SPAN_LEN], query_grad[SPAN_LEN:]
                ).astype(bf16)
                qkv_v[sp, k_at] = key_grad.astype(bf16)
                qkv_v[sp, v_at] = value_grad.astype(bf16)

        pairs = width // lanes
        for pair in range(pairs // 2) if piece == 0 else range(pairs // 2, pairs):
            pair_step(pair)

    def out_at(t, row, count):
        if t < 2:
            at = pl.multiple_of((2 * t + c) * width + row, 16)
            return o_ffo.at[pl.ds(at, count), :]
        cols = pl.multiple_of((2 * (t - 2) + c) * width, 128)
        return o_rest.at[pl.ds(pl.multiple_of(row, 16), count), pl.ds(cols, width)]

    def part_at(t, row, count):
        return part.at[2 * t + c, pl.ds(pl.multiple_of(row, 16), count), :]

    keep1 = h1 * half
    keep2 = keep1 + h2 * quarter
    own = keep2 + z * eighth

    def send(src, dst, stage, t, device):
        return pltpu.make_async_remote_copy(
            src, dst, s_sem.at[stage, t], r_sem.at[stage, t], device_id=device, device_id_type=MESH
        )

    def send_z(src, dst, stage, t, k):
        return pltpu.make_async_remote_copy(
            src,
            dst,
            zs_sem.at[stage, t, k],
            zr_sem.at[stage, t, k],
            device_id=along_z[k],
            device_id_type=MESH,
        )

    def sibling_slot(t, of):
        return sib.at[t] if t < 2 else part.at[2 * (t - 2) + 1 - of]

    def copies(stage, t):
        if stage == 0:
            return [send(part.at[2 * t + 1 - c], sibling_slot(t, 1 - c), 0, t, core)]
        if stage == 1:
            return [send(part_at(t, (1 - h1) * half, half), r1.at[t], 1, t, one)]
        if stage == 2:
            return [send(part_at(t, keep1 + (1 - h2) * quarter, quarter), r2.at[t], 2, t, two)]
        if stage == 3:
            return [
                send_z(part_at(t, keep2 + o * eighth, eighth), r3.at[t, k], 0, t, k)
                for k, o in enumerate(others)
            ]
        if stage == 4:
            return [
                send_z(part_at(t, own, eighth), out_at(t, own, eighth), 1, t, k)
                for k in range(n_z - 1)
            ]
        if stage == 5:
            place = out_at(t, keep2, quarter)
            return [send(place, place, 3, t, two)]
        if stage == 6:
            place = out_at(t, keep1, half)
            return [send(place, place, 4, t, one)]
        place = out_at(t, 0, width)
        return [send(place, place, 5, t, core)]

    def add(t, row, count, got):
        def step(i, carry):
            at = pl.ds(pl.multiple_of(row + i * 48, 16), 48)
            here = part[2 * t + c, at, :].astype(f32) + got[
                pl.ds(pl.multiple_of(i * 48, 16), 48), :
            ].astype(f32)
            part[2 * t + c, at, :] = here.astype(bf16)
            return carry

        lax.fori_loop(0, count // 48, step, 0)

    def own_store(t):
        return pltpu.make_async_copy(
            part_at(t, own, eighth), out_at(t, own, eighth), out_sem.at[tiles + t]
        )

    def advance(stage, t):
        if stage > 0:
            for copy in copies(stage - 1, t):
                copy.wait()
        if stage == 1:
            add(t, 0, width, sibling_slot(t, c))
        elif stage == 2:
            add(t, keep1, half, r1.at[t])
        elif stage == 3:
            add(t, keep2, quarter, r2.at[t])
        elif stage == 4:
            total = part_at(t, own, eighth)[...].astype(f32)
            for k in range(n_z - 1):
                total = total + r3[t, k].astype(f32)
            part_at(t, own, eighth)[...] = total.astype(bf16)
            own_store(t).start()
        elif stage == 5:
            own_store(t).wait()
        if stage < 8:
            for copy in copies(stage, t):
                copy.start()

    def vector_copies(k):
        if k < 3:
            device = (core, near_x, near_y)[k]
            ends = [(vbuf.at[2 * k], vbuf.at[2 * k + 1], k, device)]
        else:
            ends = [(vbuf.at[6], vbuf.at[7 + i], 3 + i, d) for i, d in enumerate(along_z)]
        return [
            pltpu.make_async_remote_copy(
                src, dst, vs_sem.at[s], vr_sem.at[s], device_id=d, device_id_type=MESH
            )
            for src, dst, s, d in ends
        ]

    def vector_step(k):
        if k > 0:
            for copy in vector_copies(k - 1):
                copy.wait()
        if k in (1, 2, 3):
            vbuf[2 * k] = vbuf[2 * k - 2] + vbuf[2 * k - 1]
        if k < 4:
            for copy in vector_copies(k):
                copy.start()
        else:
            total = vbuf[6]
            for i in range(n_z - 1):
                total = total + vbuf[7 + i]
            o_vec[...] = total

    entered = False
    for kind, *at in order:
        if kind == "w":
            weight_block(*at)
        elif kind == "a":
            attend_tile(*at)
        elif comm:
            if not entered:
                pl.semaphore_wait(barrier, 2 + n_z)
                entered = True
            if kind == "s":
                advance(*at)
            else:
                vector_step(*at)
    if not comm:
        o_vec[...] = vbuf[0]
        locals_ = [
            pltpu.make_async_copy(
                part.at[b],
                o_ffo.at[pl.ds(b * width, width), :]
                if b < 4
                else o_rest.at[:, pl.ds((b - 4) * width, width)],
                in_sem.at[b],
            )
            for b in range(2 * TICKS)
        ]
        for copy in locals_:
            copy.start()
        for copy in locals_:
            copy.wait()
    for tile in range(tiles):
        grad_in_store(tile).wait()


def schedule():
    return [
        ("w", 0), ("w", 1), ("s", 0, 0), ("w", 2), ("w", 3), ("s", 1, 0), ("s", 0, 1), ("w", 4),
        ("w", 5), ("s", 1, 1), ("s", 0, 2), ("w", 6), ("w", 7), ("s", 2, 0), ("s", 1, 2),
        ("s", 0, 3), ("a", 0, 0), ("s", 1, 3), ("a", 0, 1), ("a", 0, 2), ("a", 1, 0), ("s", 3, 0),
        ("s", 2, 1), ("a", 1, 1), ("a", 1, 2), ("a", 2, 0), ("a", 2, 1), ("s", 4, 0), ("s", 2, 2),
        ("a", 2, 2), ("s", 3, 1), ("s", 2, 3), ("a", 3, 0), ("a", 3, 1), ("s", 3, 2), ("a", 3, 2),
        ("s", 3, 3), ("v", 0), ("w", 8), ("w", 9), ("s", 0, 4), ("s", 5, 0), ("v", 1), ("w", 10),
        ("w", 11), ("s", 1, 4), ("s", 6, 0), ("v", 2), ("s", 0, 5), ("s", 4, 1), ("s", 1, 5),
        ("s", 4, 2), ("v", 3), ("s", 4, 3), ("s", 2, 4), ("s", 7, 0), ("s", 5, 1), ("v", 4),
        ("s", 2, 5), ("s", 8, 0), ("s", 5, 2), ("s", 5, 3), ("s", 3, 4), ("s", 6, 1), ("s", 3, 5),
        ("s", 4, 4), ("s", 6, 2), ("s", 6, 3), ("s", 4, 5), ("s", 7, 1), ("s", 5, 4), ("s", 8, 1),
        ("s", 5, 5), ("s", 7, 2), ("s", 7, 3), ("s", 6, 4), ("s", 8, 2), ("s", 8, 3), ("s", 6, 5),
        ("s", 7, 4), ("s", 7, 5), ("s", 8, 4), ("s", 8, 5),
    ]


def attend_back(act, hidden_grad, ffn_grad, mixed_low, pre_grad, context, qkv, x, w_out, w_qkv, vectors, sizes, order=None):
    rows, width = x.shape
    inner = act.shape[1]
    n_z, n_x, n_y = sizes
    comm = n_x == 2 and n_y == 2 and width % (64 * n_z) == 0
    hbm = pl.BlockSpec(memory_space=pl.ANY)
    vmem = pl.BlockSpec(memory_space=pltpu.VMEM)
    shape = jax.ShapeDtypeStruct
    tiles = rows // TILE
    scratch = [
        pltpu.VMEM((4, rows, width), bf16),
        pltpu.VMEM((rows, width), bf16),
        pltpu.VMEM((rows, width), bf16),
        pltpu.VMEM((rows, width), f32),
        pltpu.VMEM((rows, width), bf16),
        pltpu.VMEM((rows, 3 * width), bf16),
        pltpu.VMEM((rows, width), bf16),
        pltpu.VMEM((width, width), bf16),
        pltpu.VMEM((width, 3 * width), bf16),
        pltpu.VMEM((rows, width), bf16),
        pltpu.VMEM((TILE, width), bf16),
        pltpu.VMEM((2 * TICKS, width, width), bf16),
        pltpu.VMEM((2, width, width), bf16),
        pltpu.VMEM((TICKS, width // 2, width), bf16),
        pltpu.VMEM((TICKS, width // 4, width), bf16),
        pltpu.VMEM((TICKS, n_z - 1, width // 4 // n_z, width), bf16),
        pltpu.VMEM((6 + n_z,) + vectors.shape, f32),
        pltpu.SemaphoreType.DMA((16,)),
        pltpu.SemaphoreType.DMA((tiles + TICKS,)),
        pltpu.SemaphoreType.DMA((6, TICKS)),
        pltpu.SemaphoreType.DMA((6, TICKS)),
        pltpu.SemaphoreType.DMA((2, TICKS, n_z - 1)),
        pltpu.SemaphoreType.DMA((2, TICKS, n_z - 1)),
        pltpu.SemaphoreType.DMA((2 + n_z,)),
        pltpu.SemaphoreType.DMA((2 + n_z,)),
    ]
    params = dict(vmem_limit_bytes=60 * MIB)
    if comm:
        params.update(collective_id=0, has_side_effects=True)
    g_ffo, rest, grad_in, vectors = pl.pallas_call(
        functools.partial(attend_back_kernel, n_z, n_x, comm, order or schedule()),
        out_shape=(
            shape((inner, width), bf16),
            shape((width, inner + 4 * width), bf16),
            shape((rows, width), f32),
            shape(vectors.shape, f32),
        ),
        in_specs=[hbm] * 10 + [vmem],
        out_specs=(hbm, hbm, hbm, vmem),
        scratch_shapes=scratch,
        compiler_params=pltpu.CompilerParams(**params),
        name="attend_back_and_sums",
    )(act, hidden_grad, ffn_grad, mixed_low, pre_grad, context, qkv, x, w_out, w_qkv, vectors)
    if not comm:
        g_ffo, rest, vectors = lax.psum((g_ffo, rest, vectors), ("wide", "narrow"))
    return g_ffo, rest, grad_in, vectors


def widen_kernel(ffo_ref, rest_ref, vec_ref, losses_ref, w_ffo, w_in, w_out, w_qkv, span_loss, loss, b_in, *vectors):
    inner, width = w_in.shape[1], w_out.shape[1]
    w_ffo[...] = ffo_ref[...].astype(f32)
    w_in[...] = rest_ref[:, :inner].astype(f32)
    w_out[...] = rest_ref[:, inner : inner + width].astype(f32)
    w_qkv[...] = rest_ref[:, inner + width :].astype(f32)

    @pl.when(pl.program_id(0) == 0)
    def _():
        count = span_loss.shape[0]
        span_loss[...] = losses_ref[:, :count].reshape(count)
        loss[...] = losses_ref[:, count : count + 1].reshape(1)
        for k, vector in enumerate(vectors):
            vector[...] = vec_ref[k : k + 1, :].reshape(vector.shape)
        for j in range(inner // width):
            at = 8 + j
            b_in[pl.ds(j * width, width)] = vec_ref[at : at + 1, :].reshape(width)


def widen(ffo, rest, vectors, losses, span_count):
    inner, width = ffo.shape
    steps = 4
    shape = jax.ShapeDtypeStruct

    def tiles(rows, cols):
        return pl.BlockSpec((rows // steps, cols), lambda i: (i, 0))

    def whole(*sizes):
        return pl.BlockSpec(sizes, lambda i: (0,) * len(sizes))

    flat = [span_count, 1, inner] + [width] * 8
    return pl.pallas_call(
        widen_kernel,
        grid=(steps,),
        out_shape=(
            shape((inner, width), f32),
            shape((width, inner), f32),
            shape((width, width), f32),
            shape((width, 3 * width), f32),
            *(shape((n,), f32) for n in flat),
        ),
        in_specs=[
            tiles(inner, width),
            tiles(width, rest.shape[1]),
            whole(*vectors.shape),
            whole(*losses.shape),
        ],
        out_specs=(
            tiles(inner, width),
            tiles(width, inner),
            tiles(width, width),
            tiles(width, 3 * width),
            *(whole(n) for n in flat),
        ),
        compiler_params=pltpu.CompilerParams(vmem_limit_bytes=60 * MIB),
        name="widen",
    )(ffo, rest, vectors, losses)


def mesh_sizes():
    n_wide, n_narrow = lax.axis_size("wide"), lax.axis_size("narrow")
    n_y = n_narrow // 2
    n_x = n_y if n_wide % n_y == 0 else 1
    return n_wide // n_x, n_x, n_y


def per_device(
    hidden_in,
    out_grad,
    w_qkv,
    b_query,
    b_value,
    w_out,
    b_out,
    ln1_gain,
    ln1_bias,
    w_in,
    b_in,
    w_ff_out,
    b_ff_out,
    ln2_gain,
    ln2_bias,
    doc_count,
    single_flag,
):
    rows, width = hidden_in.shape
    span_count = rows // SPAN_LEN
    sizes = mesh_sizes()

    qkv, context, block_out, mixed_low, act, ffn_grad, hidden_grad, pre_one_grad, vectors, losses = middle(
        hidden_in, w_qkv, w_out, w_in, w_ff_out, out_grad, b_query, b_value, b_out, b_in, b_ff_out,
        ln1_gain, ln1_bias, ln2_gain, ln2_bias, doc_count, single_flag, sizes,
    )
    g_ffo, rest, grad_in, vectors = attend_back(
        act, hidden_grad, ffn_grad, mixed_low, pre_one_grad, context, qkv, hidden_in, w_out, w_qkv,
        vectors, sizes,
    )
    g_ffo, g_in, g_out, g_qkv, span_loss, loss, g_b_in, *rest_grads = widen(
        g_ffo, rest, vectors, losses, span_count
    )
    g_b_query, g_b_value, g_b_out, g_gain_one, g_bias_one, g_b_ffo, g_gain_two, g_bias_two = rest_grads
    return (
        block_out,
        loss.reshape(()),
        span_loss,
        grad_in,
        g_qkv,
        g_b_query,
        g_b_value,
        g_out,
        g_b_out,
        g_gain_one,
        g_bias_one,
        g_in,
        g_b_in,
        g_ffo,
        g_b_ffo,
        g_gain_two,
        g_bias_two,
    )


def solution(mesh):
    placed = (
        P(("wide", "narrow"), None),
        P(("wide", "narrow"), None),
        P(),
        P(),
        P(),
        P(),
        P(),
        P(),
        P(),
        P(),
        P(),
        P(),
        P(),
        P(),
        P(),
        P(),
        P(),
    )
    return jax.shard_map(
        per_device,
        mesh=mesh,
        in_specs=placed,
        out_specs=(
            P(("wide", "narrow"), None),
            P(),
            P(("wide", "narrow")),
            P(("wide", "narrow"), None),
            P(),
            P(),
            P(),
            P(),
            P(),
            P(),
            P(),
            P(),
            P(),
            P(),
            P(),
            P(),
            P(),
        ),
        check_vma=False,
    )
```

```python
import functools

import jax
import jax.numpy as jnp
from jax import lax
from jax.experimental import pallas as pl
from jax.experimental.pallas import tpu as pltpu
from jax.sharding import PartitionSpec as P

HEAD_DIM = 64
SPAN_LEN = 128
TILE = 256

ln_eps = 1e-06
score_scale = 0.2
far_low = -1000000000.0
head_scale = HEAD_DIM ** (-0.5)
MESH = pl.DeviceIdType.MESH
TICKS = 6
f32, bf16, i32 = jnp.float32, jnp.bfloat16, jnp.int32
MIB = 2**20


def dot(left, right):
    return jnp.dot(left, right, preferred_element_type=f32)


def dot_left_t(left, right):
    return lax.dot_general(left, right, (((0,), (0,)), ((), ())), preferred_element_type=f32)


def dot_right_t(left, right):
    return lax.dot_general(left, right, (((1,), (1,)), ((), ())), preferred_element_type=f32)


def row_mean(values):
    return jnp.mean(values, axis=1, keepdims=True)


def col_sum(values):
    return jnp.sum(values, axis=0, keepdims=True)


def norm_back(upstream, normed, scale, gain):
    scaled = upstream * gain
    return scale * (scaled - row_mean(scaled) - normed * row_mean(scaled * normed))


def head_halves():
    first = lax.broadcasted_iota(i32, (1, 2 * HEAD_DIM), 1) < HEAD_DIM
    return first, first.astype(bf16), jnp.logical_not(first).astype(bf16)


def pair_probs(stacked_queries, keys_low):
    scores = dot_right_t(stacked_queries, keys_low)
    shifted = jnp.exp((scores - jnp.max(scores, axis=1, keepdims=True)) * head_scale)
    return shifted * (1.0 / jnp.sum(shifted, axis=1, keepdims=True))


def attend_tile(at, x_ref, w_qkv_ref, b_query, b_value, w_out_ref, b_out, qkv_ref, context_ref, cent_ref):
    width = x_ref.shape[1]
    inputs = x_ref[at, :]
    for third in range(3):
        cols = pl.ds(third * width, width)
        packed = dot(inputs, w_qkv_ref[:, cols])
        if third == 0:
            packed = packed + b_query
        if third == 2:
            packed = packed + b_value
        qkv_ref[at, cols] = packed.astype(bf16)
    first, low_one, low_two = head_halves()
    lanes = 2 * HEAD_DIM
    for span in range(at.size // SPAN_LEN):
        sp = pl.ds(pl.multiple_of(at.start + span * SPAN_LEN, SPAN_LEN), SPAN_LEN)
        for pair in range(width // lanes):
            queries = qkv_ref[sp, pl.ds(pair * lanes, lanes)]
            keys_low = qkv_ref[sp, pl.ds(width + pair * lanes, lanes)]
            values_low = qkv_ref[sp, pl.ds(2 * width + pair * lanes, lanes)]
            stacked = jnp.concatenate([queries * low_one, queries * low_two], axis=0)
            mixed_values = dot(pair_probs(stacked, keys_low).astype(bf16), values_low)
            context_ref[sp, pl.ds(pair * lanes, lanes)] = jnp.where(
                first, mixed_values[:SPAN_LEN], mixed_values[SPAN_LEN:]
            ).astype(bf16)
    pre_one = inputs.astype(f32) + (dot(context_ref[at, :], w_out_ref[...]) + b_out)
    cent_ref[at, :] = pre_one - row_mean(pre_one)


def gelu_parts(values):
    cdf = 0.5 * (1.0 + lax.erf(values * 0.7071067811865476))
    pdf = 0.3989422804014327 * jnp.exp(-0.5 * values * values)
    return values * cdf, cdf + values * pdf


def contrast_rows(cls_low, count, flags, first, span_count):
    total, width = cls_low.shape
    slots, docsets = flags.shape
    block = min(total, 256)

    def layout(at):
        slot = at + lax.broadcasted_iota(i32, (block, 1), 0)
        device = slot // slots
        place = (slot - device * slots).astype(f32)
        member = lax.broadcasted_iota(i32, (block, docsets), 1) == device
        docs = jnp.sum(jnp.where(member, count, 0.0), axis=1, keepdims=True)
        single = dot_right_t(member.astype(bf16), flags.astype(bf16))
        doc = lax.broadcasted_iota(i32, (block, slots), 1).astype(f32)
        length = jnp.where(doc < docs, 2.0 - single, 0.0)
        earlier = lax.broadcasted_iota(i32, (slots, slots), 0) < lax.broadcasted_iota(
            i32, (slots, slots), 1
        )
        begins = dot(length.astype(bf16), earlier.astype(f32).astype(bf16))
        inside = (place >= begins) & (place < begins + length)
        double = inside & (length == 2.0)
        live = jnp.max(inside.astype(f32), axis=1, keepdims=True)
        pair = jnp.max(double.astype(f32), axis=1, keepdims=True)
        other = jnp.sum(jnp.where(double, 2.0 * begins + 1.0 - place, 0.0), axis=1, keepdims=True)
        mate = jnp.where(pair > 0.0, (device * slots).astype(f32) + other, slot.astype(f32))
        return slot.astype(f32), live, pair, mate

    eye = lax.broadcasted_iota(i32, (block, block), 0) == lax.broadcasted_iota(
        i32, (block, block), 1
    )
    live_row = jnp.concatenate(
        [col_sum(jnp.where(eye, layout(at)[1], 0.0)) for at in range(0, total, block)], axis=1
    )
    column = lax.broadcasted_iota(i32, (block, total), 1).astype(f32)
    pick_col = (
        lax.broadcasted_iota(i32, (span_count, total), 1)
        == first + lax.broadcasted_iota(i32, (span_count, total), 0)
    ).astype(f32).astype(bf16)
    rows_own = jnp.zeros((span_count, total), f32)
    upward = jnp.zeros((span_count, width), f32)
    own_loss = jnp.zeros((1, span_count), f32)
    loss = jnp.zeros((1, 1), f32)
    for at in range(0, total, block):
        slot, live, pair, mate = layout(at)
        cls_block = cls_low[at : at + block, :]
        sims = score_scale * dot_right_t(cls_block, cls_low)
        allowed = (live_row > 0.0) & (column != slot)
        masked = jnp.where(allowed, sims, far_low)
        top = jnp.max(masked, axis=1, keepdims=True)
        lse = top + jnp.log(jnp.sum(jnp.exp(masked - top), axis=1, keepdims=True))
        matches = column == mate
        positive = jnp.sum(jnp.where(matches, sims, 0.0), axis=1, keepdims=True)
        span_loss = jnp.where(pair > 0.0, lse - positive, 0.0)
        loss = loss + col_sum(span_loss)
        mine = at + lax.broadcasted_iota(i32, (block, span_count), 0) == (
            first + lax.broadcasted_iota(i32, (block, span_count), 1)
        )
        own_loss = own_loss + col_sum(jnp.where(mine, span_loss, 0.0))
        sim_grad = jnp.where(
            pair > 0.0, jnp.exp(masked - lse) - matches.astype(f32), 0.0
        ).astype(bf16)
        pick_row = (
            at + lax.broadcasted_iota(i32, (span_count, block), 1)
            == first + lax.broadcasted_iota(i32, (span_count, block), 0)
        ).astype(f32).astype(bf16)
        rows_own = rows_own + dot(pick_row, sim_grad)
        cols_own = dot_right_t(pick_col, sim_grad)
        upward = upward + dot(cols_own.astype(bf16), cls_block)
    upward = upward + dot(rows_own.astype(bf16), cls_low)
    return score_scale * upward, own_loss, loss


def middle_kernel(
    n_z,
    n_x,
    n_y,
    x_hbm,
    w_qkv_hbm,
    w_out_hbm,
    w_in_hbm,
    w_ffo_hbm,
    out_grad_hbm,
    b_query_ref,
    b_value_ref,
    b_out_ref,
    b_in_ref,
    b_ffo_ref,
    gain_one_ref,
    bias_one_ref,
    gain_two_ref,
    bias_two_ref,
    count_ref,
    flag_ref,
    qkv_hbm,
    context_hbm,
    block_hbm,
    mixed_hbm,
    act_hbm,
    ffn_grad_hbm,
    hidden_grad_hbm,
    pre_grad_hbm,
    vec_ref,
    losses_ref,
    x_v,
    w_qkv,
    w_out,
    qkv_v,
    context_v,
    cent_v,
    w_in,
    w_ffo,
    upper_v,
    block_v,
    mixed_v,
    act_v,
    slope_v,
    ffn_grad_v,
    two_v,
    first_v,
    cls_grad_v,
    b_in_v,
    cls_v,
    in_sem,
    out_sem,
    s_sem,
    r_sem,
):
    rows, width = cent_v.shape
    inner = w_in.shape[1]
    chunks = inner // width
    tiles = rows // TILE
    span_count = rows // SPAN_LEN
    wide, narrow = lax.axis_index("wide"), lax.axis_index("narrow")
    z, x = wide // n_x, lax.rem(wide, n_x)
    y, c = narrow // 2, lax.rem(narrow, 2)
    core = (wide, y * 2 + 1 - c)
    along_x = [(z * n_x + lax.rem(x + k, n_x), narrow) for k in range(1, n_x)]
    along_y = [(wide, lax.rem(y + k, n_y) * 2 + c) for k in range(1, n_y)]
    along_z = [(lax.rem(z + k, n_z) * n_x + x, narrow) for k in range(1, n_z)]
    partners = [core] + along_x + along_y + along_z

    barrier = pltpu.get_barrier_semaphore()
    for device in partners:
        pl.semaphore_signal(barrier, inc=1, device_id=device, device_id_type=MESH)

    loads = [
        pltpu.make_async_copy(src, dst, in_sem.at[k])
        for k, (src, dst) in enumerate(
            (
                (x_hbm, x_v),
                (w_qkv_hbm, w_qkv),
                (w_out_hbm, w_out),
                (w_in_hbm, w_in),
                (w_ffo_hbm, w_ffo),
                (out_grad_hbm, upper_v),
            )
        )
    ]
    for copy in loads:
        copy.start()

    def row(ref, at=0):
        return ref[pl.ds(at, width)].astype(f32).reshape(1, width)

    gain_one, bias_one, gain_two, bias_two, b_ffo = (
        row(r) for r in (gain_one_ref, bias_one_ref, gain_two_ref, bias_two_ref, b_ffo_ref)
    )
    for j in range(chunks):
        b_in_v[j : j + 1, :] = row(b_in_ref, j * width)

    def normed(cent):
        scale = lax.rsqrt(row_mean(cent * cent) + ln_eps)
        return cent * scale, scale

    def feed_forward(mixed, total, keep):
        mixed_low = mixed.astype(bf16)
        total[...] = mixed + b_ffo

        def step(j, carry):
            cols = pl.ds(pl.multiple_of(j * width, width), width)
            hidden = dot(mixed_low, w_in[:, cols]) + b_in_v[pl.ds(j, 1), :]
            act, slope = gelu_parts(hidden)
            act_low = act.astype(bf16)
            keep(cols, act_low, slope)
            total[...] += dot(act_low, w_ffo[cols, :])
            return carry

        lax.fori_loop(0, chunks, step, 0, unroll=True)
        pre_two = total[...]
        return pre_two - row_mean(pre_two)

    b_query, b_value, b_out = (row(r) for r in (b_query_ref, b_value_ref, b_out_ref))

    def store(src, dst, at, k):
        return pltpu.make_async_copy(src.at[at, :], dst.at[at, :], out_sem.at[k])

    def tile_rows(tile):
        return pl.ds(pl.multiple_of(tile * TILE, TILE), TILE)

    def attend_stores(tile):
        at = tile_rows(tile)
        return [
            store(qkv_v, qkv_hbm, at, 8 * tile + 6),
            store(context_v, context_hbm, at, 8 * tile + 7),
        ]

    def attend_step(tile, carry):
        attend_tile(
            tile_rows(tile), x_v, w_qkv, b_query, b_value, w_out, b_out, qkv_v, context_v, cent_v
        )
        for copy in attend_stores(tile):
            copy.start()
        return carry

    for copy in loads[:3]:
        copy.wait()
    lax.fori_loop(0, tiles, attend_step, 0)

    first_cent = jnp.concatenate(
        [cent_v[s * SPAN_LEN : s * SPAN_LEN + 1, :] for s in range(span_count)], axis=0
    )
    first_mixed = normed(first_cent)[0] * gain_one + bias_one
    loads[3].wait()
    loads[4].wait()
    first_two = feed_forward(first_mixed, first_v, lambda cols, act, slope: None)
    first_out = normed(first_two)[0] * gain_two + bias_two
    half = width // 2
    cls_v[z, x, y, c] = jnp.concatenate([first_out[:, :half], first_out[:, half:]], axis=0).astype(
        bf16
    )
    pl.semaphore_wait(barrier, len(partners))

    def gathers(stage):
        if stage == 0:
            ref, devices, base = cls_v.at[z, x, y, c], along_z, 0
        elif stage == 1:
            ref, devices, base = cls_v.at[:, x, y, c], along_x, n_z - 1
        elif stage == 2:
            ref, devices, base = cls_v.at[:, :, y, c], along_y, n_z + n_x - 2
        else:
            ref, devices, base = cls_v.at[:, :, :, c], [core], n_z + n_x + n_y - 3
        return [
            pltpu.make_async_remote_copy(
                ref, ref, s_sem.at[base + k], r_sem.at[base + k], device_id=d, device_id_type=MESH
            )
            for k, d in enumerate(devices)
        ]

    for copy in gathers(0):
        copy.start()
    loads[5].wait()

    def forward_stores(tile):
        at = tile_rows(tile)
        return [
            store(mixed_v, mixed_hbm, at, 8 * tile),
            store(block_v, block_hbm, at, 8 * tile + 1),
            store(act_v, act_hbm, at, 8 * tile + 2),
        ]

    def backward_stores(tile):
        at = tile_rows(tile)
        return [
            store(ffn_grad_v, ffn_grad_hbm, at, 8 * tile + 3),
            store(slope_v, hidden_grad_hbm, at, 8 * tile + 4),
            store(cent_v, pre_grad_hbm, at, 8 * tile + 5),
        ]

    def forward_tile(tile, carry):
        at = tile_rows(tile)
        mixed = normed(cent_v[at, :])[0] * gain_one + bias_one
        mixed_v[at, :] = mixed.astype(bf16)

        def keep(cols, act_low, slope):
            act_v[at, cols] = act_low
            slope_v[at, cols] = slope.astype(bf16)

        cent_two = feed_forward(mixed, two_v.at[at, :], keep)
        block_v[at, :] = (normed(cent_two)[0] * gain_two + bias_two).astype(bf16)
        two_v[at, :] = cent_two
        for copy in forward_stores(tile):
            copy.start()
        for stage in range(4):

            @pl.when(tile == min(stage, tiles - 1))
            def _():
                for copy in gathers(stage):
                    copy.wait()
                if stage < 3:
                    for copy in gathers(stage + 1):
                        copy.start()

        return carry

    lax.fori_loop(0, tiles, forward_tile, 0)

    low = cls_v[...].astype(f32).reshape(-1, 2 * span_count, half)
    cls_low = jnp.concatenate(
        [
            low[:, :span_count, :].reshape(-1, half),
            low[:, span_count:, :].reshape(-1, half),
        ],
        axis=1,
    ).astype(bf16)
    own = wide * (2 * n_y) + narrow
    cls_grad, own_loss, loss = contrast_rows(
        cls_low, count_ref[...].astype(f32).reshape(1, -1), flag_ref[...].astype(f32), own * span_count, span_count
    )
    cls_grad_v[...] = cls_grad
    lane = lax.broadcasted_iota(i32, losses_ref.shape, 1)
    losses_ref[...] = jnp.where(lane == span_count, loss, 0.0)
    losses_ref[:, :span_count] = own_loss

    vec_ref[...] = jnp.zeros(vec_ref.shape, f32)

    def add_row(k, values):
        vec_ref[pl.ds(k, 1), :] += col_sum(values)

    def backward_tile(tile, carry):
        at = tile_rows(tile)
        upper = upper_v[at, :].astype(f32)
        place = lax.broadcasted_iota(i32, (TILE, 1), 0)
        for span in range(TILE // SPAN_LEN):
            upper = jnp.where(
                place == span * SPAN_LEN,
                cls_grad_v[pl.ds(tile * (TILE // SPAN_LEN) + span, 1), :],
                upper,
            )
        normed_two, scale_two = normed(two_v[at, :])
        add_row(6, upper * normed_two)
        add_row(7, upper)
        pre_two_grad = norm_back(upper, normed_two, scale_two, gain_two)
        ffn_grad = pre_two_grad.astype(bf16)
        ffn_grad_v[at, :] = ffn_grad
        add_row(5, ffn_grad.astype(f32))
        two_v[at, :] = pre_two_grad

        def step(j, inner_carry):
            cols = pl.ds(pl.multiple_of(j * width, width), width)
            back = dot_right_t(ffn_grad, w_ffo[cols, :]) * slope_v[at, cols].astype(f32)
            hidden_grad = back.astype(bf16)
            slope_v[at, cols] = hidden_grad
            add_row(8 + j, hidden_grad.astype(f32))
            two_v[at, :] += dot_right_t(hidden_grad, w_in[:, cols])
            return inner_carry

        lax.fori_loop(0, chunks, step, 0, unroll=True)
        mixed_grad = two_v[at, :]
        normed_one, scale_one = normed(cent_v[at, :])
        add_row(3, mixed_grad * normed_one)
        add_row(4, mixed_grad)
        pre_one_grad = norm_back(mixed_grad, normed_one, scale_one, gain_one)
        cent_v[at, :] = pre_one_grad
        add_row(2, pre_one_grad.astype(bf16).astype(f32))
        for copy in backward_stores(tile):
            copy.start()
        return carry

    lax.fori_loop(0, tiles, backward_tile, 0)

    for tile in range(tiles):
        for copy in attend_stores(tile) + forward_stores(tile) + backward_stores(tile):
            copy.wait()


def middle(
    x,
    w_qkv,
    w_out,
    w_in,
    w_ffo,
    out_grad,
    b_query,
    b_value,
    b_out,
    b_in,
    b_ffo,
    gain_one,
    bias_one,
    gain_two,
    bias_two,
    doc_count,
    single_flag,
    sizes,
):
    rows, width = x.shape
    inner = w_in.shape[1]
    span_count = rows // SPAN_LEN
    n_z, n_x, n_y = sizes
    moves = n_z + n_x + n_y - 2
    hbm = pl.BlockSpec(memory_space=pl.ANY)
    vmem = pl.BlockSpec(memory_space=pltpu.VMEM)
    shape = jax.ShapeDtypeStruct
    return pl.pallas_call(
        functools.partial(middle_kernel, n_z, n_x, n_y),
        out_shape=(
            shape((rows, 3 * width), bf16),
            shape((rows, width), bf16),
            shape((rows, width), bf16),
            shape((rows, width), bf16),
            shape((rows, inner), bf16),
            shape((rows, width), bf16),
            shape((rows, inner), bf16),
            shape((rows, width), f32),
            shape((16, width), f32),
            shape((1, 128), f32),
        ),
        in_specs=[hbm] * 6 + [vmem] * 11,
        out_specs=(hbm,) * 8 + (vmem,) * 2,
        scratch_shapes=[
            pltpu.VMEM((rows, width), bf16),
            pltpu.VMEM((width, 3 * width), bf16),
            pltpu.VMEM((width, width), bf16),
            pltpu.VMEM((rows, 3 * width), bf16),
            pltpu.VMEM((rows, width), bf16),
            pltpu.VMEM((rows, width), f32),
            pltpu.VMEM((width, inner), bf16),
            pltpu.VMEM((inner, width), bf16),
            pltpu.VMEM((rows, width), bf16),
            pltpu.VMEM((rows, width), bf16),
            pltpu.VMEM((rows, width), bf16),
            pltpu.VMEM((rows, inner), bf16),
            pltpu.VMEM((rows, inner), bf16),
            pltpu.VMEM((rows, width), bf16),
            pltpu.VMEM((rows, width), f32),
            pltpu.VMEM((span_count, width), f32),
            pltpu.VMEM((span_count, width), f32),
            pltpu.VMEM((inner // width, width), f32),
            pltpu.VMEM((n_z, n_x, n_y, 2, 2 * span_count, width // 2), bf16),
            pltpu.SemaphoreType.DMA((6,)),
            pltpu.SemaphoreType.DMA((8 * (rows // TILE),)),
            pltpu.SemaphoreType.DMA((moves,)),
            pltpu.SemaphoreType.DMA((moves,)),
        ],
        compiler_params=pltpu.CompilerParams(
            collective_id=1, has_side_effects=True, vmem_limit_bytes=60 * MIB
        ),
        name="forward_and_loss",
    )(
        x, w_qkv, w_out, w_in, w_ffo, out_grad, b_query, b_value, b_out, b_in, b_ffo, gain_one, bias_one,
        gain_two, bias_two, doc_count, single_flag.T,
    )


def attend_back_kernel(
    n_z,
    n_x,
    comm,
    order,
    act_hbm,
    hidden_grad_hbm,
    ffn_grad_hbm,
    mixed_hbm,
    pre_grad_hbm,
    context_hbm,
    qkv_hbm,
    x_hbm,
    w_out_hbm,
    w_qkv_hbm,
    vec_ref,
    o_ffo,
    o_rest,
    grad_in_hbm,
    o_vec,
    stream,
    ffn_grad_v,
    mixed_v,
    pre_v,
    context_v,
    qkv_v,
    x_v,
    w_out,
    w_qkv,
    attn_v,
    context_grad_v,
    part,
    sib,
    r1,
    r2,
    r3,
    vbuf,
    in_sem,
    out_sem,
    s_sem,
    r_sem,
    zs_sem,
    zr_sem,
    vs_sem,
    vr_sem,
):
    rows, width = x_v.shape
    half, quarter = width // 2, width // 4
    eighth = quarter // n_z
    tiles = rows // TILE
    ahead = stream.shape[0]
    wide, narrow = lax.axis_index("wide"), lax.axis_index("narrow")
    z, x = wide // n_x, lax.rem(wide, n_x)
    y, c = narrow // 2, lax.rem(narrow, 2)
    core = (wide, y * 2 + 1 - c)
    near_x = (z * n_x + 1 - x, narrow)
    near_y = (wide, (1 - y) * 2 + c)
    one = tuple(jnp.where(c == 0, a, b) for a, b in zip(near_x, near_y))
    two = tuple(jnp.where(c == 0, b, a) for a, b in zip(near_x, near_y))
    h1 = jnp.where(c == 0, x, y)
    h2 = jnp.where(c == 0, y, x)
    others = [lax.rem(z + k, n_z) for k in range(1, n_z)]
    along_z = [(o * n_x + x, narrow) for o in others]

    if comm:
        barrier = pltpu.get_barrier_semaphore()
        for device in [core, near_x, near_y] + along_z:
            pl.semaphore_signal(barrier, inc=1, device_id=device, device_id_type=MESH)

    def stream_load(j):
        src = act_hbm if j < 4 else hidden_grad_hbm
        return pltpu.make_async_copy(
            src.at[:, pl.ds((j % 4) * width, width)], stream.at[j % ahead], in_sem.at[j]
        )

    resident = [
        pltpu.make_async_copy(src, dst, in_sem.at[8 + k])
        for k, (src, dst) in enumerate(
            (
                (ffn_grad_hbm, ffn_grad_v),
                (mixed_hbm, mixed_v),
                (pre_grad_hbm, pre_v),
                (w_out_hbm, w_out),
                (qkv_hbm, qkv_v),
                (w_qkv_hbm, w_qkv),
                (context_hbm, context_v),
                (x_hbm, x_v),
            )
        )
    ]
    stream_load(0).start()
    resident[0].start()
    for j in range(1, ahead):
        stream_load(j).start()
    for copy in resident[1:]:
        copy.start()
    vbuf[0] = vec_ref[...]
    waited = set()

    def need(*which):
        for k in which:
            if k not in waited:
                waited.add(k)
                resident[k].wait()

    first, low_one, low_two = head_halves()
    lanes = 2 * HEAD_DIM

    def weight_block(b):
        if b < 8:
            stream_load(b).wait()
        if b < 4:
            need(0)
            left, right = stream.at[b % ahead], ffn_grad_v
        elif b < 8:
            need(1)
            left, right = mixed_v, stream.at[b % ahead]
        elif b < 9:
            need(6)
            left, right = context_v, attn_v
        else:
            need(7)
            left, right = x_v, qkv_v.at[:, pl.ds((b - 9) * width, width)]

        def step(i, carry):
            at = pl.ds(pl.multiple_of(i * TILE, TILE), TILE)
            part[b, at, :] = dot_left_t(left[:, at], right[...]).astype(bf16)
            return carry

        lax.fori_loop(0, width // TILE, step, 0, unroll=True)
        if b + ahead < 8:
            stream_load(b + ahead).start()

    def grad_in_store(tile):
        at = pl.ds(tile * TILE, TILE)
        return pltpu.make_async_copy(pre_v.at[at, :], grad_in_hbm.at[at, :], out_sem.at[tile])

    def attend_tile(tile, piece):
        need(2, 3, 4, 5)
        at = pl.ds(tile * TILE, TILE)
        if piece == 0:
            attn_grad = pre_v[at, :].astype(bf16)
            attn_v[at, :] = attn_grad
            context_grad_v[...] = dot_right_t(attn_grad, w_out[...]).astype(bf16)
        if piece == 2:
            vbuf[0, 0:1, :] += col_sum(qkv_v[at, 0:width].astype(f32))
            vbuf[0, 1:2, :] += col_sum(qkv_v[at, 2 * width : 3 * width].astype(f32))
            pre_v[at, :] += dot_right_t(qkv_v[at, :], w_qkv[...])
            grad_in_store(tile).start()
            return

        def pair_step(pair):
            q_at, k_at, v_at = (pl.ds(third * width + pair * lanes, lanes) for third in range(3))
            for span in range(TILE // SPAN_LEN):
                sp = pl.ds(tile * TILE + span * SPAN_LEN, SPAN_LEN)
                queries, keys_low, values_low = qkv_v[sp, q_at], qkv_v[sp, k_at], qkv_v[sp, v_at]
                upper = context_grad_v[pl.ds(span * SPAN_LEN, SPAN_LEN), q_at]
                stacked = jnp.concatenate([queries * low_one, queries * low_two], axis=0)
                stacked_up = jnp.concatenate([upper * low_one, upper * low_two], axis=0)
                scores = dot_right_t(keys_low, stacked)
                shifted = jnp.exp((scores - jnp.max(scores, axis=0, keepdims=True)) * head_scale)
                probs = shifted * (1.0 / col_sum(shifted))
                value_grad = dot(probs.astype(bf16), stacked_up)
                prob_grad = dot_right_t(values_low, stacked_up)
                score_grad = (probs * (prob_grad - col_sum(probs * prob_grad))).astype(bf16)
                query_grad = dot_left_t(score_grad, keys_low) * head_scale
                key_grad = dot(score_grad, stacked) * head_scale
                qkv_v[sp, q_at] = jnp.where(
                    first, query_grad[:SPAN_LEN], query_grad[SPAN_LEN:]
                ).astype(bf16)
                qkv_v[sp, k_at] = key_grad.astype(bf16)
                qkv_v[sp, v_at] = value_grad.astype(bf16)

        pairs = width // lanes
        for pair in range(pairs // 2) if piece == 0 else range(pairs // 2, pairs):
            pair_step(pair)

    def out_at(t, row, count):
        if t < 2:
            at = pl.multiple_of((2 * t + c) * width + row, 16)
            return o_ffo.at[pl.ds(at, count), :]
        cols = pl.multiple_of((2 * (t - 2) + c) * width, 128)
        return o_rest.at[pl.ds(pl.multiple_of(row, 16), count), pl.ds(cols, width)]

    def part_at(t, row, count):
        return part.at[2 * t + c, pl.ds(pl.multiple_of(row, 16), count), :]

    keep1 = h1 * half
    keep2 = keep1 + h2 * quarter
    own = keep2 + z * eighth

    def send(src, dst, stage, t, device):
        return pltpu.make_async_remote_copy(
            src, dst, s_sem.at[stage, t], r_sem.at[stage, t], device_id=device, device_id_type=MESH
        )

    def send_z(src, dst, stage, t, k):
        return pltpu.make_async_remote_copy(
            src,
            dst,
            zs_sem.at[stage, t, k],
            zr_sem.at[stage, t, k],
            device_id=along_z[k],
            device_id_type=MESH,
        )

    def sibling_slot(t, of):
        return sib.at[t] if t < 2 else part.at[2 * (t - 2) + 1 - of]

    def copies(stage, t):
        if stage == 0:
            return [send(part.at[2 * t + 1 - c], sibling_slot(t, 1 - c), 0, t, core)]
        if stage == 1:
            return [send(part_at(t, (1 - h1) * half, half), r1.at[t], 1, t, one)]
        if stage == 2:
            return [send(part_at(t, keep1 + (1 - h2) * quarter, quarter), r2.at[t], 2, t, two)]
        if stage == 3:
            return [
                send_z(part_at(t, keep2 + o * eighth, eighth), r3.at[t, k], 0, t, k)
                for k, o in enumerate(others)
            ]
        if stage == 4:
            return [
                send_z(part_at(t, own, eighth), out_at(t, own, eighth), 1, t, k)
                for k in range(n_z - 1)
            ]
        if stage == 5:
            place = out_at(t, keep2, quarter)
            return [send(place, place, 3, t, two)]
        if stage == 6:
            place = out_at(t, keep1, half)
            return [send(place, place, 4, t, one)]
        place = out_at(t, 0, width)
        return [send(place, place, 5, t, core)]

    def add(t, row, count, got):
        def step(i, carry):
            at = pl.ds(pl.multiple_of(row + i * 48, 16), 48)
            here = part[2 * t + c, at, :].astype(f32) + got[
                pl.ds(pl.multiple_of(i * 48, 16), 48), :
            ].astype(f32)
            part[2 * t + c, at, :] = here.astype(bf16)
            return carry

        lax.fori_loop(0, count // 48, step, 0)

    def own_store(t):
        return pltpu.make_async_copy(
            part_at(t, own, eighth), out_at(t, own, eighth), out_sem.at[tiles + t]
        )

    def advance(stage, t):
        if stage > 0:
            for copy in copies(stage - 1, t):
                copy.wait()
        if stage == 1:
            add(t, 0, width, sibling_slot(t, c))
        elif stage == 2:
            add(t, keep1, half, r1.at[t])
        elif stage == 3:
            add(t, keep2, quarter, r2.at[t])
        elif stage == 4:
            total = part_at(t, own, eighth)[...].astype(f32)
            for k in range(n_z - 1):
                total = total + r3[t, k].astype(f32)
            part_at(t, own, eighth)[...] = total.astype(bf16)
            own_store(t).start()
        elif stage == 5:
            own_store(t).wait()
        if stage < 8:
            for copy in copies(stage, t):
                copy.start()

    def vector_copies(k):
        if k < 3:
            device = (core, near_x, near_y)[k]
            ends = [(vbuf.at[2 * k], vbuf.at[2 * k + 1], k, device)]
        else:
            ends = [(vbuf.at[6], vbuf.at[7 + i], 3 + i, d) for i, d in enumerate(along_z)]
        return [
            pltpu.make_async_remote_copy(
                src, dst, vs_sem.at[s], vr_sem.at[s], device_id=d, device_id_type=MESH
            )
            for src, dst, s, d in ends
        ]

    def vector_step(k):
        if k > 0:
            for copy in vector_copies(k - 1):
                copy.wait()
        if k in (1, 2, 3):
            vbuf[2 * k] = vbuf[2 * k - 2] + vbuf[2 * k - 1]
        if k < 4:
            for copy in vector_copies(k):
                copy.start()
        else:
            total = vbuf[6]
            for i in range(n_z - 1):
                total = total + vbuf[7 + i]
            o_vec[...] = total

    entered = False
    for kind, *at in order:
        if kind == "w":
            weight_block(*at)
        elif kind == "a":
            attend_tile(*at)
        elif comm:
            if not entered:
                pl.semaphore_wait(barrier, 2 + n_z)
                entered = True
            if kind == "s":
                advance(*at)
            else:
                vector_step(*at)
    if not comm:
        o_vec[...] = vbuf[0]
        locals_ = [
            pltpu.make_async_copy(
                part.at[b],
                o_ffo.at[pl.ds(b * width, width), :]
                if b < 4
                else o_rest.at[:, pl.ds((b - 4) * width, width)],
                in_sem.at[b],
            )
            for b in range(2 * TICKS)
        ]
        for copy in locals_:
            copy.start()
        for copy in locals_:
            copy.wait()
    for tile in range(tiles):
        grad_in_store(tile).wait()


def schedule():
    return [
        ("w", 0), ("w", 1), ("s", 0, 0), ("w", 2), ("s", 1, 0), ("w", 3), ("s", 0, 1), ("w", 4),
        ("s", 1, 1), ("w", 5), ("s", 0, 2), ("s", 2, 0), ("w", 6), ("s", 1, 2), ("w", 7),
        ("s", 0, 3), ("a", 0, 0), ("s", 1, 3), ("s", 3, 0), ("s", 2, 1), ("a", 0, 1), ("a", 0, 2),
        ("a", 1, 0), ("a", 1, 1), ("s", 4, 0), ("a", 1, 2), ("s", 2, 2), ("s", 3, 1), ("a", 2, 0),
        ("a", 2, 1), ("s", 2, 3), ("s", 3, 2), ("a", 2, 2), ("a", 3, 0), ("s", 3, 3), ("s", 5, 0),
        ("a", 3, 1), ("a", 3, 2), ("w", 8), ("v", 0), ("s", 4, 1), ("s", 6, 0), ("w", 9),
        ("s", 0, 4), ("v", 1), ("w", 10), ("s", 1, 4), ("w", 11), ("s", 0, 5), ("v", 2),
        ("s", 4, 2), ("s", 7, 0), ("s", 1, 5), ("s", 4, 3), ("v", 3), ("s", 8, 0), ("s", 2, 4),
        ("s", 5, 1), ("s", 3, 4), ("v", 4), ("s", 5, 2), ("s", 2, 5), ("s", 6, 1), ("s", 5, 3),
        ("s", 4, 4), ("s", 6, 2), ("s", 3, 5), ("s", 5, 4), ("s", 6, 3), ("s", 4, 5), ("s", 7, 1),
        ("s", 6, 4), ("s", 5, 5), ("s", 8, 1), ("s", 7, 2), ("s", 8, 2), ("s", 7, 3), ("s", 6, 5),
        ("s", 8, 3), ("s", 7, 4), ("s", 8, 4), ("s", 7, 5), ("s", 8, 5),
    ]


def attend_back(act, hidden_grad, ffn_grad, mixed_low, pre_grad, context, qkv, x, w_out, w_qkv, vectors, sizes, order=None):
    rows, width = x.shape
    inner = act.shape[1]
    n_z, n_x, n_y = sizes
    comm = n_x == 2 and n_y == 2 and width % (64 * n_z) == 0
    hbm = pl.BlockSpec(memory_space=pl.ANY)
    vmem = pl.BlockSpec(memory_space=pltpu.VMEM)
    shape = jax.ShapeDtypeStruct
    tiles = rows // TILE
    scratch = [
        pltpu.VMEM((4, rows, width), bf16),
        pltpu.VMEM((rows, width), bf16),
        pltpu.VMEM((rows, width), bf16),
        pltpu.VMEM((rows, width), f32),
        pltpu.VMEM((rows, width), bf16),
        pltpu.VMEM((rows, 3 * width), bf16),
        pltpu.VMEM((rows, width), bf16),
        pltpu.VMEM((width, width), bf16),
        pltpu.VMEM((width, 3 * width), bf16),
        pltpu.VMEM((rows, width), bf16),
        pltpu.VMEM((TILE, width), bf16),
        pltpu.VMEM((2 * TICKS, width, width), bf16),
        pltpu.VMEM((2, width, width), bf16),
        pltpu.VMEM((TICKS, width // 2, width), bf16),
        pltpu.VMEM((TICKS, width // 4, width), bf16),
        pltpu.VMEM((TICKS, n_z - 1, width // 4 // n_z, width), bf16),
        pltpu.VMEM((6 + n_z,) + vectors.shape, f32),
        pltpu.SemaphoreType.DMA((16,)),
        pltpu.SemaphoreType.DMA((tiles + TICKS,)),
        pltpu.SemaphoreType.DMA((6, TICKS)),
        pltpu.SemaphoreType.DMA((6, TICKS)),
        pltpu.SemaphoreType.DMA((2, TICKS, n_z - 1)),
        pltpu.SemaphoreType.DMA((2, TICKS, n_z - 1)),
        pltpu.SemaphoreType.DMA((2 + n_z,)),
        pltpu.SemaphoreType.DMA((2 + n_z,)),
    ]
    params = dict(vmem_limit_bytes=60 * MIB)
    if comm:
        params.update(collective_id=0, has_side_effects=True)
    g_ffo, rest, grad_in, vectors = pl.pallas_call(
        functools.partial(attend_back_kernel, n_z, n_x, comm, order or schedule()),
        out_shape=(
            shape((inner, width), bf16),
            shape((width, inner + 4 * width), bf16),
            shape((rows, width), f32),
            shape(vectors.shape, f32),
        ),
        in_specs=[hbm] * 10 + [vmem],
        out_specs=(hbm, hbm, hbm, vmem),
        scratch_shapes=scratch,
        compiler_params=pltpu.CompilerParams(**params),
        name="attend_back_and_sums",
    )(act, hidden_grad, ffn_grad, mixed_low, pre_grad, context, qkv, x, w_out, w_qkv, vectors)
    if not comm:
        g_ffo, rest, vectors = lax.psum((g_ffo, rest, vectors), ("wide", "narrow"))
    return g_ffo, rest, grad_in, vectors


def widen_kernel(
    ffo_ref,
    rest_ref,
    block_ref,
    grad_ref,
    vec_ref,
    losses_ref,
    w_ffo,
    w_in,
    w_out,
    w_qkv,
    block,
    grad,
    span_loss,
    loss,
    b_in,
    *vectors,
):
    inner, width = w_in.shape[1], w_out.shape[1]
    block[...] = block_ref[...]
    grad[...] = grad_ref[...]
    w_ffo[...] = ffo_ref[...].astype(f32)
    w_in[...] = rest_ref[:, :inner].astype(f32)
    w_out[...] = rest_ref[:, inner : inner + width].astype(f32)
    w_qkv[...] = rest_ref[:, inner + width :].astype(f32)

    @pl.when(pl.program_id(0) == 0)
    def _():
        count = span_loss.shape[0]
        span_loss[...] = losses_ref[:, :count].reshape(count)
        loss[...] = losses_ref[:, count : count + 1].reshape(1)
        for k, vector in enumerate(vectors):
            vector[...] = vec_ref[k : k + 1, :].reshape(vector.shape)
        for j in range(inner // width):
            at = 8 + j
            b_in[pl.ds(j * width, width)] = vec_ref[at : at + 1, :].reshape(width)


def widen(ffo, rest, block, grad, vectors, losses, span_count):
    rows = block.shape[0]
    inner, width = ffo.shape
    steps = 2
    shape = jax.ShapeDtypeStruct

    def tiles(rows, cols):
        return pl.BlockSpec((rows // steps, cols), lambda i: (i, 0))

    def whole(*sizes):
        return pl.BlockSpec(sizes, lambda i: (0,) * len(sizes))

    flat = [span_count, 1, inner] + [width] * 8
    return pl.pallas_call(
        widen_kernel,
        grid=(steps,),
        out_shape=(
            shape((inner, width), f32),
            shape((width, inner), f32),
            shape((width, width), f32),
            shape((width, 3 * width), f32),
            shape(block.shape, block.dtype),
            shape(grad.shape, grad.dtype),
            *(shape((n,), f32) for n in flat),
        ),
        in_specs=[
            tiles(inner, width),
            tiles(width, rest.shape[1]),
            tiles(rows, width),
            tiles(rows, width),
            whole(*vectors.shape),
            whole(*losses.shape),
        ],
        out_specs=(
            tiles(inner, width),
            tiles(width, inner),
            tiles(width, width),
            tiles(width, 3 * width),
            tiles(rows, width),
            tiles(rows, width),
            *(whole(n) for n in flat),
        ),
        compiler_params=pltpu.CompilerParams(vmem_limit_bytes=60 * MIB),
        name="widen",
    )(ffo, rest, block, grad, vectors, losses)


def mesh_sizes():
    n_wide, n_narrow = lax.axis_size("wide"), lax.axis_size("narrow")
    n_y = n_narrow // 2
    n_x = n_y if n_wide % n_y == 0 else 1
    return n_wide // n_x, n_x, n_y


def per_device(
    hidden_in,
    out_grad,
    w_qkv,
    b_query,
    b_value,
    w_out,
    b_out,
    ln1_gain,
    ln1_bias,
    w_in,
    b_in,
    w_ff_out,
    b_ff_out,
    ln2_gain,
    ln2_bias,
    doc_count,
    single_flag,
):
    rows, width = hidden_in.shape
    span_count = rows // SPAN_LEN
    sizes = mesh_sizes()

    qkv, context, block_out, mixed_low, act, ffn_grad, hidden_grad, pre_one_grad, vectors, losses = middle(
        hidden_in, w_qkv, w_out, w_in, w_ff_out, out_grad, b_query, b_value, b_out, b_in, b_ff_out,
        ln1_gain, ln1_bias, ln2_gain, ln2_bias, doc_count, single_flag, sizes,
    )
    g_ffo, rest, grad_in, vectors = attend_back(
        act, hidden_grad, ffn_grad, mixed_low, pre_one_grad, context, qkv, hidden_in, w_out, w_qkv,
        vectors, sizes,
    )
    (
        g_ffo, g_in, g_out, g_qkv, block_out, grad_in, span_loss, loss, g_b_in, *rest_grads
    ) = widen(g_ffo, rest, block_out, grad_in, vectors, losses, span_count)
    g_b_query, g_b_value, g_b_out, g_gain_one, g_bias_one, g_b_ffo, g_gain_two, g_bias_two = rest_grads
    return (
        block_out,
        loss.reshape(()),
        span_loss,
        grad_in,
        g_qkv,
        g_b_query,
        g_b_value,
        g_out,
        g_b_out,
        g_gain_one,
        g_bias_one,
        g_in,
        g_b_in,
        g_ffo,
        g_b_ffo,
        g_gain_two,
        g_bias_two,
    )


def solution(mesh):
    placed = (
        P(("wide", "narrow"), None),
        P(("wide", "narrow"), None),
        P(),
        P(),
        P(),
        P(),
        P(),
        P(),
        P(),
        P(),
        P(),
        P(),
        P(),
        P(),
        P(),
        P(),
        P(),
    )
    return jax.shard_map(
        per_device,
        mesh=mesh,
        in_specs=placed,
        out_specs=(
            P(("wide", "narrow"), None),
            P(),
            P(("wide", "narrow")),
            P(("wide", "narrow"), None),
            P(),
            P(),
            P(),
            P(),
            P(),
            P(),
            P(),
            P(),
            P(),
            P(),
            P(),
            P(),
            P(),
        ),
        check_vma=False,
    )
```

```python
import functools

import jax
import jax.numpy as jnp
from jax import lax
from jax.experimental import pallas as pl
from jax.experimental.pallas import tpu as pltpu
from jax.sharding import PartitionSpec as P

HEAD_DIM = 64
SPAN_LEN = 128
TILE = 256

ln_eps = 1e-06
score_scale = 0.2
far_low = -1000000000.0
head_scale = HEAD_DIM ** (-0.5)
MESH = pl.DeviceIdType.MESH
TICKS = 6
f32, bf16, i32 = jnp.float32, jnp.bfloat16, jnp.int32
MIB = 2**20


def dot(left, right):
    return jnp.dot(left, right, preferred_element_type=f32)


def dot_left_t(left, right):
    return lax.dot_general(left, right, (((0,), (0,)), ((), ())), preferred_element_type=f32)


def dot_right_t(left, right):
    return lax.dot_general(left, right, (((1,), (1,)), ((), ())), preferred_element_type=f32)


def row_mean(values):
    return jnp.mean(values, axis=1, keepdims=True)


def col_sum(values):
    return jnp.sum(values, axis=0, keepdims=True)


def norm_back(upstream, normed, scale, gain):
    scaled = upstream * gain
    return scale * (scaled - row_mean(scaled) - normed * row_mean(scaled * normed))


def head_halves():
    first = lax.broadcasted_iota(i32, (1, 2 * HEAD_DIM), 1) < HEAD_DIM
    return first, first.astype(bf16), jnp.logical_not(first).astype(bf16)


def pair_probs(stacked_queries, keys_low):
    scores = dot_right_t(stacked_queries, keys_low)
    shifted = jnp.exp((scores - jnp.max(scores, axis=1, keepdims=True)) * head_scale)
    return shifted * (1.0 / jnp.sum(shifted, axis=1, keepdims=True))


def attend_tile(at, x_ref, w_qkv_ref, b_query, b_value, w_out_ref, b_out, qkv_ref, context_ref, cent_ref):
    width = x_ref.shape[1]
    inputs = x_ref[at, :]
    for third in range(3):
        cols = pl.ds(third * width, width)
        packed = dot(inputs, w_qkv_ref[:, cols])
        if third == 0:
            packed = packed + b_query
        if third == 2:
            packed = packed + b_value
        qkv_ref[at, cols] = packed.astype(bf16)
    first, low_one, low_two = head_halves()
    lanes = 2 * HEAD_DIM
    for span in range(at.size // SPAN_LEN):
        sp = pl.ds(pl.multiple_of(at.start + span * SPAN_LEN, SPAN_LEN), SPAN_LEN)
        for pair in range(width // lanes):
            queries = qkv_ref[sp, pl.ds(pair * lanes, lanes)]
            keys_low = qkv_ref[sp, pl.ds(width + pair * lanes, lanes)]
            values_low = qkv_ref[sp, pl.ds(2 * width + pair * lanes, lanes)]
            stacked = jnp.concatenate([queries * low_one, queries * low_two], axis=0)
            mixed_values = dot(pair_probs(stacked, keys_low).astype(bf16), values_low)
            context_ref[sp, pl.ds(pair * lanes, lanes)] = jnp.where(
                first, mixed_values[:SPAN_LEN], mixed_values[SPAN_LEN:]
            ).astype(bf16)
    pre_one = inputs.astype(f32) + (dot(context_ref[at, :], w_out_ref[...]) + b_out)
    cent_ref[at, :] = pre_one - row_mean(pre_one)


def gelu_parts(values):
    cdf = 0.5 * (1.0 + lax.erf(values * 0.7071067811865476))
    pdf = 0.3989422804014327 * jnp.exp(-0.5 * values * values)
    return values * cdf, cdf + values * pdf


def contrast_rows(cls_low, count, flags, first, span_count):
    total, width = cls_low.shape
    slots, docsets = flags.shape
    block = min(total, 256)

    def layout(at):
        slot = at + lax.broadcasted_iota(i32, (block, 1), 0)
        device = slot // slots
        place = (slot - device * slots).astype(f32)
        member = lax.broadcasted_iota(i32, (block, docsets), 1) == device
        docs = jnp.sum(jnp.where(member, count, 0.0), axis=1, keepdims=True)
        single = dot_right_t(member.astype(bf16), flags.astype(bf16))
        doc = lax.broadcasted_iota(i32, (block, slots), 1).astype(f32)
        length = jnp.where(doc < docs, 2.0 - single, 0.0)
        earlier = lax.broadcasted_iota(i32, (slots, slots), 0) < lax.broadcasted_iota(
            i32, (slots, slots), 1
        )
        begins = dot(length.astype(bf16), earlier.astype(f32).astype(bf16))
        inside = (place >= begins) & (place < begins + length)
        double = inside & (length == 2.0)
        live = jnp.max(inside.astype(f32), axis=1, keepdims=True)
        pair = jnp.max(double.astype(f32), axis=1, keepdims=True)
        other = jnp.sum(jnp.where(double, 2.0 * begins + 1.0 - place, 0.0), axis=1, keepdims=True)
        mate = jnp.where(pair > 0.0, (device * slots).astype(f32) + other, slot.astype(f32))
        return slot.astype(f32), live, pair, mate

    eye = lax.broadcasted_iota(i32, (block, block), 0) == lax.broadcasted_iota(
        i32, (block, block), 1
    )
    live_row = jnp.concatenate(
        [col_sum(jnp.where(eye, layout(at)[1], 0.0)) for at in range(0, total, block)], axis=1
    )
    column = lax.broadcasted_iota(i32, (block, total), 1).astype(f32)
    pick_col = (
        lax.broadcasted_iota(i32, (span_count, total), 1)
        == first + lax.broadcasted_iota(i32, (span_count, total), 0)
    ).astype(f32).astype(bf16)
    rows_own = jnp.zeros((span_count, total), f32)
    upward = jnp.zeros((span_count, width), f32)
    own_loss = jnp.zeros((1, span_count), f32)
    loss = jnp.zeros((1, 1), f32)
    for at in range(0, total, block):
        slot, live, pair, mate = layout(at)
        cls_block = cls_low[at : at + block, :]
        sims = score_scale * dot_right_t(cls_block, cls_low)
        allowed = (live_row > 0.0) & (column != slot)
        masked = jnp.where(allowed, sims, far_low)
        top = jnp.max(masked, axis=1, keepdims=True)
        lse = top + jnp.log(jnp.sum(jnp.exp(masked - top), axis=1, keepdims=True))
        matches = column == mate
        positive = jnp.sum(jnp.where(matches, sims, 0.0), axis=1, keepdims=True)
        span_loss = jnp.where(pair > 0.0, lse - positive, 0.0)
        loss = loss + col_sum(span_loss)
        mine = at + lax.broadcasted_iota(i32, (block, span_count), 0) == (
            first + lax.broadcasted_iota(i32, (block, span_count), 1)
        )
        own_loss = own_loss + col_sum(jnp.where(mine, span_loss, 0.0))
        sim_grad = jnp.where(
            pair > 0.0, jnp.exp(masked - lse) - matches.astype(f32), 0.0
        ).astype(bf16)
        pick_row = (
            at + lax.broadcasted_iota(i32, (span_count, block), 1)
            == first + lax.broadcasted_iota(i32, (span_count, block), 0)
        ).astype(f32).astype(bf16)
        rows_own = rows_own + dot(pick_row, sim_grad)
        cols_own = dot_right_t(pick_col, sim_grad)
        upward = upward + dot(cols_own.astype(bf16), cls_block)
    upward = upward + dot(rows_own.astype(bf16), cls_low)
    return score_scale * upward, own_loss, loss


def middle_kernel(
    n_z,
    n_x,
    n_y,
    x_hbm,
    w_qkv_hbm,
    w_out_hbm,
    w_in_hbm,
    w_ffo_hbm,
    out_grad_hbm,
    b_query_ref,
    b_value_ref,
    b_out_ref,
    b_in_ref,
    b_ffo_ref,
    gain_one_ref,
    bias_one_ref,
    gain_two_ref,
    bias_two_ref,
    count_ref,
    flag_ref,
    qkv_hbm,
    context_hbm,
    block_hbm,
    mixed_hbm,
    act_hbm,
    ffn_grad_hbm,
    hidden_grad_hbm,
    pre_grad_hbm,
    vec_ref,
    losses_ref,
    x_v,
    w_qkv,
    w_out,
    qkv_v,
    context_v,
    cent_v,
    w_in,
    w_ffo,
    upper_v,
    block_v,
    mixed_v,
    act_v,
    slope_v,
    ffn_grad_v,
    two_v,
    first_v,
    cls_grad_v,
    b_in_v,
    cls_v,
    in_sem,
    out_sem,
    s_sem,
    r_sem,
):
    rows, width = cent_v.shape
    inner = w_in.shape[1]
    chunks = inner // width
    tiles = rows // TILE
    span_count = rows // SPAN_LEN
    wide, narrow = lax.axis_index("wide"), lax.axis_index("narrow")
    z, x = wide // n_x, lax.rem(wide, n_x)
    y, c = narrow // 2, lax.rem(narrow, 2)
    core = (wide, y * 2 + 1 - c)
    along_x = [(z * n_x + lax.rem(x + k, n_x), narrow) for k in range(1, n_x)]
    along_y = [(wide, lax.rem(y + k, n_y) * 2 + c) for k in range(1, n_y)]
    along_z = [(lax.rem(z + k, n_z) * n_x + x, narrow) for k in range(1, n_z)]
    partners = [core] + along_x + along_y + along_z

    barrier = pltpu.get_barrier_semaphore()
    for device in partners:
        pl.semaphore_signal(barrier, inc=1, device_id=device, device_id_type=MESH)

    loads = [
        pltpu.make_async_copy(src, dst, in_sem.at[k])
        for k, (src, dst) in enumerate(
            (
                (x_hbm, x_v),
                (w_qkv_hbm, w_qkv),
                (w_out_hbm, w_out),
                (w_in_hbm, w_in),
                (w_ffo_hbm, w_ffo),
                (out_grad_hbm, upper_v),
            )
        )
    ]
    for copy in loads:
        copy.start()

    def row(ref, at=0):
        return ref[pl.ds(at, width)].astype(f32).reshape(1, width)

    gain_one, bias_one, gain_two, bias_two, b_ffo = (
        row(r) for r in (gain_one_ref, bias_one_ref, gain_two_ref, bias_two_ref, b_ffo_ref)
    )
    for j in range(chunks):
        b_in_v[j : j + 1, :] = row(b_in_ref, j * width)

    def normed(cent):
        scale = lax.rsqrt(row_mean(cent * cent) + ln_eps)
        return cent * scale, scale

    def feed_forward(mixed, total, keep):
        mixed_low = mixed.astype(bf16)
        total[...] = mixed + b_ffo

        def step(j, carry):
            cols = pl.ds(pl.multiple_of(j * width, width), width)
            hidden = dot(mixed_low, w_in[:, cols]) + b_in_v[pl.ds(j, 1), :]
            act, slope = gelu_parts(hidden)
            act_low = act.astype(bf16)
            keep(cols, act_low, slope)
            total[...] += dot(act_low, w_ffo[cols, :])
            return carry

        lax.fori_loop(0, chunks, step, 0, unroll=True)
        pre_two = total[...]
        return pre_two - row_mean(pre_two)

    b_query, b_value, b_out = (row(r) for r in (b_query_ref, b_value_ref, b_out_ref))

    def store(src, dst, at, k):
        return pltpu.make_async_copy(src.at[at, :], dst.at[at, :], out_sem.at[k])

    def tile_rows(tile):
        return pl.ds(pl.multiple_of(tile * TILE, TILE), TILE)

    def attend_stores(tile):
        at = tile_rows(tile)
        return [
            store(qkv_v, qkv_hbm, at, 8 * tile + 6),
            store(context_v, context_hbm, at, 8 * tile + 7),
        ]

    def attend_step(tile, carry):
        attend_tile(
            tile_rows(tile), x_v, w_qkv, b_query, b_value, w_out, b_out, qkv_v, context_v, cent_v
        )
        for copy in attend_stores(tile):
            copy.start()
        return carry

    for copy in loads[:3]:
        copy.wait()
    lax.fori_loop(0, tiles, attend_step, 0)

    first_cent = jnp.concatenate(
        [cent_v[s * SPAN_LEN : s * SPAN_LEN + 1, :] for s in range(span_count)], axis=0
    )
    first_mixed = normed(first_cent)[0] * gain_one + bias_one
    loads[3].wait()
    loads[4].wait()
    first_two = feed_forward(first_mixed, first_v, lambda cols, act, slope: None)
    first_out = normed(first_two)[0] * gain_two + bias_two
    half = width // 2
    cls_v[z, x, y, c] = jnp.concatenate([first_out[:, :half], first_out[:, half:]], axis=0).astype(
        bf16
    )
    pl.semaphore_wait(barrier, len(partners))

    def gathers(stage):
        if stage == 0:
            ref, devices, base = cls_v.at[z, x, y, c], along_z, 0
        elif stage == 1:
            ref, devices, base = cls_v.at[:, x, y, c], along_x, n_z - 1
        elif stage == 2:
            ref, devices, base = cls_v.at[:, :, y, c], along_y, n_z + n_x - 2
        else:
            ref, devices, base = cls_v.at[:, :, :, c], [core], n_z + n_x + n_y - 3
        return [
            pltpu.make_async_remote_copy(
                ref, ref, s_sem.at[base + k], r_sem.at[base + k], device_id=d, device_id_type=MESH
            )
            for k, d in enumerate(devices)
        ]

    for copy in gathers(0):
        copy.start()
    loads[5].wait()

    def forward_stores(tile):
        at = tile_rows(tile)
        return [
            store(mixed_v, mixed_hbm, at, 8 * tile),
            store(block_v, block_hbm, at, 8 * tile + 1),
            store(act_v, act_hbm, at, 8 * tile + 2),
        ]

    def backward_stores(tile):
        at = tile_rows(tile)
        return [
            store(ffn_grad_v, ffn_grad_hbm, at, 8 * tile + 3),
            store(slope_v, hidden_grad_hbm, at, 8 * tile + 4),
            store(cent_v, pre_grad_hbm, at, 8 * tile + 5),
        ]

    def forward_tile(tile, carry):
        at = tile_rows(tile)
        mixed = normed(cent_v[at, :])[0] * gain_one + bias_one
        mixed_v[at, :] = mixed.astype(bf16)

        def keep(cols, act_low, slope):
            act_v[at, cols] = act_low
            slope_v[at, cols] = slope.astype(bf16)

        cent_two = feed_forward(mixed, two_v.at[at, :], keep)
        block_v[at, :] = (normed(cent_two)[0] * gain_two + bias_two).astype(bf16)
        two_v[at, :] = cent_two
        for copy in forward_stores(tile):
            copy.start()
        for stage in range(4):

            @pl.when(tile == min(stage, tiles - 1))
            def _():
                for copy in gathers(stage):
                    copy.wait()
                if stage < 3:
                    for copy in gathers(stage + 1):
                        copy.start()

        return carry

    lax.fori_loop(0, tiles, forward_tile, 0)

    low = cls_v[...].astype(f32).reshape(-1, 2 * span_count, half)
    cls_low = jnp.concatenate(
        [
            low[:, :span_count, :].reshape(-1, half),
            low[:, span_count:, :].reshape(-1, half),
        ],
        axis=1,
    ).astype(bf16)
    own = wide * (2 * n_y) + narrow
    cls_grad, own_loss, loss = contrast_rows(
        cls_low, count_ref[...].astype(f32).reshape(1, -1), flag_ref[...].astype(f32), own * span_count, span_count
    )
    cls_grad_v[...] = cls_grad
    lane = lax.broadcasted_iota(i32, losses_ref.shape, 1)
    losses_ref[...] = jnp.where(lane == span_count, loss, 0.0)
    losses_ref[:, :span_count] = own_loss

    vec_ref[...] = jnp.zeros(vec_ref.shape, f32)

    def add_row(k, values):
        vec_ref[pl.ds(k, 1), :] += col_sum(values)

    def backward_tile(tile, carry):
        at = tile_rows(tile)
        upper = upper_v[at, :].astype(f32)
        place = lax.broadcasted_iota(i32, (TILE, 1), 0)
        for span in range(TILE // SPAN_LEN):
            upper = jnp.where(
                place == span * SPAN_LEN,
                cls_grad_v[pl.ds(tile * (TILE // SPAN_LEN) + span, 1), :],
                upper,
            )
        normed_two, scale_two = normed(two_v[at, :])
        add_row(6, upper * normed_two)
        add_row(7, upper)
        pre_two_grad = norm_back(upper, normed_two, scale_two, gain_two)
        ffn_grad = pre_two_grad.astype(bf16)
        ffn_grad_v[at, :] = ffn_grad
        add_row(5, ffn_grad.astype(f32))
        two_v[at, :] = pre_two_grad

        def step(j, inner_carry):
            cols = pl.ds(pl.multiple_of(j * width, width), width)
            back = dot_right_t(ffn_grad, w_ffo[cols, :]) * slope_v[at, cols].astype(f32)
            hidden_grad = back.astype(bf16)
            slope_v[at, cols] = hidden_grad
            add_row(8 + j, hidden_grad.astype(f32))
            two_v[at, :] += dot_right_t(hidden_grad, w_in[:, cols])
            return inner_carry

        lax.fori_loop(0, chunks, step, 0, unroll=True)
        mixed_grad = two_v[at, :]
        normed_one, scale_one = normed(cent_v[at, :])
        add_row(3, mixed_grad * normed_one)
        add_row(4, mixed_grad)
        pre_one_grad = norm_back(mixed_grad, normed_one, scale_one, gain_one)
        cent_v[at, :] = pre_one_grad
        add_row(2, pre_one_grad.astype(bf16).astype(f32))
        for copy in backward_stores(tile):
            copy.start()
        return carry

    lax.fori_loop(0, tiles, backward_tile, 0)

    for tile in range(tiles):
        for copy in attend_stores(tile) + forward_stores(tile) + backward_stores(tile):
            copy.wait()


def middle(
    x,
    w_qkv,
    w_out,
    w_in,
    w_ffo,
    out_grad,
    b_query,
    b_value,
    b_out,
    b_in,
    b_ffo,
    gain_one,
    bias_one,
    gain_two,
    bias_two,
    doc_count,
    single_flag,
    sizes,
):
    rows, width = x.shape
    inner = w_in.shape[1]
    span_count = rows // SPAN_LEN
    n_z, n_x, n_y = sizes
    moves = n_z + n_x + n_y - 2
    hbm = pl.BlockSpec(memory_space=pl.ANY)
    vmem = pl.BlockSpec(memory_space=pltpu.VMEM)
    shape = jax.ShapeDtypeStruct
    return pl.pallas_call(
        functools.partial(middle_kernel, n_z, n_x, n_y),
        out_shape=(
            shape((rows, 3 * width), bf16),
            shape((rows, width), bf16),
            shape((rows, width), bf16),
            shape((rows, width), bf16),
            shape((rows, inner), bf16),
            shape((rows, width), bf16),
            shape((rows, inner), bf16),
            shape((rows, width), f32),
            shape((16, width), f32),
            shape((1, 128), f32),
        ),
        in_specs=[hbm] * 6 + [vmem] * 11,
        out_specs=(hbm,) * 8 + (vmem,) * 2,
        scratch_shapes=[
            pltpu.VMEM((rows, width), bf16),
            pltpu.VMEM((width, 3 * width), bf16),
            pltpu.VMEM((width, width), bf16),
            pltpu.VMEM((rows, 3 * width), bf16),
            pltpu.VMEM((rows, width), bf16),
            pltpu.VMEM((rows, width), f32),
            pltpu.VMEM((width, inner), bf16),
            pltpu.VMEM((inner, width), bf16),
            pltpu.VMEM((rows, width), bf16),
            pltpu.VMEM((rows, width), bf16),
            pltpu.VMEM((rows, width), bf16),
            pltpu.VMEM((rows, inner), bf16),
            pltpu.VMEM((rows, inner), bf16),
            pltpu.VMEM((rows, width), bf16),
            pltpu.VMEM((rows, width), f32),
            pltpu.VMEM((span_count, width), f32),
            pltpu.VMEM((span_count, width), f32),
            pltpu.VMEM((inner // width, width), f32),
            pltpu.VMEM((n_z, n_x, n_y, 2, 2 * span_count, width // 2), bf16),
            pltpu.SemaphoreType.DMA((6,)),
            pltpu.SemaphoreType.DMA((8 * (rows // TILE),)),
            pltpu.SemaphoreType.DMA((moves,)),
            pltpu.SemaphoreType.DMA((moves,)),
        ],
        compiler_params=pltpu.CompilerParams(
            collective_id=1, has_side_effects=True, vmem_limit_bytes=60 * MIB
        ),
        name="forward_and_loss",
    )(
        x, w_qkv, w_out, w_in, w_ffo, out_grad, b_query, b_value, b_out, b_in, b_ffo, gain_one, bias_one,
        gain_two, bias_two, doc_count, single_flag.T,
    )


def attend_back_kernel(
    n_z,
    n_x,
    comm,
    order,
    act_hbm,
    hidden_grad_hbm,
    ffn_grad_hbm,
    mixed_hbm,
    pre_grad_hbm,
    context_hbm,
    qkv_hbm,
    x_hbm,
    w_out_hbm,
    w_qkv_hbm,
    vec_ref,
    o_ffo,
    o_rest,
    grad_in_hbm,
    o_vec,
    stream,
    ffn_grad_v,
    mixed_v,
    pre_v,
    context_v,
    qkv_v,
    x_v,
    w_out,
    w_qkv,
    attn_v,
    context_grad_v,
    part,
    sib,
    r1,
    r2,
    r3,
    vbuf,
    in_sem,
    out_sem,
    s_sem,
    r_sem,
    zs_sem,
    zr_sem,
    vs_sem,
    vr_sem,
):
    rows, width = x_v.shape
    half, quarter = width // 2, width // 4
    eighth = quarter // n_z
    tiles = rows // TILE
    ahead = stream.shape[0]
    wide, narrow = lax.axis_index("wide"), lax.axis_index("narrow")
    z, x = wide // n_x, lax.rem(wide, n_x)
    y, c = narrow // 2, lax.rem(narrow, 2)
    core = (wide, y * 2 + 1 - c)
    near_x = (z * n_x + 1 - x, narrow)
    near_y = (wide, (1 - y) * 2 + c)
    one = tuple(jnp.where(c == 0, a, b) for a, b in zip(near_x, near_y))
    two = tuple(jnp.where(c == 0, b, a) for a, b in zip(near_x, near_y))
    h1 = jnp.where(c == 0, x, y)
    h2 = jnp.where(c == 0, y, x)
    others = [lax.rem(z + k, n_z) for k in range(1, n_z)]
    along_z = [(o * n_x + x, narrow) for o in others]

    if comm:
        barrier = pltpu.get_barrier_semaphore()
        for device in [core, near_x, near_y] + along_z:
            pl.semaphore_signal(barrier, inc=1, device_id=device, device_id_type=MESH)

    def stream_load(j):
        src = act_hbm if j < 4 else hidden_grad_hbm
        return pltpu.make_async_copy(
            src.at[:, pl.ds((j % 4) * width, width)], stream.at[j % ahead], in_sem.at[j]
        )

    resident = [
        pltpu.make_async_copy(src, dst, in_sem.at[8 + k])
        for k, (src, dst) in enumerate(
            (
                (ffn_grad_hbm, ffn_grad_v),
                (mixed_hbm, mixed_v),
                (pre_grad_hbm, pre_v),
                (w_out_hbm, w_out),
                (qkv_hbm, qkv_v),
                (w_qkv_hbm, w_qkv),
                (context_hbm, context_v),
                (x_hbm, x_v),
            )
        )
    ]
    stream_load(0).start()
    resident[0].start()
    for j in range(1, ahead):
        stream_load(j).start()
    for copy in resident[1:]:
        copy.start()
    vbuf[0] = vec_ref[...]
    waited = set()

    def need(*which):
        for k in which:
            if k not in waited:
                waited.add(k)
                resident[k].wait()

    first, low_one, low_two = head_halves()
    lanes = 2 * HEAD_DIM

    def weight_block(b):
        if b < 8:
            stream_load(b).wait()
        if b < 4:
            need(0)
            left, right = stream.at[b % ahead], ffn_grad_v
        elif b < 8:
            need(1)
            left, right = mixed_v, stream.at[b % ahead]
        elif b < 9:
            need(6)
            left, right = context_v, attn_v
        else:
            need(7)
            left, right = x_v, qkv_v.at[:, pl.ds((b - 9) * width, width)]

        def step(i, carry):
            at = pl.ds(pl.multiple_of(i * TILE, TILE), TILE)
            part[b, at, :] = dot_left_t(left[:, at], right[...]).astype(bf16)
            return carry

        lax.fori_loop(0, width // TILE, step, 0, unroll=True)
        if b + ahead < 8:
            stream_load(b + ahead).start()

    def grad_in_store(tile):
        at = pl.ds(tile * TILE, TILE)
        return pltpu.make_async_copy(pre_v.at[at, :], grad_in_hbm.at[at, :], out_sem.at[tile])

    def attend_tile(tile, piece):
        need(2, 3, 4, 5)
        at = pl.ds(tile * TILE, TILE)
        if piece == 0:
            attn_grad = pre_v[at, :].astype(bf16)
            attn_v[at, :] = attn_grad
            context_grad_v[...] = dot_right_t(attn_grad, w_out[...]).astype(bf16)
        if piece == 2:
            vbuf[0, 0:1, :] += col_sum(qkv_v[at, 0:width].astype(f32))
            vbuf[0, 1:2, :] += col_sum(qkv_v[at, 2 * width : 3 * width].astype(f32))
            pre_v[at, :] += dot_right_t(qkv_v[at, :], w_qkv[...])
            grad_in_store(tile).start()
            return

        def pair_step(pair):
            q_at, k_at, v_at = (pl.ds(third * width + pair * lanes, lanes) for third in range(3))
            for span in range(TILE // SPAN_LEN):
                sp = pl.ds(tile * TILE + span * SPAN_LEN, SPAN_LEN)
                queries, keys_low, values_low = qkv_v[sp, q_at], qkv_v[sp, k_at], qkv_v[sp, v_at]
                upper = context_grad_v[pl.ds(span * SPAN_LEN, SPAN_LEN), q_at]
                stacked = jnp.concatenate([queries * low_one, queries * low_two], axis=0)
                stacked_up = jnp.concatenate([upper * low_one, upper * low_two], axis=0)
                scores = dot_right_t(keys_low, stacked)
                shifted = jnp.exp((scores - jnp.max(scores, axis=0, keepdims=True)) * head_scale)
                probs = shifted * (1.0 / col_sum(shifted))
                value_grad = dot(probs.astype(bf16), stacked_up)
                prob_grad = dot_right_t(values_low, stacked_up)
                score_grad = (probs * (prob_grad - col_sum(probs * prob_grad))).astype(bf16)
                query_grad = dot_left_t(score_grad, keys_low) * head_scale
                key_grad = dot(score_grad, stacked) * head_scale
                qkv_v[sp, q_at] = jnp.where(
                    first, query_grad[:SPAN_LEN], query_grad[SPAN_LEN:]
                ).astype(bf16)
                qkv_v[sp, k_at] = key_grad.astype(bf16)
                qkv_v[sp, v_at] = value_grad.astype(bf16)

        pairs = width // lanes
        for pair in range(pairs // 2) if piece == 0 else range(pairs // 2, pairs):
            pair_step(pair)

    def out_at(t, row, count):
        if t < 2:
            at = pl.multiple_of((2 * t + c) * width + row, 16)
            return o_ffo.at[pl.ds(at, count), :]
        cols = pl.multiple_of((2 * (t - 2) + c) * width, 128)
        return o_rest.at[pl.ds(pl.multiple_of(row, 16), count), pl.ds(cols, width)]

    def part_at(t, row, count):
        return part.at[2 * t + c, pl.ds(pl.multiple_of(row, 16), count), :]

    keep1 = h1 * half
    keep2 = keep1 + h2 * quarter
    own = keep2 + z * eighth

    def send(src, dst, stage, t, device):
        return pltpu.make_async_remote_copy(
            src, dst, s_sem.at[stage, t], r_sem.at[stage, t], device_id=device, device_id_type=MESH
        )

    def send_z(src, dst, stage, t, k):
        return pltpu.make_async_remote_copy(
            src,
            dst,
            zs_sem.at[stage, t, k],
            zr_sem.at[stage, t, k],
            device_id=along_z[k],
            device_id_type=MESH,
        )

    def sibling_slot(t, of):
        return sib.at[t] if t < 2 else part.at[2 * (t - 2) + 1 - of]

    def copies(stage, t):
        if stage == 0:
            return [send(part.at[2 * t + 1 - c], sibling_slot(t, 1 - c), 0, t, core)]
        if stage == 1:
            return [send(part_at(t, (1 - h1) * half, half), r1.at[t], 1, t, one)]
        if stage == 2:
            return [send(part_at(t, keep1 + (1 - h2) * quarter, quarter), r2.at[t], 2, t, two)]
        if stage == 3:
            return [
                send_z(part_at(t, keep2 + o * eighth, eighth), r3.at[t, k], 0, t, k)
                for k, o in enumerate(others)
            ]
        if stage == 4:
            return [
                send_z(part_at(t, own, eighth), out_at(t, own, eighth), 1, t, k)
                for k in range(n_z - 1)
            ]
        if stage == 5:
            place = out_at(t, keep2, quarter)
            return [send(place, place, 3, t, two)]
        if stage == 6:
            place = out_at(t, keep1, half)
            return [send(place, place, 4, t, one)]
        place = out_at(t, 0, width)
        return [send(place, place, 5, t, core)]

    def add(t, row, count, got):
        def step(i, carry):
            at = pl.ds(pl.multiple_of(row + i * 48, 16), 48)
            here = part[2 * t + c, at, :].astype(f32) + got[
                pl.ds(pl.multiple_of(i * 48, 16), 48), :
            ].astype(f32)
            part[2 * t + c, at, :] = here.astype(bf16)
            return carry

        lax.fori_loop(0, count // 48, step, 0)

    def own_store(t):
        return pltpu.make_async_copy(
            part_at(t, own, eighth), out_at(t, own, eighth), out_sem.at[tiles + t]
        )

    def advance(stage, t):
        if stage > 0:
            for copy in copies(stage - 1, t):
                copy.wait()
        if stage == 1:
            add(t, 0, width, sibling_slot(t, c))
        elif stage == 2:
            add(t, keep1, half, r1.at[t])
        elif stage == 3:
            add(t, keep2, quarter, r2.at[t])
        elif stage == 4:
            total = part_at(t, own, eighth)[...].astype(f32)
            for k in range(n_z - 1):
                total = total + r3[t, k].astype(f32)
            part_at(t, own, eighth)[...] = total.astype(bf16)
            own_store(t).start()
        elif stage == 5:
            own_store(t).wait()
        if stage < 8:
            for copy in copies(stage, t):
                copy.start()

    def vector_copies(k):
        if k < 3:
            device = (core, near_x, near_y)[k]
            ends = [(vbuf.at[2 * k], vbuf.at[2 * k + 1], k, device)]
        else:
            ends = [(vbuf.at[6], vbuf.at[7 + i], 3 + i, d) for i, d in enumerate(along_z)]
        return [
            pltpu.make_async_remote_copy(
                src, dst, vs_sem.at[s], vr_sem.at[s], device_id=d, device_id_type=MESH
            )
            for src, dst, s, d in ends
        ]

    def vector_step(k):
        if k > 0:
            for copy in vector_copies(k - 1):
                copy.wait()
        if k in (1, 2, 3):
            vbuf[2 * k] = vbuf[2 * k - 2] + vbuf[2 * k - 1]
        if k < 4:
            for copy in vector_copies(k):
                copy.start()
        else:
            total = vbuf[6]
            for i in range(n_z - 1):
                total = total + vbuf[7 + i]
            o_vec[...] = total

    entered = False
    for kind, *at in order:
        if kind == "w":
            weight_block(*at)
        elif kind == "a":
            attend_tile(*at)
        elif comm:
            if not entered:
                pl.semaphore_wait(barrier, 2 + n_z)
                entered = True
            if kind == "s":
                advance(*at)
            else:
                vector_step(*at)
    if not comm:
        o_vec[...] = vbuf[0]
        locals_ = [
            pltpu.make_async_copy(
                part.at[b],
                o_ffo.at[pl.ds(b * width, width), :]
                if b < 4
                else o_rest.at[:, pl.ds((b - 4) * width, width)],
                in_sem.at[b],
            )
            for b in range(2 * TICKS)
        ]
        for copy in locals_:
            copy.start()
        for copy in locals_:
            copy.wait()
    for tile in range(tiles):
        grad_in_store(tile).wait()


def schedule():
    return [
        ("w", 0), ("w", 1), ("s", 0, 0), ("w", 2), ("w", 3), ("s", 1, 0), ("s", 0, 1), ("w", 4),
        ("w", 5), ("s", 1, 1), ("w", 6), ("s", 0, 2), ("w", 7), ("s", 2, 0), ("a", 0, 0),
        ("a", 0, 1), ("s", 1, 2), ("s", 3, 0), ("s", 0, 3), ("a", 0, 2), ("a", 1, 0), ("s", 2, 1),
        ("a", 1, 1), ("s", 4, 0), ("s", 1, 3), ("s", 2, 2), ("a", 1, 2), ("s", 3, 1), ("a", 2, 0),
        ("a", 2, 1), ("a", 2, 2), ("s", 5, 0), ("a", 3, 0), ("s", 4, 1), ("s", 2, 3), ("s", 6, 0),
        ("a", 3, 1), ("s", 3, 2), ("a", 3, 2), ("w", 8), ("v", 0), ("w", 9), ("s", 0, 4),
        ("s", 5, 1), ("w", 10), ("v", 1), ("s", 3, 3), ("s", 1, 4), ("w", 11), ("s", 0, 5),
        ("v", 2), ("s", 4, 2), ("s", 1, 5), ("s", 2, 4), ("s", 4, 3), ("v", 3), ("s", 5, 2),
        ("s", 3, 4), ("s", 6, 1), ("s", 2, 5), ("v", 4), ("s", 5, 3), ("s", 4, 4), ("s", 7, 0),
        ("s", 3, 5), ("s", 6, 3), ("s", 6, 2), ("s", 5, 4), ("s", 7, 1), ("s", 4, 5), ("s", 6, 4),
        ("s", 8, 0), ("s", 5, 5), ("s", 7, 2), ("s", 7, 3), ("s", 6, 5), ("s", 8, 3), ("s", 7, 4),
        ("s", 7, 5), ("s", 8, 4), ("s", 8, 1), ("s", 8, 2), ("s", 8, 5),
    ]


def attend_back(act, hidden_grad, ffn_grad, mixed_low, pre_grad, context, qkv, x, w_out, w_qkv, vectors, sizes, order=None):
    rows, width = x.shape
    inner = act.shape[1]
    n_z, n_x, n_y = sizes
    comm = n_x == 2 and n_y == 2 and width % (64 * n_z) == 0
    hbm = pl.BlockSpec(memory_space=pl.ANY)
    vmem = pl.BlockSpec(memory_space=pltpu.VMEM)
    shape = jax.ShapeDtypeStruct
    tiles = rows // TILE
    scratch = [
        pltpu.VMEM((4, rows, width), bf16),
        pltpu.VMEM((rows, width), bf16),
        pltpu.VMEM((rows, width), bf16),
        pltpu.VMEM((rows, width), f32),
        pltpu.VMEM((rows, width), bf16),
        pltpu.VMEM((rows, 3 * width), bf16),
        pltpu.VMEM((rows, width), bf16),
        pltpu.VMEM((width, width), bf16),
        pltpu.VMEM((width, 3 * width), bf16),
        pltpu.VMEM((rows, width), bf16),
        pltpu.VMEM((TILE, width), bf16),
        pltpu.VMEM((2 * TICKS, width, width), bf16),
        pltpu.VMEM((2, width, width), bf16),
        pltpu.VMEM((TICKS, width // 2, width), bf16),
        pltpu.VMEM((TICKS, width // 4, width), bf16),
        pltpu.VMEM((TICKS, n_z - 1, width // 4 // n_z, width), bf16),
        pltpu.VMEM((6 + n_z,) + vectors.shape, f32),
        pltpu.SemaphoreType.DMA((16,)),
        pltpu.SemaphoreType.DMA((tiles + TICKS,)),
        pltpu.SemaphoreType.DMA((6, TICKS)),
        pltpu.SemaphoreType.DMA((6, TICKS)),
        pltpu.SemaphoreType.DMA((2, TICKS, n_z - 1)),
        pltpu.SemaphoreType.DMA((2, TICKS, n_z - 1)),
        pltpu.SemaphoreType.DMA((2 + n_z,)),
        pltpu.SemaphoreType.DMA((2 + n_z,)),
    ]
    params = dict(vmem_limit_bytes=60 * MIB)
    if comm:
        params.update(collective_id=0, has_side_effects=True)
    g_ffo, rest, grad_in, vectors = pl.pallas_call(
        functools.partial(attend_back_kernel, n_z, n_x, comm, order or schedule()),
        out_shape=(
            shape((inner, width), bf16),
            shape((width, inner + 4 * width), bf16),
            shape((rows, width), f32),
            shape(vectors.shape, f32),
        ),
        in_specs=[hbm] * 10 + [vmem],
        out_specs=(hbm, hbm, hbm, vmem),
        scratch_shapes=scratch,
        compiler_params=pltpu.CompilerParams(**params),
        name="attend_back_and_sums",
    )(act, hidden_grad, ffn_grad, mixed_low, pre_grad, context, qkv, x, w_out, w_qkv, vectors)
    if not comm:
        g_ffo, rest, vectors = lax.psum((g_ffo, rest, vectors), ("wide", "narrow"))
    return g_ffo, rest, grad_in, vectors


def widen_kernel(
    ffo_ref,
    rest_ref,
    block_ref,
    grad_ref,
    vec_ref,
    losses_ref,
    w_ffo,
    w_in,
    w_out,
    w_qkv,
    block,
    grad,
    span_loss,
    loss,
    b_in,
    *vectors,
):
    inner, width = w_in.shape[1], w_out.shape[1]
    block[...] = block_ref[...]
    grad[...] = grad_ref[...]
    w_ffo[...] = ffo_ref[...].astype(f32)
    w_in[...] = rest_ref[:, :inner].astype(f32)
    w_out[...] = rest_ref[:, inner : inner + width].astype(f32)
    w_qkv[...] = rest_ref[:, inner + width :].astype(f32)

    @pl.when(pl.program_id(0) == 0)
    def _():
        count = span_loss.shape[0]
        span_loss[...] = losses_ref[:, :count].reshape(count)
        loss[...] = losses_ref[:, count : count + 1].reshape(1)
        for k, vector in enumerate(vectors):
            vector[...] = vec_ref[k : k + 1, :].reshape(vector.shape)
        for j in range(inner // width):
            at = 8 + j
            b_in[pl.ds(j * width, width)] = vec_ref[at : at + 1, :].reshape(width)


def widen(ffo, rest, block, grad, vectors, losses, span_count):
    rows = block.shape[0]
    inner, width = ffo.shape
    steps = 2
    shape = jax.ShapeDtypeStruct

    def tiles(rows, cols):
        return pl.BlockSpec((rows // steps, cols), lambda i: (i, 0))

    def whole(*sizes):
        return pl.BlockSpec(sizes, lambda i: (0,) * len(sizes))

    flat = [span_count, 1, inner] + [width] * 8
    return pl.pallas_call(
        widen_kernel,
        grid=(steps,),
        out_shape=(
            shape((inner, width), f32),
            shape((width, inner), f32),
            shape((width, width), f32),
            shape((width, 3 * width), f32),
            shape(block.shape, block.dtype),
            shape(grad.shape, grad.dtype),
            *(shape((n,), f32) for n in flat),
        ),
        in_specs=[
            tiles(inner, width),
            tiles(width, rest.shape[1]),
            tiles(rows, width),
            tiles(rows, width),
            whole(*vectors.shape),
            whole(*losses.shape),
        ],
        out_specs=(
            tiles(inner, width),
            tiles(width, inner),
            tiles(width, width),
            tiles(width, 3 * width),
            tiles(rows, width),
            tiles(rows, width),
            *(whole(n) for n in flat),
        ),
        compiler_params=pltpu.CompilerParams(vmem_limit_bytes=60 * MIB),
        name="widen",
    )(ffo, rest, block, grad, vectors, losses)


def mesh_sizes():
    n_wide, n_narrow = lax.axis_size("wide"), lax.axis_size("narrow")
    n_y = n_narrow // 2
    n_x = n_y if n_wide % n_y == 0 else 1
    return n_wide // n_x, n_x, n_y


def per_device(
    hidden_in,
    out_grad,
    w_qkv,
    b_query,
    b_value,
    w_out,
    b_out,
    ln1_gain,
    ln1_bias,
    w_in,
    b_in,
    w_ff_out,
    b_ff_out,
    ln2_gain,
    ln2_bias,
    doc_count,
    single_flag,
):
    rows, width = hidden_in.shape
    span_count = rows // SPAN_LEN
    sizes = mesh_sizes()

    qkv, context, block_out, mixed_low, act, ffn_grad, hidden_grad, pre_one_grad, vectors, losses = middle(
        hidden_in, w_qkv, w_out, w_in, w_ff_out, out_grad, b_query, b_value, b_out, b_in, b_ff_out,
        ln1_gain, ln1_bias, ln2_gain, ln2_bias, doc_count, single_flag, sizes,
    )
    g_ffo, rest, grad_in, vectors = attend_back(
        act, hidden_grad, ffn_grad, mixed_low, pre_one_grad, context, qkv, hidden_in, w_out, w_qkv,
        vectors, sizes,
    )
    (
        g_ffo, g_in, g_out, g_qkv, block_out, grad_in, span_loss, loss, g_b_in, *rest_grads
    ) = widen(g_ffo, rest, block_out, grad_in, vectors, losses, span_count)
    g_b_query, g_b_value, g_b_out, g_gain_one, g_bias_one, g_b_ffo, g_gain_two, g_bias_two = rest_grads
    return (
        block_out,
        loss.reshape(()),
        span_loss,
        grad_in,
        g_qkv,
        g_b_query,
        g_b_value,
        g_out,
        g_b_out,
        g_gain_one,
        g_bias_one,
        g_in,
        g_b_in,
        g_ffo,
        g_b_ffo,
        g_gain_two,
        g_bias_two,
    )


def solution(mesh):
    placed = (
        P(("wide", "narrow"), None),
        P(("wide", "narrow"), None),
        P(),
        P(),
        P(),
        P(),
        P(),
        P(),
        P(),
        P(),
        P(),
        P(),
        P(),
        P(),
        P(),
        P(),
        P(),
    )
    return jax.shard_map(
        per_device,
        mesh=mesh,
        in_specs=placed,
        out_specs=(
            P(("wide", "narrow"), None),
            P(),
            P(("wide", "narrow")),
            P(("wide", "narrow"), None),
            P(),
            P(),
            P(),
            P(),
            P(),
            P(),
            P(),
            P(),
            P(),
            P(),
            P(),
            P(),
            P(),
        ),
        check_vma=False,
    )
```

```python
import functools

import jax
import jax.numpy as jnp
from jax import lax
from jax.experimental import pallas as pl
from jax.experimental.pallas import tpu as pltpu
from jax.sharding import PartitionSpec as P

HEAD_DIM = 64
SPAN_LEN = 128
TILE = 256

ln_eps = 1e-06
score_scale = 0.2
far_low = -1000000000.0
head_scale = HEAD_DIM ** (-0.5)
MESH = pl.DeviceIdType.MESH
TICKS = 6
f32, bf16, i32 = jnp.float32, jnp.bfloat16, jnp.int32
MIB = 2**20


def dot(left, right):
    return jnp.dot(left, right, preferred_element_type=f32)


def dot_left_t(left, right):
    return lax.dot_general(left, right, (((0,), (0,)), ((), ())), preferred_element_type=f32)


def dot_right_t(left, right):
    return lax.dot_general(left, right, (((1,), (1,)), ((), ())), preferred_element_type=f32)


def row_mean(values):
    return jnp.mean(values, axis=1, keepdims=True)


def col_sum(values):
    return jnp.sum(values, axis=0, keepdims=True)


def norm_back(upstream, normed, scale, gain):
    scaled = upstream * gain
    return scale * (scaled - row_mean(scaled) - normed * row_mean(scaled * normed))


def head_halves():
    first = lax.broadcasted_iota(i32, (1, 2 * HEAD_DIM), 1) < HEAD_DIM
    return first, first.astype(bf16), jnp.logical_not(first).astype(bf16)


def pair_probs(stacked_queries, keys_low):
    scores = dot_right_t(stacked_queries, keys_low)
    shifted = jnp.exp((scores - jnp.max(scores, axis=1, keepdims=True)) * head_scale)
    return shifted * (1.0 / jnp.sum(shifted, axis=1, keepdims=True))


def attend_tile(at, x_ref, w_qkv_ref, b_query, b_value, w_out_ref, b_out, qkv_ref, context_ref, cent_ref):
    width = x_ref.shape[1]
    inputs = x_ref[at, :]
    for third in range(3):
        cols = pl.ds(third * width, width)
        packed = dot(inputs, w_qkv_ref[:, cols])
        if third == 0:
            packed = packed + b_query
        if third == 2:
            packed = packed + b_value
        qkv_ref[at, cols] = packed.astype(bf16)
    first, low_one, low_two = head_halves()
    lanes = 2 * HEAD_DIM
    for span in range(at.size // SPAN_LEN):
        sp = pl.ds(pl.multiple_of(at.start + span * SPAN_LEN, SPAN_LEN), SPAN_LEN)
        for pair in range(width // lanes):
            queries = qkv_ref[sp, pl.ds(pair * lanes, lanes)]
            keys_low = qkv_ref[sp, pl.ds(width + pair * lanes, lanes)]
            values_low = qkv_ref[sp, pl.ds(2 * width + pair * lanes, lanes)]
            stacked = jnp.concatenate([queries * low_one, queries * low_two], axis=0)
            mixed_values = dot(pair_probs(stacked, keys_low).astype(bf16), values_low)
            context_ref[sp, pl.ds(pair * lanes, lanes)] = jnp.where(
                first, mixed_values[:SPAN_LEN], mixed_values[SPAN_LEN:]
            ).astype(bf16)
    pre_one = inputs.astype(f32) + (dot(context_ref[at, :], w_out_ref[...]) + b_out)
    cent_ref[at, :] = pre_one - row_mean(pre_one)


def gelu_parts(values):
    cdf = 0.5 * (1.0 + lax.erf(values * 0.7071067811865476))
    pdf = 0.3989422804014327 * jnp.exp(-0.5 * values * values)
    return values * cdf, cdf + values * pdf


def contrast_rows(cls_low, count, flags, first, span_count):
    total, width = cls_low.shape
    slots, docsets = flags.shape
    block = min(total, 256)

    def layout(at):
        slot = at + lax.broadcasted_iota(i32, (block, 1), 0)
        device = slot // slots
        place = (slot - device * slots).astype(f32)
        member = lax.broadcasted_iota(i32, (block, docsets), 1) == device
        docs = jnp.sum(jnp.where(member, count, 0.0), axis=1, keepdims=True)
        single = dot_right_t(member.astype(bf16), flags.astype(bf16))
        doc = lax.broadcasted_iota(i32, (block, slots), 1).astype(f32)
        length = jnp.where(doc < docs, 2.0 - single, 0.0)
        earlier = lax.broadcasted_iota(i32, (slots, slots), 0) < lax.broadcasted_iota(
            i32, (slots, slots), 1
        )
        begins = dot(length.astype(bf16), earlier.astype(f32).astype(bf16))
        inside = (place >= begins) & (place < begins + length)
        double = inside & (length == 2.0)
        live = jnp.max(inside.astype(f32), axis=1, keepdims=True)
        pair = jnp.max(double.astype(f32), axis=1, keepdims=True)
        other = jnp.sum(jnp.where(double, 2.0 * begins + 1.0 - place, 0.0), axis=1, keepdims=True)
        mate = jnp.where(pair > 0.0, (device * slots).astype(f32) + other, slot.astype(f32))
        return slot.astype(f32), live, pair, mate

    eye = lax.broadcasted_iota(i32, (block, block), 0) == lax.broadcasted_iota(
        i32, (block, block), 1
    )
    live_row = jnp.concatenate(
        [col_sum(jnp.where(eye, layout(at)[1], 0.0)) for at in range(0, total, block)], axis=1
    )
    column = lax.broadcasted_iota(i32, (block, total), 1).astype(f32)
    pick_col = (
        lax.broadcasted_iota(i32, (span_count, total), 1)
        == first + lax.broadcasted_iota(i32, (span_count, total), 0)
    ).astype(f32).astype(bf16)
    rows_own = jnp.zeros((span_count, total), f32)
    upward = jnp.zeros((span_count, width), f32)
    own_loss = jnp.zeros((1, span_count), f32)
    loss = jnp.zeros((1, 1), f32)
    for at in range(0, total, block):
        slot, live, pair, mate = layout(at)
        cls_block = cls_low[at : at + block, :]
        sims = score_scale * dot_right_t(cls_block, cls_low)
        allowed = (live_row > 0.0) & (column != slot)
        masked = jnp.where(allowed, sims, far_low)
        top = jnp.max(masked, axis=1, keepdims=True)
        lse = top + jnp.log(jnp.sum(jnp.exp(masked - top), axis=1, keepdims=True))
        matches = column == mate
        positive = jnp.sum(jnp.where(matches, sims, 0.0), axis=1, keepdims=True)
        span_loss = jnp.where(pair > 0.0, lse - positive, 0.0)
        loss = loss + col_sum(span_loss)
        mine = at + lax.broadcasted_iota(i32, (block, span_count), 0) == (
            first + lax.broadcasted_iota(i32, (block, span_count), 1)
        )
        own_loss = own_loss + col_sum(jnp.where(mine, span_loss, 0.0))
        sim_grad = jnp.where(
            pair > 0.0, jnp.exp(masked - lse) - matches.astype(f32), 0.0
        ).astype(bf16)
        pick_row = (
            at + lax.broadcasted_iota(i32, (span_count, block), 1)
            == first + lax.broadcasted_iota(i32, (span_count, block), 0)
        ).astype(f32).astype(bf16)
        rows_own = rows_own + dot(pick_row, sim_grad)
        cols_own = dot_right_t(pick_col, sim_grad)
        upward = upward + dot(cols_own.astype(bf16), cls_block)
    upward = upward + dot(rows_own.astype(bf16), cls_low)
    return score_scale * upward, own_loss, loss


def middle_kernel(
    n_z,
    n_x,
    n_y,
    x_hbm,
    w_qkv_hbm,
    w_out_hbm,
    w_in_hbm,
    w_ffo_hbm,
    out_grad_hbm,
    b_query_ref,
    b_value_ref,
    b_out_ref,
    b_in_ref,
    b_ffo_ref,
    gain_one_ref,
    bias_one_ref,
    gain_two_ref,
    bias_two_ref,
    count_ref,
    flag_ref,
    qkv_hbm,
    context_hbm,
    block_hbm,
    mixed_hbm,
    act_hbm,
    ffn_grad_hbm,
    hidden_grad_hbm,
    pre_grad_hbm,
    vec_ref,
    losses_ref,
    x_v,
    w_qkv,
    w_out,
    qkv_v,
    context_v,
    cent_v,
    w_in,
    w_ffo,
    upper_v,
    block_v,
    mixed_v,
    act_v,
    slope_v,
    ffn_grad_v,
    two_v,
    first_v,
    cls_grad_v,
    b_in_v,
    cls_v,
    in_sem,
    out_sem,
    s_sem,
    r_sem,
):
    rows, width = cent_v.shape
    inner = w_in.shape[1]
    chunks = inner // width
    tiles = rows // TILE
    span_count = rows // SPAN_LEN
    wide, narrow = lax.axis_index("wide"), lax.axis_index("narrow")
    z, x = wide // n_x, lax.rem(wide, n_x)
    y, c = narrow // 2, lax.rem(narrow, 2)
    core = (wide, y * 2 + 1 - c)
    along_x = [(z * n_x + lax.rem(x + k, n_x), narrow) for k in range(1, n_x)]
    along_y = [(wide, lax.rem(y + k, n_y) * 2 + c) for k in range(1, n_y)]
    along_z = [(lax.rem(z + k, n_z) * n_x + x, narrow) for k in range(1, n_z)]
    partners = [core] + along_x + along_y + along_z

    barrier = pltpu.get_barrier_semaphore()
    for device in partners:
        pl.semaphore_signal(barrier, inc=1, device_id=device, device_id_type=MESH)

    loads = [
        pltpu.make_async_copy(src, dst, in_sem.at[k])
        for k, (src, dst) in enumerate(
            (
                (x_hbm, x_v),
                (w_qkv_hbm, w_qkv),
                (w_out_hbm, w_out),
                (w_in_hbm, w_in),
                (w_ffo_hbm, w_ffo),
                (out_grad_hbm, upper_v),
            )
        )
    ]
    for copy in loads:
        copy.start()

    def row(ref, at=0):
        return ref[pl.ds(at, width)].astype(f32).reshape(1, width)

    gain_one, bias_one, gain_two, bias_two, b_ffo = (
        row(r) for r in (gain_one_ref, bias_one_ref, gain_two_ref, bias_two_ref, b_ffo_ref)
    )
    for j in range(chunks):
        b_in_v[j : j + 1, :] = row(b_in_ref, j * width)

    def normed(cent):
        scale = lax.rsqrt(row_mean(cent * cent) + ln_eps)
        return cent * scale, scale

    def feed_forward(mixed, total, keep):
        mixed_low = mixed.astype(bf16)
        total[...] = mixed + b_ffo

        def step(j, carry):
            cols = pl.ds(pl.multiple_of(j * width, width), width)
            hidden = dot(mixed_low, w_in[:, cols]) + b_in_v[pl.ds(j, 1), :]
            act, slope = gelu_parts(hidden)
            act_low = act.astype(bf16)
            keep(cols, act_low, slope)
            total[...] += dot(act_low, w_ffo[cols, :])
            return carry

        lax.fori_loop(0, chunks, step, 0, unroll=True)
        pre_two = total[...]
        return pre_two - row_mean(pre_two)

    b_query, b_value, b_out = (row(r) for r in (b_query_ref, b_value_ref, b_out_ref))

    def store(src, dst, at, k):
        return pltpu.make_async_copy(src.at[at, :], dst.at[at, :], out_sem.at[k])

    def tile_rows(tile):
        return pl.ds(pl.multiple_of(tile * TILE, TILE), TILE)

    def attend_stores(tile):
        at = tile_rows(tile)
        return [
            store(qkv_v, qkv_hbm, at, 8 * tile + 6),
            store(context_v, context_hbm, at, 8 * tile + 7),
        ]

    def attend_step(tile, carry):
        attend_tile(
            tile_rows(tile), x_v, w_qkv, b_query, b_value, w_out, b_out, qkv_v, context_v, cent_v
        )
        for copy in attend_stores(tile):
            copy.start()
        return carry

    for copy in loads[:3]:
        copy.wait()
    lax.fori_loop(0, tiles, attend_step, 0)

    first_cent = jnp.concatenate(
        [cent_v[s * SPAN_LEN : s * SPAN_LEN + 1, :] for s in range(span_count)], axis=0
    )
    first_mixed = normed(first_cent)[0] * gain_one + bias_one
    loads[3].wait()
    loads[4].wait()
    first_two = feed_forward(first_mixed, first_v, lambda cols, act, slope: None)
    first_out = normed(first_two)[0] * gain_two + bias_two
    half = width // 2
    cls_v[z, x, y, c] = jnp.concatenate([first_out[:, :half], first_out[:, half:]], axis=0).astype(
        bf16
    )
    pl.semaphore_wait(barrier, len(partners))

    def gathers(stage):
        if stage == 0:
            ref, devices, base = cls_v.at[z, x, y, c], along_z, 0
        elif stage == 1:
            ref, devices, base = cls_v.at[:, x, y, c], along_x, n_z - 1
        elif stage == 2:
            ref, devices, base = cls_v.at[:, :, y, c], along_y, n_z + n_x - 2
        else:
            ref, devices, base = cls_v.at[:, :, :, c], [core], n_z + n_x + n_y - 3
        return [
            pltpu.make_async_remote_copy(
                ref, ref, s_sem.at[base + k], r_sem.at[base + k], device_id=d, device_id_type=MESH
            )
            for k, d in enumerate(devices)
        ]

    for copy in gathers(0):
        copy.start()
    loads[5].wait()

    def forward_stores(tile):
        at = tile_rows(tile)
        return [
            store(mixed_v, mixed_hbm, at, 8 * tile),
            store(block_v, block_hbm, at, 8 * tile + 1),
            store(act_v, act_hbm, at, 8 * tile + 2),
        ]

    def backward_stores(tile):
        at = tile_rows(tile)
        return [
            store(ffn_grad_v, ffn_grad_hbm, at, 8 * tile + 3),
            store(slope_v, hidden_grad_hbm, at, 8 * tile + 4),
            store(cent_v, pre_grad_hbm, at, 8 * tile + 5),
        ]

    def forward_tile(tile, carry):
        at = tile_rows(tile)
        mixed = normed(cent_v[at, :])[0] * gain_one + bias_one
        mixed_v[at, :] = mixed.astype(bf16)

        def keep(cols, act_low, slope):
            act_v[at, cols] = act_low
            slope_v[at, cols] = slope.astype(bf16)

        cent_two = feed_forward(mixed, two_v.at[at, :], keep)
        block_v[at, :] = (normed(cent_two)[0] * gain_two + bias_two).astype(bf16)
        two_v[at, :] = cent_two
        for copy in forward_stores(tile):
            copy.start()
        for stage in range(4):

            @pl.when(tile == min(stage, tiles - 1))
            def _():
                for copy in gathers(stage):
                    copy.wait()
                if stage < 3:
                    for copy in gathers(stage + 1):
                        copy.start()

        return carry

    lax.fori_loop(0, tiles, forward_tile, 0)

    low = cls_v[...].astype(f32).reshape(-1, 2 * span_count, half)
    cls_low = jnp.concatenate(
        [
            low[:, :span_count, :].reshape(-1, half),
            low[:, span_count:, :].reshape(-1, half),
        ],
        axis=1,
    ).astype(bf16)
    own = wide * (2 * n_y) + narrow
    cls_grad, own_loss, loss = contrast_rows(
        cls_low, count_ref[...].astype(f32).reshape(1, -1), flag_ref[...].astype(f32), own * span_count, span_count
    )
    cls_grad_v[...] = cls_grad
    lane = lax.broadcasted_iota(i32, losses_ref.shape, 1)
    losses_ref[...] = jnp.where(lane == span_count, loss, 0.0)
    losses_ref[:, :span_count] = own_loss

    vec_ref[...] = jnp.zeros(vec_ref.shape, f32)

    def add_row(k, values):
        vec_ref[pl.ds(k, 1), :] += col_sum(values)

    def backward_tile(tile, carry):
        at = tile_rows(tile)
        upper = upper_v[at, :].astype(f32)
        place = lax.broadcasted_iota(i32, (TILE, 1), 0)
        for span in range(TILE // SPAN_LEN):
            upper = jnp.where(
                place == span * SPAN_LEN,
                cls_grad_v[pl.ds(tile * (TILE // SPAN_LEN) + span, 1), :],
                upper,
            )
        normed_two, scale_two = normed(two_v[at, :])
        add_row(6, upper * normed_two)
        add_row(7, upper)
        pre_two_grad = norm_back(upper, normed_two, scale_two, gain_two)
        ffn_grad = pre_two_grad.astype(bf16)
        ffn_grad_v[at, :] = ffn_grad
        add_row(5, ffn_grad.astype(f32))
        two_v[at, :] = pre_two_grad

        def step(j, inner_carry):
            cols = pl.ds(pl.multiple_of(j * width, width), width)
            back = dot_right_t(ffn_grad, w_ffo[cols, :]) * slope_v[at, cols].astype(f32)
            hidden_grad = back.astype(bf16)
            slope_v[at, cols] = hidden_grad
            add_row(8 + j, hidden_grad.astype(f32))
            two_v[at, :] += dot_right_t(hidden_grad, w_in[:, cols])
            return inner_carry

        lax.fori_loop(0, chunks, step, 0, unroll=True)
        mixed_grad = two_v[at, :]
        normed_one, scale_one = normed(cent_v[at, :])
        add_row(3, mixed_grad * normed_one)
        add_row(4, mixed_grad)
        pre_one_grad = norm_back(mixed_grad, normed_one, scale_one, gain_one)
        cent_v[at, :] = pre_one_grad
        add_row(2, pre_one_grad.astype(bf16).astype(f32))
        for copy in backward_stores(tile):
            copy.start()
        return carry

    lax.fori_loop(0, tiles, backward_tile, 0)

    for tile in range(tiles):
        for copy in attend_stores(tile) + forward_stores(tile) + backward_stores(tile):
            copy.wait()


def middle(
    x,
    w_qkv,
    w_out,
    w_in,
    w_ffo,
    out_grad,
    b_query,
    b_value,
    b_out,
    b_in,
    b_ffo,
    gain_one,
    bias_one,
    gain_two,
    bias_two,
    doc_count,
    single_flag,
    sizes,
):
    rows, width = x.shape
    inner = w_in.shape[1]
    span_count = rows // SPAN_LEN
    n_z, n_x, n_y = sizes
    moves = n_z + n_x + n_y - 2
    hbm = pl.BlockSpec(memory_space=pl.ANY)
    vmem = pl.BlockSpec(memory_space=pltpu.VMEM)
    shape = jax.ShapeDtypeStruct
    return pl.pallas_call(
        functools.partial(middle_kernel, n_z, n_x, n_y),
        out_shape=(
            shape((rows, 3 * width), bf16),
            shape((rows, width), bf16),
            shape((rows, width), bf16),
            shape((rows, width), bf16),
            shape((rows, inner), bf16),
            shape((rows, width), bf16),
            shape((rows, inner), bf16),
            shape((rows, width), f32),
            shape((16, width), f32),
            shape((1, 128), f32),
        ),
        in_specs=[hbm] * 6 + [vmem] * 11,
        out_specs=(hbm,) * 8 + (vmem,) * 2,
        scratch_shapes=[
            pltpu.VMEM((rows, width), bf16),
            pltpu.VMEM((width, 3 * width), bf16),
            pltpu.VMEM((width, width), bf16),
            pltpu.VMEM((rows, 3 * width), bf16),
            pltpu.VMEM((rows, width), bf16),
            pltpu.VMEM((rows, width), f32),
            pltpu.VMEM((width, inner), bf16),
            pltpu.VMEM((inner, width), bf16),
            pltpu.VMEM((rows, width), bf16),
            pltpu.VMEM((rows, width), bf16),
            pltpu.VMEM((rows, width), bf16),
            pltpu.VMEM((rows, inner), bf16),
            pltpu.VMEM((rows, inner), bf16),
            pltpu.VMEM((rows, width), bf16),
            pltpu.VMEM((rows, width), f32),
            pltpu.VMEM((span_count, width), f32),
            pltpu.VMEM((span_count, width), f32),
            pltpu.VMEM((inner // width, width), f32),
            pltpu.VMEM((n_z, n_x, n_y, 2, 2 * span_count, width // 2), bf16),
            pltpu.SemaphoreType.DMA((6,)),
            pltpu.SemaphoreType.DMA((8 * (rows // TILE),)),
            pltpu.SemaphoreType.DMA((moves,)),
            pltpu.SemaphoreType.DMA((moves,)),
        ],
        compiler_params=pltpu.CompilerParams(
            collective_id=1, has_side_effects=True, vmem_limit_bytes=60 * MIB
        ),
        name="forward_and_loss",
    )(
        x, w_qkv, w_out, w_in, w_ffo, out_grad, b_query, b_value, b_out, b_in, b_ffo, gain_one, bias_one,
        gain_two, bias_two, doc_count, single_flag.T,
    )


def attend_back_kernel(
    n_z,
    n_x,
    comm,
    order,
    act_hbm,
    hidden_grad_hbm,
    ffn_grad_hbm,
    mixed_hbm,
    pre_grad_hbm,
    context_hbm,
    qkv_hbm,
    x_hbm,
    w_out_hbm,
    w_qkv_hbm,
    vec_ref,
    o_ffo,
    o_rest,
    grad_in_hbm,
    o_vec,
    stream,
    ffn_grad_v,
    mixed_v,
    pre_v,
    context_v,
    qkv_v,
    x_v,
    w_out,
    w_qkv,
    attn_v,
    context_grad_v,
    part,
    sib,
    r1,
    r2,
    r3,
    vbuf,
    in_sem,
    out_sem,
    s_sem,
    r_sem,
    zs_sem,
    zr_sem,
    vs_sem,
    vr_sem,
):
    rows, width = x_v.shape
    half, quarter = width // 2, width // 4
    eighth = quarter // n_z
    tiles = rows // TILE
    ahead = stream.shape[0]
    wide, narrow = lax.axis_index("wide"), lax.axis_index("narrow")
    z, x = wide // n_x, lax.rem(wide, n_x)
    y, c = narrow // 2, lax.rem(narrow, 2)
    core = (wide, y * 2 + 1 - c)
    near_x = (z * n_x + 1 - x, narrow)
    near_y = (wide, (1 - y) * 2 + c)
    one = tuple(jnp.where(c == 0, a, b) for a, b in zip(near_x, near_y))
    two = tuple(jnp.where(c == 0, b, a) for a, b in zip(near_x, near_y))
    h1 = jnp.where(c == 0, x, y)
    h2 = jnp.where(c == 0, y, x)
    others = [lax.rem(z + k, n_z) for k in range(1, n_z)]
    along_z = [(o * n_x + x, narrow) for o in others]

    if comm:
        barrier = pltpu.get_barrier_semaphore()
        for device in [core, near_x, near_y] + along_z:
            pl.semaphore_signal(barrier, inc=1, device_id=device, device_id_type=MESH)

    def stream_load(j):
        src = act_hbm if j < 4 else hidden_grad_hbm
        return pltpu.make_async_copy(
            src.at[:, pl.ds((j % 4) * width, width)], stream.at[j % ahead], in_sem.at[j]
        )

    resident = [
        pltpu.make_async_copy(src, dst, in_sem.at[8 + k])
        for k, (src, dst) in enumerate(
            (
                (ffn_grad_hbm, ffn_grad_v),
                (mixed_hbm, mixed_v),
                (pre_grad_hbm, pre_v),
                (w_out_hbm, w_out),
                (qkv_hbm, qkv_v),
                (w_qkv_hbm, w_qkv),
                (context_hbm, context_v),
                (x_hbm, x_v),
            )
        )
    ]
    stream_load(0).start()
    resident[0].start()
    for j in range(1, ahead):
        stream_load(j).start()
    for copy in resident[1:]:
        copy.start()
    vbuf[0] = vec_ref[...]
    waited = set()

    def need(*which):
        for k in which:
            if k not in waited:
                waited.add(k)
                resident[k].wait()

    first, low_one, low_two = head_halves()
    lanes = 2 * HEAD_DIM

    def weight_block(b):
        pair, second = b // 2, b % 2
        which = c if second else 1 - c
        block = b if pair == 4 else 2 * pair + which
        if b < 8:
            if not second:
                stream_load(b).wait()
                stream_load(b + 1).wait()
            streamed = stream.at[b // 2 * 2 % ahead + which]
        if b < 4:
            need(0)
            left, right = streamed, ffn_grad_v
        elif b < 8:
            need(1)
            left, right = mixed_v, streamed
        elif b < 9:
            need(6)
            left, right = context_v, attn_v
        else:
            need(7)
            cols = pl.multiple_of((block - 9) * width, 128)
            left, right = x_v, qkv_v.at[:, pl.ds(cols, width)]

        def step(i, carry):
            at = pl.ds(pl.multiple_of(i * TILE, TILE), TILE)
            part[block, at, :] = dot_left_t(left[:, at], right[...]).astype(bf16)
            return carry

        lax.fori_loop(0, width // TILE, step, 0, unroll=True)
        if second and b - 1 + ahead < 8:
            stream_load(b - 1 + ahead).start()
            stream_load(b + ahead).start()

    def grad_in_store(tile):
        at = pl.ds(tile * TILE, TILE)
        return pltpu.make_async_copy(pre_v.at[at, :], grad_in_hbm.at[at, :], out_sem.at[tile])

    def attend_tile(tile, piece):
        need(2, 3, 4, 5)
        at = pl.ds(tile * TILE, TILE)
        if piece == 0:
            attn_grad = pre_v[at, :].astype(bf16)
            attn_v[at, :] = attn_grad
            context_grad_v[...] = dot_right_t(attn_grad, w_out[...]).astype(bf16)
        if piece == 2:
            vbuf[0, 0:1, :] += col_sum(qkv_v[at, 0:width].astype(f32))
            vbuf[0, 1:2, :] += col_sum(qkv_v[at, 2 * width : 3 * width].astype(f32))
            pre_v[at, :] += dot_right_t(qkv_v[at, :], w_qkv[...])
            grad_in_store(tile).start()
            return

        def pair_step(pair):
            q_at, k_at, v_at = (pl.ds(third * width + pair * lanes, lanes) for third in range(3))
            for span in range(TILE // SPAN_LEN):
                sp = pl.ds(tile * TILE + span * SPAN_LEN, SPAN_LEN)
                queries, keys_low, values_low = qkv_v[sp, q_at], qkv_v[sp, k_at], qkv_v[sp, v_at]
                upper = context_grad_v[pl.ds(span * SPAN_LEN, SPAN_LEN), q_at]
                stacked = jnp.concatenate([queries * low_one, queries * low_two], axis=0)
                stacked_up = jnp.concatenate([upper * low_one, upper * low_two], axis=0)
                scores = dot_right_t(keys_low, stacked)
                shifted = jnp.exp((scores - jnp.max(scores, axis=0, keepdims=True)) * head_scale)
                probs = shifted * (1.0 / col_sum(shifted))
                value_grad = dot(probs.astype(bf16), stacked_up)
                prob_grad = dot_right_t(values_low, stacked_up)
                score_grad = (probs * (prob_grad - col_sum(probs * prob_grad))).astype(bf16)
                query_grad = dot_left_t(score_grad, keys_low) * head_scale
                key_grad = dot(score_grad, stacked) * head_scale
                qkv_v[sp, q_at] = jnp.where(
                    first, query_grad[:SPAN_LEN], query_grad[SPAN_LEN:]
                ).astype(bf16)
                qkv_v[sp, k_at] = key_grad.astype(bf16)
                qkv_v[sp, v_at] = value_grad.astype(bf16)

        pairs = width // lanes
        for pair in range(pairs // 2) if piece == 0 else range(pairs // 2, pairs):
            pair_step(pair)

    def out_at(t, row, count):
        if t < 2:
            at = pl.multiple_of((2 * t + c) * width + row, 16)
            return o_ffo.at[pl.ds(at, count), :]
        cols = pl.multiple_of((2 * (t - 2) + c) * width, 128)
        return o_rest.at[pl.ds(pl.multiple_of(row, 16), count), pl.ds(cols, width)]

    def part_at(t, row, count):
        return part.at[2 * t + c, pl.ds(pl.multiple_of(row, 16), count), :]

    keep1 = h1 * half
    keep2 = keep1 + h2 * quarter
    own = keep2 + z * eighth

    def send(src, dst, stage, t, device):
        return pltpu.make_async_remote_copy(
            src, dst, s_sem.at[stage, t], r_sem.at[stage, t], device_id=device, device_id_type=MESH
        )

    def send_z(src, dst, stage, t, k):
        return pltpu.make_async_remote_copy(
            src,
            dst,
            zs_sem.at[stage, t, k],
            zr_sem.at[stage, t, k],
            device_id=along_z[k],
            device_id_type=MESH,
        )

    def sibling_slot(t, of):
        return sib.at[t] if t < 2 else part.at[2 * (t - 2) + 1 - of]

    def copies(stage, t):
        if stage == 0:
            return [send(part.at[2 * t + 1 - c], sibling_slot(t, 1 - c), 0, t, core)]
        if stage == 1:
            return [send(part_at(t, (1 - h1) * half, half), r1.at[t], 1, t, one)]
        if stage == 2:
            return [send(part_at(t, keep1 + (1 - h2) * quarter, quarter), r2.at[t], 2, t, two)]
        if stage == 3:
            return [
                send_z(part_at(t, keep2 + o * eighth, eighth), r3.at[t, k], 0, t, k)
                for k, o in enumerate(others)
            ]
        if stage == 4:
            return [
                send_z(part_at(t, own, eighth), out_at(t, own, eighth), 1, t, k)
                for k in range(n_z - 1)
            ]
        if stage == 5:
            place = out_at(t, keep2, quarter)
            return [send(place, place, 3, t, two)]
        if stage == 6:
            place = out_at(t, keep1, half)
            return [send(place, place, 4, t, one)]
        place = out_at(t, 0, width)
        return [send(place, place, 5, t, core)]

    def add(t, row, count, got):
        def step(i, carry):
            at = pl.ds(pl.multiple_of(row + i * 48, 16), 48)
            here = part[2 * t + c, at, :].astype(f32) + got[
                pl.ds(pl.multiple_of(i * 48, 16), 48), :
            ].astype(f32)
            part[2 * t + c, at, :] = here.astype(bf16)
            return carry

        lax.fori_loop(0, count // 48, step, 0)

    def own_store(t):
        return pltpu.make_async_copy(
            part_at(t, own, eighth), out_at(t, own, eighth), out_sem.at[tiles + t]
        )

    def advance(stage, t):
        if stage > 0:
            for copy in copies(stage - 1, t):
                copy.wait()
        if stage == 1:
            add(t, 0, width, sibling_slot(t, c))
        elif stage == 2:
            add(t, keep1, half, r1.at[t])
        elif stage == 3:
            add(t, keep2, quarter, r2.at[t])
        elif stage == 4:
            total = part_at(t, own, eighth)[...].astype(f32)
            for k in range(n_z - 1):
                total = total + r3[t, k].astype(f32)
            part_at(t, own, eighth)[...] = total.astype(bf16)
            own_store(t).start()
        elif stage == 5:
            own_store(t).wait()
        if stage < 8:
            for copy in copies(stage, t):
                copy.start()

    def vector_copies(k):
        if k < 3:
            device = (core, near_x, near_y)[k]
            ends = [(vbuf.at[2 * k], vbuf.at[2 * k + 1], k, device)]
        else:
            ends = [(vbuf.at[6], vbuf.at[7 + i], 3 + i, d) for i, d in enumerate(along_z)]
        return [
            pltpu.make_async_remote_copy(
                src, dst, vs_sem.at[s], vr_sem.at[s], device_id=d, device_id_type=MESH
            )
            for src, dst, s, d in ends
        ]

    def vector_step(k):
        if k > 0:
            for copy in vector_copies(k - 1):
                copy.wait()
        if k in (1, 2, 3):
            vbuf[2 * k] = vbuf[2 * k - 2] + vbuf[2 * k - 1]
        if k < 4:
            for copy in vector_copies(k):
                copy.start()
        else:
            total = vbuf[6]
            for i in range(n_z - 1):
                total = total + vbuf[7 + i]
            o_vec[...] = total

    entered = False
    for kind, *at in order:
        if kind == "w":
            weight_block(*at)
        elif kind == "a":
            attend_tile(*at)
        elif comm:
            if not entered:
                pl.semaphore_wait(barrier, 2 + n_z)
                entered = True
            if kind == "s":
                advance(*at)
            else:
                vector_step(*at)
    if not comm:
        o_vec[...] = vbuf[0]
        locals_ = [
            pltpu.make_async_copy(
                part.at[b],
                o_ffo.at[pl.ds(b * width, width), :]
                if b < 4
                else o_rest.at[:, pl.ds((b - 4) * width, width)],
                in_sem.at[b],
            )
            for b in range(2 * TICKS)
        ]
        for copy in locals_:
            copy.start()
        for copy in locals_:
            copy.wait()
    for tile in range(tiles):
        grad_in_store(tile).wait()


def schedule():
    return [
        ("w", 0), ("s", 0, 0), ("w", 1), ("w", 2), ("s", 1, 0), ("w", 3), ("s", 0, 1), ("w", 4),
        ("w", 5), ("s", 1, 1), ("w", 6), ("s", 0, 2), ("w", 7), ("s", 2, 0), ("a", 0, 0),
        ("a", 0, 1), ("s", 1, 2), ("s", 3, 0), ("s", 0, 3), ("a", 0, 2), ("a", 1, 0), ("s", 2, 1),
        ("a", 1, 1), ("s", 4, 0), ("s", 1, 3), ("s", 2, 2), ("a", 1, 2), ("s", 3, 1), ("a", 2, 0),
        ("a", 2, 1), ("a", 2, 2), ("s", 5, 0), ("a", 3, 0), ("s", 4, 1), ("s", 2, 3), ("s", 6, 0),
        ("a", 3, 1), ("s", 3, 2), ("a", 3, 2), ("w", 8), ("v", 0), ("w", 9), ("s", 0, 4),
        ("s", 5, 1), ("w", 10), ("v", 1), ("s", 3, 3), ("s", 1, 4), ("w", 11), ("s", 0, 5),
        ("v", 2), ("s", 4, 2), ("s", 1, 5), ("s", 2, 4), ("s", 4, 3), ("v", 3), ("s", 5, 2),
        ("s", 3, 4), ("s", 6, 1), ("s", 2, 5), ("v", 4), ("s", 5, 3), ("s", 4, 4), ("s", 7, 0),
        ("s", 3, 5), ("s", 6, 3), ("s", 6, 2), ("s", 5, 4), ("s", 7, 1), ("s", 4, 5), ("s", 6, 4),
        ("s", 8, 0), ("s", 5, 5), ("s", 7, 2), ("s", 7, 3), ("s", 6, 5), ("s", 8, 3), ("s", 7, 4),
        ("s", 7, 5), ("s", 8, 4), ("s", 8, 1), ("s", 8, 2), ("s", 8, 5),
    ]


def attend_back(act, hidden_grad, ffn_grad, mixed_low, pre_grad, context, qkv, x, w_out, w_qkv, vectors, sizes, order=None):
    rows, width = x.shape
    inner = act.shape[1]
    n_z, n_x, n_y = sizes
    comm = n_x == 2 and n_y == 2 and width % (64 * n_z) == 0
    hbm = pl.BlockSpec(memory_space=pl.ANY)
    vmem = pl.BlockSpec(memory_space=pltpu.VMEM)
    shape = jax.ShapeDtypeStruct
    tiles = rows // TILE
    scratch = [
        pltpu.VMEM((4, rows, width), bf16),
        pltpu.VMEM((rows, width), bf16),
        pltpu.VMEM((rows, width), bf16),
        pltpu.VMEM((rows, width), f32),
        pltpu.VMEM((rows, width), bf16),
        pltpu.VMEM((rows, 3 * width), bf16),
        pltpu.VMEM((rows, width), bf16),
        pltpu.VMEM((width, width), bf16),
        pltpu.VMEM((width, 3 * width), bf16),
        pltpu.VMEM((rows, width), bf16),
        pltpu.VMEM((TILE, width), bf16),
        pltpu.VMEM((2 * TICKS, width, width), bf16),
        pltpu.VMEM((2, width, width), bf16),
        pltpu.VMEM((TICKS, width // 2, width), bf16),
        pltpu.VMEM((TICKS, width // 4, width), bf16),
        pltpu.VMEM((TICKS, n_z - 1, width // 4 // n_z, width), bf16),
        pltpu.VMEM((6 + n_z,) + vectors.shape, f32),
        pltpu.SemaphoreType.DMA((16,)),
        pltpu.SemaphoreType.DMA((tiles + TICKS,)),
        pltpu.SemaphoreType.DMA((6, TICKS)),
        pltpu.SemaphoreType.DMA((6, TICKS)),
        pltpu.SemaphoreType.DMA((2, TICKS, n_z - 1)),
        pltpu.SemaphoreType.DMA((2, TICKS, n_z - 1)),
        pltpu.SemaphoreType.DMA((2 + n_z,)),
        pltpu.SemaphoreType.DMA((2 + n_z,)),
    ]
    params = dict(vmem_limit_bytes=60 * MIB)
    if comm:
        params.update(collective_id=0, has_side_effects=True)
    g_ffo, rest, grad_in, vectors = pl.pallas_call(
        functools.partial(attend_back_kernel, n_z, n_x, comm, order or schedule()),
        out_shape=(
            shape((inner, width), bf16),
            shape((width, inner + 4 * width), bf16),
            shape((rows, width), f32),
            shape(vectors.shape, f32),
        ),
        in_specs=[hbm] * 10 + [vmem],
        out_specs=(hbm, hbm, hbm, vmem),
        scratch_shapes=scratch,
        compiler_params=pltpu.CompilerParams(**params),
        name="attend_back_and_sums",
    )(act, hidden_grad, ffn_grad, mixed_low, pre_grad, context, qkv, x, w_out, w_qkv, vectors)
    if not comm:
        g_ffo, rest, vectors = lax.psum((g_ffo, rest, vectors), ("wide", "narrow"))
    return g_ffo, rest, grad_in, vectors


def widen_kernel(
    ffo_ref,
    rest_ref,
    block_ref,
    grad_ref,
    vec_ref,
    losses_ref,
    w_ffo,
    w_in,
    w_out,
    w_qkv,
    block,
    grad,
    span_loss,
    loss,
    b_in,
    *vectors,
):
    inner, width = w_in.shape[1], w_out.shape[1]
    block[...] = block_ref[...]
    grad[...] = grad_ref[...]
    w_ffo[...] = ffo_ref[...].astype(f32)
    w_in[...] = rest_ref[:, :inner].astype(f32)
    w_out[...] = rest_ref[:, inner : inner + width].astype(f32)
    w_qkv[...] = rest_ref[:, inner + width :].astype(f32)

    @pl.when(pl.program_id(0) == 0)
    def _():
        count = span_loss.shape[0]
        span_loss[...] = losses_ref[:, :count].reshape(count)
        loss[...] = losses_ref[:, count : count + 1].reshape(1)
        for k, vector in enumerate(vectors):
            vector[...] = vec_ref[k : k + 1, :].reshape(vector.shape)
        for j in range(inner // width):
            at = 8 + j
            b_in[pl.ds(j * width, width)] = vec_ref[at : at + 1, :].reshape(width)


def widen(ffo, rest, block, grad, vectors, losses, span_count):
    rows = block.shape[0]
    inner, width = ffo.shape
    steps = 2
    shape = jax.ShapeDtypeStruct

    def tiles(rows, cols):
        return pl.BlockSpec((rows // steps, cols), lambda i: (i, 0))

    def whole(*sizes):
        return pl.BlockSpec(sizes, lambda i: (0,) * len(sizes))

    flat = [span_count, 1, inner] + [width] * 8
    return pl.pallas_call(
        widen_kernel,
        grid=(steps,),
        out_shape=(
            shape((inner, width), f32),
            shape((width, inner), f32),
            shape((width, width), f32),
            shape((width, 3 * width), f32),
            shape(block.shape, block.dtype),
            shape(grad.shape, grad.dtype),
            *(shape((n,), f32) for n in flat),
        ),
        in_specs=[
            tiles(inner, width),
            tiles(width, rest.shape[1]),
            tiles(rows, width),
            tiles(rows, width),
            whole(*vectors.shape),
            whole(*losses.shape),
        ],
        out_specs=(
            tiles(inner, width),
            tiles(width, inner),
            tiles(width, width),
            tiles(width, 3 * width),
            tiles(rows, width),
            tiles(rows, width),
            *(whole(n) for n in flat),
        ),
        compiler_params=pltpu.CompilerParams(vmem_limit_bytes=60 * MIB),
        name="widen",
    )(ffo, rest, block, grad, vectors, losses)


def mesh_sizes():
    n_wide, n_narrow = lax.axis_size("wide"), lax.axis_size("narrow")
    n_y = n_narrow // 2
    n_x = n_y if n_wide % n_y == 0 else 1
    return n_wide // n_x, n_x, n_y


def per_device(
    hidden_in,
    out_grad,
    w_qkv,
    b_query,
    b_value,
    w_out,
    b_out,
    ln1_gain,
    ln1_bias,
    w_in,
    b_in,
    w_ff_out,
    b_ff_out,
    ln2_gain,
    ln2_bias,
    doc_count,
    single_flag,
):
    rows, width = hidden_in.shape
    span_count = rows // SPAN_LEN
    sizes = mesh_sizes()

    qkv, context, block_out, mixed_low, act, ffn_grad, hidden_grad, pre_one_grad, vectors, losses = middle(
        hidden_in, w_qkv, w_out, w_in, w_ff_out, out_grad, b_query, b_value, b_out, b_in, b_ff_out,
        ln1_gain, ln1_bias, ln2_gain, ln2_bias, doc_count, single_flag, sizes,
    )
    g_ffo, rest, grad_in, vectors = attend_back(
        act, hidden_grad, ffn_grad, mixed_low, pre_one_grad, context, qkv, hidden_in, w_out, w_qkv,
        vectors, sizes,
    )
    (
        g_ffo, g_in, g_out, g_qkv, block_out, grad_in, span_loss, loss, g_b_in, *rest_grads
    ) = widen(g_ffo, rest, block_out, grad_in, vectors, losses, span_count)
    g_b_query, g_b_value, g_b_out, g_gain_one, g_bias_one, g_b_ffo, g_gain_two, g_bias_two = rest_grads
    return (
        block_out,
        loss.reshape(()),
        span_loss,
        grad_in,
        g_qkv,
        g_b_query,
        g_b_value,
        g_out,
        g_b_out,
        g_gain_one,
        g_bias_one,
        g_in,
        g_b_in,
        g_ffo,
        g_b_ffo,
        g_gain_two,
        g_bias_two,
    )


def solution(mesh):
    placed = (
        P(("wide", "narrow"), None),
        P(("wide", "narrow"), None),
        P(),
        P(),
        P(),
        P(),
        P(),
        P(),
        P(),
        P(),
        P(),
        P(),
        P(),
        P(),
        P(),
        P(),
        P(),
    )
    return jax.shard_map(
        per_device,
        mesh=mesh,
        in_specs=placed,
        out_specs=(
            P(("wide", "narrow"), None),
            P(),
            P(("wide", "narrow")),
            P(("wide", "narrow"), None),
            P(),
            P(),
            P(),
            P(),
            P(),
            P(),
            P(),
            P(),
            P(),
            P(),
            P(),
            P(),
            P(),
        ),
        check_vma=False,
    )
```

```python
import functools

import jax
import jax.numpy as jnp
from jax import lax
from jax.experimental import pallas as pl
from jax.experimental.pallas import tpu as pltpu
from jax.sharding import PartitionSpec as P

HEAD_DIM = 64
SPAN_LEN = 128
TILE = 256

ln_eps = 1e-06
score_scale = 0.2
far_low = -1000000000.0
head_scale = HEAD_DIM ** (-0.5)
MESH = pl.DeviceIdType.MESH
TICKS = 6
f32, bf16, i32 = jnp.float32, jnp.bfloat16, jnp.int32
MIB = 2**20


def dot(left, right):
    return jnp.dot(left, right, preferred_element_type=f32)


def dot_left_t(left, right):
    return lax.dot_general(left, right, (((0,), (0,)), ((), ())), preferred_element_type=f32)


def dot_right_t(left, right):
    return lax.dot_general(left, right, (((1,), (1,)), ((), ())), preferred_element_type=f32)


def row_mean(values):
    return jnp.mean(values, axis=1, keepdims=True)


def col_sum(values):
    return jnp.sum(values, axis=0, keepdims=True)


def norm_back(upstream, normed, scale, gain):
    scaled = upstream * gain
    return scale * (scaled - row_mean(scaled) - normed * row_mean(scaled * normed))


def head_halves():
    first = lax.broadcasted_iota(i32, (1, 2 * HEAD_DIM), 1) < HEAD_DIM
    return first, first.astype(bf16), jnp.logical_not(first).astype(bf16)


def pair_probs(stacked_queries, keys_low):
    scores = dot_right_t(stacked_queries, keys_low)
    shifted = jnp.exp((scores - jnp.max(scores, axis=1, keepdims=True)) * head_scale)
    return shifted * (1.0 / jnp.sum(shifted, axis=1, keepdims=True))


def attend_tile(at, x_ref, w_qkv_ref, b_query, b_value, w_out_ref, b_out, qkv_ref, context_ref, cent_ref):
    width = x_ref.shape[1]
    inputs = x_ref[at, :]
    for third in range(3):
        cols = pl.ds(third * width, width)
        packed = dot(inputs, w_qkv_ref[:, cols])
        if third == 0:
            packed = packed + b_query
        if third == 2:
            packed = packed + b_value
        qkv_ref[at, cols] = packed.astype(bf16)
    first, low_one, low_two = head_halves()
    lanes = 2 * HEAD_DIM
    for span in range(at.size // SPAN_LEN):
        sp = pl.ds(pl.multiple_of(at.start + span * SPAN_LEN, SPAN_LEN), SPAN_LEN)
        for pair in range(width // lanes):
            queries = qkv_ref[sp, pl.ds(pair * lanes, lanes)]
            keys_low = qkv_ref[sp, pl.ds(width + pair * lanes, lanes)]
            values_low = qkv_ref[sp, pl.ds(2 * width + pair * lanes, lanes)]
            stacked = jnp.concatenate([queries * low_one, queries * low_two], axis=0)
            mixed_values = dot(pair_probs(stacked, keys_low).astype(bf16), values_low)
            context_ref[sp, pl.ds(pair * lanes, lanes)] = jnp.where(
                first, mixed_values[:SPAN_LEN], mixed_values[SPAN_LEN:]
            ).astype(bf16)
    pre_one = inputs.astype(f32) + (dot(context_ref[at, :], w_out_ref[...]) + b_out)
    cent_ref[at, :] = pre_one - row_mean(pre_one)


def gelu_parts(values):
    cdf = 0.5 * (1.0 + lax.erf(values * 0.7071067811865476))
    pdf = 0.3989422804014327 * jnp.exp(-0.5 * values * values)
    return values * cdf, cdf + values * pdf


def contrast_rows(cls_low, count, flags, first, span_count):
    total, width = cls_low.shape
    slots, docsets = flags.shape
    block = min(total, 256)

    def layout(at):
        slot = at + lax.broadcasted_iota(i32, (block, 1), 0)
        device = slot // slots
        place = (slot - device * slots).astype(f32)
        member = lax.broadcasted_iota(i32, (block, docsets), 1) == device
        docs = jnp.sum(jnp.where(member, count, 0.0), axis=1, keepdims=True)
        single = dot_right_t(member.astype(bf16), flags.astype(bf16))
        doc = lax.broadcasted_iota(i32, (block, slots), 1).astype(f32)
        length = jnp.where(doc < docs, 2.0 - single, 0.0)
        earlier = lax.broadcasted_iota(i32, (slots, slots), 0) < lax.broadcasted_iota(
            i32, (slots, slots), 1
        )
        begins = dot(length.astype(bf16), earlier.astype(f32).astype(bf16))
        inside = (place >= begins) & (place < begins + length)
        double = inside & (length == 2.0)
        live = jnp.max(inside.astype(f32), axis=1, keepdims=True)
        pair = jnp.max(double.astype(f32), axis=1, keepdims=True)
        other = jnp.sum(jnp.where(double, 2.0 * begins + 1.0 - place, 0.0), axis=1, keepdims=True)
        mate = jnp.where(pair > 0.0, (device * slots).astype(f32) + other, slot.astype(f32))
        return slot.astype(f32), live, pair, mate

    eye = lax.broadcasted_iota(i32, (block, block), 0) == lax.broadcasted_iota(
        i32, (block, block), 1
    )
    live_row = jnp.concatenate(
        [col_sum(jnp.where(eye, layout(at)[1], 0.0)) for at in range(0, total, block)], axis=1
    )
    column = lax.broadcasted_iota(i32, (block, total), 1).astype(f32)
    pick_col = (
        lax.broadcasted_iota(i32, (span_count, total), 1)
        == first + lax.broadcasted_iota(i32, (span_count, total), 0)
    ).astype(f32).astype(bf16)
    rows_own = jnp.zeros((span_count, total), f32)
    upward = jnp.zeros((span_count, width), f32)
    own_loss = jnp.zeros((1, span_count), f32)
    loss = jnp.zeros((1, 1), f32)
    for at in range(0, total, block):
        slot, live, pair, mate = layout(at)
        cls_block = cls_low[at : at + block, :]
        sims = score_scale * dot_right_t(cls_block, cls_low)
        allowed = (live_row > 0.0) & (column != slot)
        masked = jnp.where(allowed, sims, far_low)
        top = jnp.max(masked, axis=1, keepdims=True)
        lse = top + jnp.log(jnp.sum(jnp.exp(masked - top), axis=1, keepdims=True))
        matches = column == mate
        positive = jnp.sum(jnp.where(matches, sims, 0.0), axis=1, keepdims=True)
        span_loss = jnp.where(pair > 0.0, lse - positive, 0.0)
        loss = loss + col_sum(span_loss)
        mine = at + lax.broadcasted_iota(i32, (block, span_count), 0) == (
            first + lax.broadcasted_iota(i32, (block, span_count), 1)
        )
        own_loss = own_loss + col_sum(jnp.where(mine, span_loss, 0.0))
        sim_grad = jnp.where(
            pair > 0.0, jnp.exp(masked - lse) - matches.astype(f32), 0.0
        ).astype(bf16)
        pick_row = (
            at + lax.broadcasted_iota(i32, (span_count, block), 1)
            == first + lax.broadcasted_iota(i32, (span_count, block), 0)
        ).astype(f32).astype(bf16)
        rows_own = rows_own + dot(pick_row, sim_grad)
        cols_own = dot_right_t(pick_col, sim_grad)
        upward = upward + dot(cols_own.astype(bf16), cls_block)
    upward = upward + dot(rows_own.astype(bf16), cls_low)
    return score_scale * upward, own_loss, loss


def middle_kernel(
    n_z,
    n_x,
    n_y,
    x_hbm,
    w_qkv_hbm,
    w_out_hbm,
    w_in_hbm,
    w_ffo_hbm,
    out_grad_hbm,
    b_query_ref,
    b_value_ref,
    b_out_ref,
    b_in_ref,
    b_ffo_ref,
    gain_one_ref,
    bias_one_ref,
    gain_two_ref,
    bias_two_ref,
    count_ref,
    flag_ref,
    qkv_hbm,
    context_hbm,
    block_hbm,
    mixed_hbm,
    act_hbm,
    ffn_grad_hbm,
    hidden_grad_hbm,
    pre_grad_hbm,
    vec_ref,
    losses_ref,
    x_v,
    w_qkv,
    w_out,
    qkv_v,
    context_v,
    cent_v,
    w_in,
    w_ffo,
    upper_v,
    block_v,
    mixed_v,
    act_v,
    slope_v,
    ffn_grad_v,
    two_v,
    first_v,
    cls_grad_v,
    b_in_v,
    cls_v,
    in_sem,
    out_sem,
    s_sem,
    r_sem,
):
    rows, width = cent_v.shape
    inner = w_in.shape[1]
    chunks = inner // width
    tiles = rows // TILE
    span_count = rows // SPAN_LEN
    wide, narrow = lax.axis_index("wide"), lax.axis_index("narrow")
    z, x = wide // n_x, lax.rem(wide, n_x)
    y, c = narrow // 2, lax.rem(narrow, 2)
    core = (wide, y * 2 + 1 - c)
    along_x = [(z * n_x + lax.rem(x + k, n_x), narrow) for k in range(1, n_x)]
    along_y = [(wide, lax.rem(y + k, n_y) * 2 + c) for k in range(1, n_y)]
    along_z = [(lax.rem(z + k, n_z) * n_x + x, narrow) for k in range(1, n_z)]
    partners = [core] + along_x + along_y + along_z

    barrier = pltpu.get_barrier_semaphore()
    for device in partners:
        pl.semaphore_signal(barrier, inc=1, device_id=device, device_id_type=MESH)

    loads = [
        pltpu.make_async_copy(src, dst, in_sem.at[k])
        for k, (src, dst) in enumerate(
            (
                (x_hbm, x_v),
                (w_qkv_hbm, w_qkv),
                (w_out_hbm, w_out),
                (w_in_hbm, w_in),
                (w_ffo_hbm, w_ffo),
                (out_grad_hbm, upper_v),
            )
        )
    ]
    for copy in loads:
        copy.start()

    def row(ref, at=0):
        return ref[pl.ds(at, width)].astype(f32).reshape(1, width)

    gain_one, bias_one, gain_two, bias_two, b_ffo = (
        row(r) for r in (gain_one_ref, bias_one_ref, gain_two_ref, bias_two_ref, b_ffo_ref)
    )
    for j in range(chunks):
        b_in_v[j : j + 1, :] = row(b_in_ref, j * width)

    def normed(cent):
        scale = lax.rsqrt(row_mean(cent * cent) + ln_eps)
        return cent * scale, scale

    def feed_forward(mixed, total, keep):
        mixed_low = mixed.astype(bf16)
        total[...] = mixed + b_ffo

        def step(j, carry):
            cols = pl.ds(pl.multiple_of(j * width, width), width)
            hidden = dot(mixed_low, w_in[:, cols]) + b_in_v[pl.ds(j, 1), :]
            act, slope = gelu_parts(hidden)
            act_low = act.astype(bf16)
            keep(cols, act_low, slope)
            total[...] += dot(act_low, w_ffo[cols, :])
            return carry

        lax.fori_loop(0, chunks, step, 0, unroll=True)
        pre_two = total[...]
        return pre_two - row_mean(pre_two)

    b_query, b_value, b_out = (row(r) for r in (b_query_ref, b_value_ref, b_out_ref))

    def store(src, dst, at, k):
        return pltpu.make_async_copy(src.at[at, :], dst.at[at, :], out_sem.at[k])

    def tile_rows(tile):
        return pl.ds(pl.multiple_of(tile * TILE, TILE), TILE)

    def attend_stores(tile):
        at = tile_rows(tile)
        return [
            store(qkv_v, qkv_hbm, at, 8 * tile + 6),
            store(context_v, context_hbm, at, 8 * tile + 7),
        ]

    def attend_step(tile, carry):
        attend_tile(
            tile_rows(tile), x_v, w_qkv, b_query, b_value, w_out, b_out, qkv_v, context_v, cent_v
        )
        for copy in attend_stores(tile):
            copy.start()
        return carry

    for copy in loads[:3]:
        copy.wait()
    lax.fori_loop(0, tiles, attend_step, 0)

    first_cent = jnp.concatenate(
        [cent_v[s * SPAN_LEN : s * SPAN_LEN + 1, :] for s in range(span_count)], axis=0
    )
    first_mixed = normed(first_cent)[0] * gain_one + bias_one
    loads[3].wait()
    loads[4].wait()
    first_two = feed_forward(first_mixed, first_v, lambda cols, act, slope: None)
    first_out = normed(first_two)[0] * gain_two + bias_two
    half = width // 2
    cls_v[z, x, y, c] = jnp.concatenate([first_out[:, :half], first_out[:, half:]], axis=0).astype(
        bf16
    )
    pl.semaphore_wait(barrier, len(partners))

    def gathers(stage):
        if stage == 0:
            ref, devices, base = cls_v.at[z, x, y, c], along_z, 0
        elif stage == 1:
            ref, devices, base = cls_v.at[:, x, y, c], along_x, n_z - 1
        elif stage == 2:
            ref, devices, base = cls_v.at[:, :, y, c], along_y, n_z + n_x - 2
        else:
            ref, devices, base = cls_v.at[:, :, :, c], [core], n_z + n_x + n_y - 3
        return [
            pltpu.make_async_remote_copy(
                ref, ref, s_sem.at[base + k], r_sem.at[base + k], device_id=d, device_id_type=MESH
            )
            for k, d in enumerate(devices)
        ]

    for copy in gathers(0):
        copy.start()
    loads[5].wait()

    def forward_stores(tile):
        at = tile_rows(tile)
        return [
            store(mixed_v, mixed_hbm, at, 8 * tile),
            store(block_v, block_hbm, at, 8 * tile + 1),
            store(act_v, act_hbm, at, 8 * tile + 2),
        ]

    def backward_stores(tile):
        at = tile_rows(tile)
        return [
            store(ffn_grad_v, ffn_grad_hbm, at, 8 * tile + 3),
            store(slope_v, hidden_grad_hbm, at, 8 * tile + 4),
            store(cent_v, pre_grad_hbm, at, 8 * tile + 5),
        ]

    def forward_tile(tile, carry):
        at = tile_rows(tile)
        mixed = normed(cent_v[at, :])[0] * gain_one + bias_one
        mixed_v[at, :] = mixed.astype(bf16)

        def keep(cols, act_low, slope):
            act_v[at, cols] = act_low
            slope_v[at, cols] = slope.astype(bf16)

        cent_two = feed_forward(mixed, two_v.at[at, :], keep)
        block_v[at, :] = (normed(cent_two)[0] * gain_two + bias_two).astype(bf16)
        two_v[at, :] = cent_two
        for copy in forward_stores(tile):
            copy.start()
        for stage in range(4):

            @pl.when(tile == min(stage, tiles - 1))
            def _():
                for copy in gathers(stage):
                    copy.wait()
                if stage < 3:
                    for copy in gathers(stage + 1):
                        copy.start()

        return carry

    lax.fori_loop(0, tiles, forward_tile, 0)

    low = cls_v[...].astype(f32).reshape(-1, 2 * span_count, half)
    cls_low = jnp.concatenate(
        [
            low[:, :span_count, :].reshape(-1, half),
            low[:, span_count:, :].reshape(-1, half),
        ],
        axis=1,
    ).astype(bf16)
    own = wide * (2 * n_y) + narrow
    cls_grad, own_loss, loss = contrast_rows(
        cls_low, count_ref[...].astype(f32).reshape(1, -1), flag_ref[...].astype(f32), own * span_count, span_count
    )
    cls_grad_v[...] = cls_grad
    lane = lax.broadcasted_iota(i32, losses_ref.shape, 1)
    losses_ref[...] = jnp.where(lane == span_count, loss, 0.0)
    losses_ref[:, :span_count] = own_loss

    vec_ref[...] = jnp.zeros(vec_ref.shape, f32)

    def add_row(k, values):
        vec_ref[pl.ds(k, 1), :] += col_sum(values)

    def backward_tile(tile, carry):
        at = tile_rows(tile)
        upper = upper_v[at, :].astype(f32)
        place = lax.broadcasted_iota(i32, (TILE, 1), 0)
        for span in range(TILE // SPAN_LEN):
            upper = jnp.where(
                place == span * SPAN_LEN,
                cls_grad_v[pl.ds(tile * (TILE // SPAN_LEN) + span, 1), :],
                upper,
            )
        normed_two, scale_two = normed(two_v[at, :])
        add_row(6, upper * normed_two)
        add_row(7, upper)
        pre_two_grad = norm_back(upper, normed_two, scale_two, gain_two)
        ffn_grad = pre_two_grad.astype(bf16)
        ffn_grad_v[at, :] = ffn_grad
        add_row(5, ffn_grad.astype(f32))
        two_v[at, :] = pre_two_grad

        def step(j, inner_carry):
            cols = pl.ds(pl.multiple_of(j * width, width), width)
            back = dot_right_t(ffn_grad, w_ffo[cols, :]) * slope_v[at, cols].astype(f32)
            hidden_grad = back.astype(bf16)
            slope_v[at, cols] = hidden_grad
            add_row(8 + j, hidden_grad.astype(f32))
            two_v[at, :] += dot_right_t(hidden_grad, w_in[:, cols])
            return inner_carry

        lax.fori_loop(0, chunks, step, 0, unroll=True)
        mixed_grad = two_v[at, :]
        normed_one, scale_one = normed(cent_v[at, :])
        add_row(3, mixed_grad * normed_one)
        add_row(4, mixed_grad)
        pre_one_grad = norm_back(mixed_grad, normed_one, scale_one, gain_one)
        cent_v[at, :] = pre_one_grad
        add_row(2, pre_one_grad.astype(bf16).astype(f32))
        for copy in backward_stores(tile):
            copy.start()
        return carry

    lax.fori_loop(0, tiles, backward_tile, 0)

    for tile in range(tiles):
        for copy in attend_stores(tile) + forward_stores(tile) + backward_stores(tile):
            copy.wait()


def middle(
    x,
    w_qkv,
    w_out,
    w_in,
    w_ffo,
    out_grad,
    b_query,
    b_value,
    b_out,
    b_in,
    b_ffo,
    gain_one,
    bias_one,
    gain_two,
    bias_two,
    doc_count,
    single_flag,
    sizes,
):
    rows, width = x.shape
    inner = w_in.shape[1]
    span_count = rows // SPAN_LEN
    n_z, n_x, n_y = sizes
    moves = n_z + n_x + n_y - 2
    hbm = pl.BlockSpec(memory_space=pl.ANY)
    vmem = pl.BlockSpec(memory_space=pltpu.VMEM)
    shape = jax.ShapeDtypeStruct
    return pl.pallas_call(
        functools.partial(middle_kernel, n_z, n_x, n_y),
        out_shape=(
            shape((rows, 3 * width), bf16),
            shape((rows, width), bf16),
            shape((rows, width), bf16),
            shape((rows, width), bf16),
            shape((rows, inner), bf16),
            shape((rows, width), bf16),
            shape((rows, inner), bf16),
            shape((rows, width), f32),
            shape((16, width), f32),
            shape((1, 128), f32),
        ),
        in_specs=[hbm] * 6 + [vmem] * 11,
        out_specs=(hbm,) * 8 + (vmem,) * 2,
        scratch_shapes=[
            pltpu.VMEM((rows, width), bf16),
            pltpu.VMEM((width, 3 * width), bf16),
            pltpu.VMEM((width, width), bf16),
            pltpu.VMEM((rows, 3 * width), bf16),
            pltpu.VMEM((rows, width), bf16),
            pltpu.VMEM((rows, width), f32),
            pltpu.VMEM((width, inner), bf16),
            pltpu.VMEM((inner, width), bf16),
            pltpu.VMEM((rows, width), bf16),
            pltpu.VMEM((rows, width), bf16),
            pltpu.VMEM((rows, width), bf16),
            pltpu.VMEM((rows, inner), bf16),
            pltpu.VMEM((rows, inner), bf16),
            pltpu.VMEM((rows, width), bf16),
            pltpu.VMEM((rows, width), f32),
            pltpu.VMEM((span_count, width), f32),
            pltpu.VMEM((span_count, width), f32),
            pltpu.VMEM((inner // width, width), f32),
            pltpu.VMEM((n_z, n_x, n_y, 2, 2 * span_count, width // 2), bf16),
            pltpu.SemaphoreType.DMA((6,)),
            pltpu.SemaphoreType.DMA((8 * (rows // TILE),)),
            pltpu.SemaphoreType.DMA((moves,)),
            pltpu.SemaphoreType.DMA((moves,)),
        ],
        compiler_params=pltpu.CompilerParams(
            collective_id=1, has_side_effects=True, vmem_limit_bytes=60 * MIB
        ),
        name="forward_and_loss",
    )(
        x, w_qkv, w_out, w_in, w_ffo, out_grad, b_query, b_value, b_out, b_in, b_ffo, gain_one, bias_one,
        gain_two, bias_two, doc_count, single_flag.T,
    )


def attend_back_kernel(
    n_z,
    n_x,
    comm,
    order,
    act_hbm,
    hidden_grad_hbm,
    ffn_grad_hbm,
    mixed_hbm,
    pre_grad_hbm,
    context_hbm,
    qkv_hbm,
    x_hbm,
    w_out_hbm,
    w_qkv_hbm,
    vec_ref,
    o_ffo,
    o_rest,
    grad_in_hbm,
    o_vec,
    stream,
    ffn_grad_v,
    mixed_v,
    pre_v,
    context_v,
    qkv_v,
    x_v,
    w_out,
    w_qkv,
    attn_v,
    context_grad_v,
    part,
    sib,
    r1,
    r2,
    r3,
    vbuf,
    in_sem,
    out_sem,
    s_sem,
    r_sem,
    zs_sem,
    zr_sem,
    vs_sem,
    vr_sem,
):
    rows, width = x_v.shape
    half, quarter = width // 2, width // 4
    eighth = quarter // n_z
    tiles = rows // TILE
    ahead = stream.shape[0]
    wide, narrow = lax.axis_index("wide"), lax.axis_index("narrow")
    z, x = wide // n_x, lax.rem(wide, n_x)
    y, c = narrow // 2, lax.rem(narrow, 2)
    core = (wide, y * 2 + 1 - c)
    near_x = (z * n_x + 1 - x, narrow)
    near_y = (wide, (1 - y) * 2 + c)
    one = tuple(jnp.where(c == 0, a, b) for a, b in zip(near_x, near_y))
    two = tuple(jnp.where(c == 0, b, a) for a, b in zip(near_x, near_y))
    h1 = jnp.where(c == 0, x, y)
    h2 = jnp.where(c == 0, y, x)
    others = [lax.rem(z + k, n_z) for k in range(1, n_z)]
    along_z = [(o * n_x + x, narrow) for o in others]

    if comm:
        barrier = pltpu.get_barrier_semaphore()
        for device in [core, near_x, near_y] + along_z:
            pl.semaphore_signal(barrier, inc=1, device_id=device, device_id_type=MESH)

    def stream_load(j):
        src = act_hbm if j < 4 else hidden_grad_hbm
        return pltpu.make_async_copy(
            src.at[:, pl.ds((j % 4) * width, width)], stream.at[j % ahead], in_sem.at[j]
        )

    resident = [
        pltpu.make_async_copy(src, dst, in_sem.at[8 + k])
        for k, (src, dst) in enumerate(
            (
                (ffn_grad_hbm, ffn_grad_v),
                (mixed_hbm, mixed_v),
                (pre_grad_hbm, pre_v),
                (w_out_hbm, w_out),
                (qkv_hbm, qkv_v),
                (w_qkv_hbm, w_qkv),
                (context_hbm, context_v),
                (x_hbm, x_v),
            )
        )
    ]
    stream_load(0).start()
    resident[0].start()
    for j in range(1, ahead):
        stream_load(j).start()
    for copy in resident[1:]:
        copy.start()
    vbuf[0] = vec_ref[...]
    waited = set()

    def need(*which):
        for k in which:
            if k not in waited:
                waited.add(k)
                resident[k].wait()

    first, low_one, low_two = head_halves()
    lanes = 2 * HEAD_DIM

    def weight_block(b):
        pair, second = b // 2, b % 2
        which = c if second else 1 - c
        block = b if pair == 4 else 2 * pair + which
        if b < 8:
            if not second:
                stream_load(b).wait()
                stream_load(b + 1).wait()
            streamed = stream.at[b // 2 * 2 % ahead + which]
        if b < 4:
            need(0)
            left, right = streamed, ffn_grad_v
        elif b < 8:
            need(1)
            left, right = mixed_v, streamed
        elif b < 9:
            need(6)
            left, right = context_v, attn_v
        else:
            need(7)
            cols = pl.multiple_of((block - 9) * width, 128)
            left, right = x_v, qkv_v.at[:, pl.ds(cols, width)]

        def step(i, carry):
            at = pl.ds(pl.multiple_of(i * TILE, TILE), TILE)
            part[block, at, :] = dot_left_t(left[:, at], right[...]).astype(bf16)
            return carry

        lax.fori_loop(0, width // TILE, step, 0, unroll=True)
        if second and b - 1 + ahead < 8:
            stream_load(b - 1 + ahead).start()
            stream_load(b + ahead).start()

    def grad_in_store(tile):
        at = pl.ds(tile * TILE, TILE)
        return pltpu.make_async_copy(pre_v.at[at, :], grad_in_hbm.at[at, :], out_sem.at[tile])

    def attend_tile(tile, piece):
        need(2, 3, 4, 5)
        at = pl.ds(tile * TILE, TILE)
        if piece == 0:
            attn_grad = pre_v[at, :].astype(bf16)
            attn_v[at, :] = attn_grad
            context_grad_v[...] = dot_right_t(attn_grad, w_out[...]).astype(bf16)
        if piece == 2:
            vbuf[0, 0:1, :] += col_sum(qkv_v[at, 0:width].astype(f32))
            vbuf[0, 1:2, :] += col_sum(qkv_v[at, 2 * width : 3 * width].astype(f32))
            pre_v[at, :] += dot_right_t(qkv_v[at, :], w_qkv[...])
            grad_in_store(tile).start()
            return

        def pair_step(pair):
            q_at, k_at, v_at = (pl.ds(third * width + pair * lanes, lanes) for third in range(3))
            for span in range(TILE // SPAN_LEN):
                sp = pl.ds(tile * TILE + span * SPAN_LEN, SPAN_LEN)
                queries, keys_low, values_low = qkv_v[sp, q_at], qkv_v[sp, k_at], qkv_v[sp, v_at]
                upper = context_grad_v[pl.ds(span * SPAN_LEN, SPAN_LEN), q_at]
                stacked = jnp.concatenate([queries * low_one, queries * low_two], axis=0)
                stacked_up = jnp.concatenate([upper * low_one, upper * low_two], axis=0)
                scores = dot_right_t(keys_low, stacked)
                shifted = jnp.exp((scores - jnp.max(scores, axis=0, keepdims=True)) * head_scale)
                probs = shifted * (1.0 / col_sum(shifted))
                value_grad = dot(probs.astype(bf16), stacked_up)
                prob_grad = dot_right_t(values_low, stacked_up)
                score_grad = (probs * (prob_grad - col_sum(probs * prob_grad))).astype(bf16)
                query_grad = dot_left_t(score_grad, keys_low) * head_scale
                key_grad = dot(score_grad, stacked) * head_scale
                qkv_v[sp, q_at] = jnp.where(
                    first, query_grad[:SPAN_LEN], query_grad[SPAN_LEN:]
                ).astype(bf16)
                qkv_v[sp, k_at] = key_grad.astype(bf16)
                qkv_v[sp, v_at] = value_grad.astype(bf16)

        pairs = width // lanes
        for pair in range(pairs // 2) if piece == 0 else range(pairs // 2, pairs):
            pair_step(pair)

    def out_at(t, row, count):
        if t < 2:
            at = pl.multiple_of((2 * t + c) * width + row, 16)
            return o_ffo.at[pl.ds(at, count), :]
        cols = pl.multiple_of((2 * (t - 2) + c) * width, 128)
        return o_rest.at[pl.ds(pl.multiple_of(row, 16), count), pl.ds(cols, width)]

    def part_at(t, row, count):
        return part.at[2 * t + c, pl.ds(pl.multiple_of(row, 16), count), :]

    keep1 = h1 * half
    keep2 = keep1 + h2 * quarter
    own = keep2 + z * eighth

    def send(src, dst, stage, t, device):
        return pltpu.make_async_remote_copy(
            src, dst, s_sem.at[stage, t], r_sem.at[stage, t], device_id=device, device_id_type=MESH
        )

    def send_z(src, dst, stage, t, k):
        return pltpu.make_async_remote_copy(
            src,
            dst,
            zs_sem.at[stage, t, k],
            zr_sem.at[stage, t, k],
            device_id=along_z[k],
            device_id_type=MESH,
        )

    def sibling_slot(t, of):
        return sib.at[t] if t < 2 else part.at[2 * (t - 2) + 1 - of]

    def copies(stage, t):
        if stage == 0:
            return [send(part.at[2 * t + 1 - c], sibling_slot(t, 1 - c), 0, t, core)]
        if stage == 1:
            return [send(part_at(t, (1 - h1) * half, half), r1.at[t], 1, t, one)]
        if stage == 2:
            return [send(part_at(t, keep1 + (1 - h2) * quarter, quarter), r2.at[t], 2, t, two)]
        if stage == 3:
            return [
                send_z(part_at(t, keep2 + o * eighth, eighth), r3.at[t, k], 0, t, k)
                for k, o in enumerate(others)
            ]
        if stage == 4:
            return [
                send_z(part_at(t, own, eighth), out_at(t, own, eighth), 1, t, k)
                for k in range(n_z - 1)
            ]
        if stage == 5:
            place = out_at(t, keep2, quarter)
            return [send(place, place, 3, t, two)]
        if stage == 6:
            place = out_at(t, keep1, half)
            return [send(place, place, 4, t, one)]
        place = out_at(t, 0, width)
        return [send(place, place, 5, t, core)]

    def add(t, row, count, got):
        def step(i, carry):
            at = pl.ds(pl.multiple_of(row + i * 48, 16), 48)
            here = part[2 * t + c, at, :].astype(f32) + got[
                pl.ds(pl.multiple_of(i * 48, 16), 48), :
            ].astype(f32)
            part[2 * t + c, at, :] = here.astype(bf16)
            return carry

        lax.fori_loop(0, count // 48, step, 0)

    def own_store(t):
        return pltpu.make_async_copy(
            part_at(t, own, eighth), out_at(t, own, eighth), out_sem.at[tiles + t]
        )

    def advance(stage, t):
        if stage > 0:
            for copy in copies(stage - 1, t):
                copy.wait()
        if stage == 1:
            add(t, 0, width, sibling_slot(t, c))
        elif stage == 2:
            add(t, keep1, half, r1.at[t])
        elif stage == 3:
            add(t, keep2, quarter, r2.at[t])
        elif stage == 4:
            total = part_at(t, own, eighth)[...].astype(f32)
            for k in range(n_z - 1):
                total = total + r3[t, k].astype(f32)
            part_at(t, own, eighth)[...] = total.astype(bf16)
            own_store(t).start()
        elif stage == 5:
            own_store(t).wait()
        if stage < 8:
            for copy in copies(stage, t):
                copy.start()

    def vector_copies(k):
        if k < 3:
            device = (core, near_x, near_y)[k]
            ends = [(vbuf.at[2 * k], vbuf.at[2 * k + 1], k, device)]
        else:
            ends = [(vbuf.at[6], vbuf.at[7 + i], 3 + i, d) for i, d in enumerate(along_z)]
        return [
            pltpu.make_async_remote_copy(
                src, dst, vs_sem.at[s], vr_sem.at[s], device_id=d, device_id_type=MESH
            )
            for src, dst, s, d in ends
        ]

    def vector_step(k):
        if k > 0:
            for copy in vector_copies(k - 1):
                copy.wait()
        if k in (1, 2, 3):
            vbuf[2 * k] = vbuf[2 * k - 2] + vbuf[2 * k - 1]
        if k < 4:
            for copy in vector_copies(k):
                copy.start()
        else:
            total = vbuf[6]
            for i in range(n_z - 1):
                total = total + vbuf[7 + i]
            o_vec[...] = total

    entered = False
    for kind, *at in order:
        if kind == "w":
            weight_block(*at)
        elif kind == "a":
            attend_tile(*at)
        elif comm:
            if not entered:
                pl.semaphore_wait(barrier, 2 + n_z)
                entered = True
            if kind == "s":
                advance(*at)
            else:
                vector_step(*at)
    if not comm:
        o_vec[...] = vbuf[0]
        locals_ = [
            pltpu.make_async_copy(
                part.at[b],
                o_ffo.at[pl.ds(b * width, width), :]
                if b < 4
                else o_rest.at[:, pl.ds((b - 4) * width, width)],
                in_sem.at[b],
            )
            for b in range(2 * TICKS)
        ]
        for copy in locals_:
            copy.start()
        for copy in locals_:
            copy.wait()
    for tile in range(tiles):
        grad_in_store(tile).wait()


def schedule():
    return [
        ("w", 0), ("s", 0, 0), ("w", 1), ("w", 2), ("s", 1, 0), ("s", 0, 1), ("w", 3), ("w", 4),
        ("s", 1, 1), ("w", 5), ("w", 6), ("s", 0, 2), ("w", 7), ("s", 2, 0), ("a", 0, 0),
        ("a", 0, 1), ("s", 1, 2), ("s", 3, 0), ("s", 0, 3), ("a", 0, 2), ("a", 1, 0), ("s", 2, 1),
        ("a", 1, 1), ("s", 4, 0), ("s", 1, 3), ("s", 2, 2), ("a", 1, 2), ("s", 3, 1), ("a", 2, 0),
        ("a", 2, 1), ("a", 2, 2), ("s", 5, 0), ("a", 3, 0), ("s", 4, 1), ("s", 2, 3), ("s", 6, 0),
        ("a", 3, 1), ("s", 3, 2), ("a", 3, 2), ("w", 8), ("v", 0), ("w", 9), ("s", 0, 4),
        ("s", 5, 1), ("w", 10), ("v", 1), ("s", 3, 3), ("s", 1, 4), ("w", 11), ("s", 0, 5),
        ("v", 2), ("s", 4, 2), ("s", 1, 5), ("s", 2, 4), ("s", 4, 3), ("v", 3), ("s", 5, 2),
        ("s", 3, 4), ("s", 6, 1), ("s", 2, 5), ("v", 4), ("s", 5, 3), ("s", 4, 4), ("s", 7, 0),
        ("s", 3, 5), ("s", 6, 3), ("s", 6, 2), ("s", 5, 4), ("s", 7, 1), ("s", 4, 5), ("s", 6, 4),
        ("s", 8, 0), ("s", 5, 5), ("s", 7, 2), ("s", 7, 3), ("s", 6, 5), ("s", 8, 3), ("s", 7, 4),
        ("s", 7, 5), ("s", 8, 4), ("s", 8, 1), ("s", 8, 2), ("s", 8, 5),
    ]


def attend_back(act, hidden_grad, ffn_grad, mixed_low, pre_grad, context, qkv, x, w_out, w_qkv, vectors, sizes, order=None):
    rows, width = x.shape
    inner = act.shape[1]
    n_z, n_x, n_y = sizes
    comm = n_x == 2 and n_y == 2 and width % (64 * n_z) == 0
    hbm = pl.BlockSpec(memory_space=pl.ANY)
    vmem = pl.BlockSpec(memory_space=pltpu.VMEM)
    shape = jax.ShapeDtypeStruct
    tiles = rows // TILE
    scratch = [
        pltpu.VMEM((4, rows, width), bf16),
        pltpu.VMEM((rows, width), bf16),
        pltpu.VMEM((rows, width), bf16),
        pltpu.VMEM((rows, width), f32),
        pltpu.VMEM((rows, width), bf16),
        pltpu.VMEM((rows, 3 * width), bf16),
        pltpu.VMEM((rows, width), bf16),
        pltpu.VMEM((width, width), bf16),
        pltpu.VMEM((width, 3 * width), bf16),
        pltpu.VMEM((rows, width), bf16),
        pltpu.VMEM((TILE, width), bf16),
        pltpu.VMEM((2 * TICKS, width, width), bf16),
        pltpu.VMEM((2, width, width), bf16),
        pltpu.VMEM((TICKS, width // 2, width), bf16),
        pltpu.VMEM((TICKS, width // 4, width), bf16),
        pltpu.VMEM((TICKS, n_z - 1, width // 4 // n_z, width), bf16),
        pltpu.VMEM((6 + n_z,) + vectors.shape, f32),
        pltpu.SemaphoreType.DMA((16,)),
        pltpu.SemaphoreType.DMA((tiles + TICKS,)),
        pltpu.SemaphoreType.DMA((6, TICKS)),
        pltpu.SemaphoreType.DMA((6, TICKS)),
        pltpu.SemaphoreType.DMA((2, TICKS, n_z - 1)),
        pltpu.SemaphoreType.DMA((2, TICKS, n_z - 1)),
        pltpu.SemaphoreType.DMA((2 + n_z,)),
        pltpu.SemaphoreType.DMA((2 + n_z,)),
    ]
    params = dict(vmem_limit_bytes=60 * MIB)
    if comm:
        params.update(collective_id=0, has_side_effects=True)
    g_ffo, rest, grad_in, vectors = pl.pallas_call(
        functools.partial(attend_back_kernel, n_z, n_x, comm, order or schedule()),
        out_shape=(
            shape((inner, width), bf16),
            shape((width, inner + 4 * width), bf16),
            shape((rows, width), f32),
            shape(vectors.shape, f32),
        ),
        in_specs=[hbm] * 10 + [vmem],
        out_specs=(hbm, hbm, hbm, vmem),
        scratch_shapes=scratch,
        compiler_params=pltpu.CompilerParams(**params),
        name="attend_back_and_sums",
    )(act, hidden_grad, ffn_grad, mixed_low, pre_grad, context, qkv, x, w_out, w_qkv, vectors)
    if not comm:
        g_ffo, rest, vectors = lax.psum((g_ffo, rest, vectors), ("wide", "narrow"))
    return g_ffo, rest, grad_in, vectors


def widen_kernel(
    ffo_ref,
    rest_ref,
    block_ref,
    grad_ref,
    vec_ref,
    losses_ref,
    w_ffo,
    w_in,
    w_out,
    w_qkv,
    block,
    grad,
    span_loss,
    loss,
    b_in,
    *vectors,
):
    inner, width = w_in.shape[1], w_out.shape[1]
    block[...] = block_ref[...]
    grad[...] = grad_ref[...]
    w_ffo[...] = ffo_ref[...].astype(f32)
    w_in[...] = rest_ref[:, :inner].astype(f32)
    w_out[...] = rest_ref[:, inner : inner + width].astype(f32)
    w_qkv[...] = rest_ref[:, inner + width :].astype(f32)

    @pl.when(pl.program_id(0) == 0)
    def _():
        count = span_loss.shape[0]
        span_loss[...] = losses_ref[:, :count].reshape(count)
        loss[...] = losses_ref[:, count : count + 1].reshape(1)
        for k, vector in enumerate(vectors):
            vector[...] = vec_ref[k : k + 1, :].reshape(vector.shape)
        for j in range(inner // width):
            at = 8 + j
            b_in[pl.ds(j * width, width)] = vec_ref[at : at + 1, :].reshape(width)


def widen(ffo, rest, block, grad, vectors, losses, span_count):
    rows = block.shape[0]
    inner, width = ffo.shape
    steps = 2
    shape = jax.ShapeDtypeStruct

    def tiles(rows, cols):
        return pl.BlockSpec((rows // steps, cols), lambda i: (i, 0))

    def whole(*sizes):
        return pl.BlockSpec(sizes, lambda i: (0,) * len(sizes))

    flat = [span_count, 1, inner] + [width] * 8
    return pl.pallas_call(
        widen_kernel,
        grid=(steps,),
        out_shape=(
            shape((inner, width), f32),
            shape((width, inner), f32),
            shape((width, width), f32),
            shape((width, 3 * width), f32),
            shape(block.shape, block.dtype),
            shape(grad.shape, grad.dtype),
            *(shape((n,), f32) for n in flat),
        ),
        in_specs=[
            tiles(inner, width),
            tiles(width, rest.shape[1]),
            tiles(rows, width),
            tiles(rows, width),
            whole(*vectors.shape),
            whole(*losses.shape),
        ],
        out_specs=(
            tiles(inner, width),
            tiles(width, inner),
            tiles(width, width),
            tiles(width, 3 * width),
            tiles(rows, width),
            tiles(rows, width),
            *(whole(n) for n in flat),
        ),
        compiler_params=pltpu.CompilerParams(vmem_limit_bytes=60 * MIB),
        name="widen",
    )(ffo, rest, block, grad, vectors, losses)


def mesh_sizes():
    n_wide, n_narrow = lax.axis_size("wide"), lax.axis_size("narrow")
    n_y = n_narrow // 2
    n_x = n_y if n_wide % n_y == 0 else 1
    return n_wide // n_x, n_x, n_y


def per_device(
    hidden_in,
    out_grad,
    w_qkv,
    b_query,
    b_value,
    w_out,
    b_out,
    ln1_gain,
    ln1_bias,
    w_in,
    b_in,
    w_ff_out,
    b_ff_out,
    ln2_gain,
    ln2_bias,
    doc_count,
    single_flag,
):
    rows, width = hidden_in.shape
    span_count = rows // SPAN_LEN
    sizes = mesh_sizes()

    qkv, context, block_out, mixed_low, act, ffn_grad, hidden_grad, pre_one_grad, vectors, losses = middle(
        hidden_in, w_qkv, w_out, w_in, w_ff_out, out_grad, b_query, b_value, b_out, b_in, b_ff_out,
        ln1_gain, ln1_bias, ln2_gain, ln2_bias, doc_count, single_flag, sizes,
    )
    g_ffo, rest, grad_in, vectors = attend_back(
        act, hidden_grad, ffn_grad, mixed_low, pre_one_grad, context, qkv, hidden_in, w_out, w_qkv,
        vectors, sizes,
    )
    (
        g_ffo, g_in, g_out, g_qkv, block_out, grad_in, span_loss, loss, g_b_in, *rest_grads
    ) = widen(g_ffo, rest, block_out, grad_in, vectors, losses, span_count)
    g_b_query, g_b_value, g_b_out, g_gain_one, g_bias_one, g_b_ffo, g_gain_two, g_bias_two = rest_grads
    return (
        block_out,
        loss.reshape(()),
        span_loss,
        grad_in,
        g_qkv,
        g_b_query,
        g_b_value,
        g_out,
        g_b_out,
        g_gain_one,
        g_bias_one,
        g_in,
        g_b_in,
        g_ffo,
        g_b_ffo,
        g_gain_two,
        g_bias_two,
    )


def solution(mesh):
    placed = (
        P(("wide", "narrow"), None),
        P(("wide", "narrow"), None),
        P(),
        P(),
        P(),
        P(),
        P(),
        P(),
        P(),
        P(),
        P(),
        P(),
        P(),
        P(),
        P(),
        P(),
        P(),
    )
    return jax.shard_map(
        per_device,
        mesh=mesh,
        in_specs=placed,
        out_specs=(
            P(("wide", "narrow"), None),
            P(),
            P(("wide", "narrow")),
            P(("wide", "narrow"), None),
            P(),
            P(),
            P(),
            P(),
            P(),
            P(),
            P(),
            P(),
            P(),
            P(),
            P(),
            P(),
            P(),
        ),
        check_vma=False,
    )
```
